32 devices in a mesh: dp: 16 (over z, y, x), pipe: 2 (over core).
Axes of the slice: x: 2, y: 2, z: 4, core: 2. Of those that a mesh axis runs over, the one named last changes fastest.
Arguments:
- layer_ends: bfloat16 [2, 16384, 1024], P('pipe', 'dp'), may hold values from -6 to 6
- segment_ids: int32 [32, 512], P('dp'), may hold values from 0 to 7, never falling along the last dimension, each value on 1 to 256 neighbouring positions
- mixture: int32 [16384], P('dp'), may hold values from 0 to 15
- noise: float32 [16384, 512], P('dp'), may hold values from -5 to 5
- plan_step: int32 [1], replicated, may hold values from 0 to 1999
- ln1_gain: bfloat16 [1024], P(('dp', 'pipe')), may hold values from 0.5 to 1.5
- w_qkv: bfloat16 [1024, 3072], P(('dp', 'pipe')), may hold values from -0.1875 to 0.1875
- w_out: bfloat16 [1024, 1024], P(('dp', 'pipe')), may hold values from -0.75 to 0.75
- ln2_gain: bfloat16 [1024], P(('dp', 'pipe')), may hold values from 0.5 to 1.5
- w_up: bfloat16 [1024, 4096], P(('dp', 'pipe')), may hold values from -0.1875 to 0.1875
- w_down: bfloat16 [4096, 1024], P(('dp', 'pipe')), may hold values from -0.09375 to 0.09375
- w_latent: bfloat16 [1024, 1024], P(('dp', 'pipe')), may hold values from -0.09375 to 0.09375
- w_decode: bfloat16 [512, 1024], P(('dp', 'pipe')), may hold values from -0.25 to 0.25
- decode_bias: bfloat16 [1024], P(('dp', 'pipe')), may hold values from -3 to 3
- comp_mean: bfloat16 [16, 512], P(None, ('dp', 'pipe')), may hold values from -4 to 4
- comp_logvar: bfloat16 [16, 512], P(None, ('dp', 'pipe')), may hold values from -0.5 to 0.5
Outputs:
- result_ends: float32 [2, 16384, 1024], P('pipe', 'dp')
- grad_ln1_gain: float32 [1024], P(('dp', 'pipe'))
- grad_qkv: float32 [1024, 3072], P(('dp', 'pipe'))
- grad_out: float32 [1024, 1024], P(('dp', 'pipe'))
- grad_ln2_gain: float32 [1024], P(('dp', 'pipe'))
- grad_up: float32 [1024, 4096], P(('dp', 'pipe'))
- grad_down: float32 [4096, 1024], P(('dp', 'pipe'))
- grad_latent: float32 [1024, 1024], P(('dp', 'pipe'))
- grad_decode: float32 [512, 1024], P(('dp', 'pipe'))
- grad_bias: float32 [1024], P(('dp', 'pipe'))
- grad_comp_mean: float32 [16, 512], P(None, ('dp', 'pipe'))
- grad_comp_logvar: float32 [16, 512], P(None, ('dp', 'pipe'))
The draws below stay inside these ranges and needn't reach their ends.
Inputs may be any that keep to these rules, and one draw needn't show every extreme that they name: `segment_ids`: within each row of 512 cells ids never fall; each slide covers 1 to 256 cells, and one covers exactly that many.
All inputs are finite; a program needn't handle non-finite values.
Results may differ from the reference program's by a relative error of at most 0.012.
The reference program's roundings to bfloat16 on the way count: a program that leaves them out, or rounds other values in their place, can miss the bound.
Values may be sent and summed in bfloat16 or wider, within the bound.
No kernel may reach another device: no remote copies, remote signals or barrier semaphores. Data moves between devices by JAX's collectives and lax.ppermute only.
A program may use at most 448 MiB of HBM per device.

```python
import math
import jax
import jax.numpy as jnp
import numpy as np
from jax import lax

D = 1024
HEADS = 16
FF = 4096
LATENT = 512
COMPS = 16
CELLS_MB = 512
MB = 2
WARM = 1000
TOKENS = 16384
N_DP = 16


def set_ends(array, rng, least, largest):
    place = [jax.random.randint(jax.random.fold_in(rng, axis), (), 0, length) for axis, length in enumerate(array.shape)]
    main_axis = array.shape.index(max(array.shape))
    next_to = place[:main_axis] + [(place[main_axis] + 1) % array.shape[main_axis]] + place[main_axis + 1:]
    return array.at[tuple(place)].set(least).at[tuple(next_to)].set(largest)


def levels(rng, shape, split, least, high):
    factor_of = 1.0
    for dim, blocks in split:
        steps = jax.random.uniform(jax.random.fold_in(jax.random.fold_in(rng, 6), dim), (blocks,), jnp.float32, least / len(split), high / len(split))
        factor_of = factor_of * jnp.repeat(jnp.exp(steps), shape[dim] // blocks).reshape((-1,) + (1,) * (len(shape) - 1 - dim))
    return factor_of


def length_profile(number_of, total, reach, slope):
    loads = [(1 << 20) // math.isqrt(grade ** slope) + 1 for grade in range(2, number_of + 1)]
    rest, counts = total - reach - (number_of - 1), [1] * (number_of - 1)
    while rest > 0:
        movable = [i for i in range(number_of - 1) if counts[i] < reach]
        pool, left = sum([loads[i] for i in movable]), rest
        for i in movable:
            more = min(reach - counts[i], max(1, left * loads[i] // pool), rest)
            counts[i] = counts[i] + more
            rest = rest - more
    return np.array([reach] + counts)


def ragged_sizes(stream_key, count, total, bound, skew):
    if count == 2:
        one = jax.random.randint(stream_key, (), max(1, total - bound), min(bound, total - 1) + 1)
        return jnp.stack([one, total - one])
    tallies = jnp.asarray(length_profile(count, total, bound, skew), jnp.int32)
    twos = (count - 1) // 2
    source_of, sink = tallies[1:1 + 2 * twos:2], tallies[2:2 + 2 * twos:2]
    margin = jnp.minimum(source_of - 1, bound - sink)
    shifted = jax.random.randint(jax.random.fold_in(stream_key, 1), (twos,), 0, 1 << 20) % (margin + 1)
    tallies = tallies.at[1:1 + 2 * twos:2].set(source_of - shifted).at[2:2 + 2 * twos:2].set(sink + shifted)
    return tallies[jax.random.permutation(jax.random.fold_in(stream_key, 2), count)]


def gaussian(own_key, extent, scale, most, shards=(), kind=jnp.bfloat16):
    array = jax.random.normal(own_key, extent, jnp.float32) * scale
    if len(shards) > 0:
        array = levels(own_key, extent, shards, -0.22, 0.18) * array
    return jnp.clip(array, min=-most, max=most).astype(kind)


def setup_inputs(seed: int = 0) -> dict:
    streams_of = jax.random.split(jax.random.key(seed), 17)
    return {
        "layer_ends": gaussian(streams_of[0], (2, TOKENS, D), 1.0, 6.0, ((0, 2), (1, 16))),
        "segment_ids": jax.vmap(lambda own: jnp.searchsorted(jnp.cumsum(ragged_sizes(own, max(4, CELLS_MB // 64), CELLS_MB, CELLS_MB // 2, 0)), jnp.arange(CELLS_MB), side="right"))(jax.random.split(streams_of[1], (N_DP * MB))).reshape((N_DP * MB, CELLS_MB)).astype(jnp.int32),
        "mixture": set_ends(jax.random.randint(streams_of[2], (TOKENS,), 0, COMPS), jax.random.fold_in(streams_of[2], 1), 0, COMPS - 1).astype(jnp.int32),
        "noise": gaussian(streams_of[3], (TOKENS, LATENT), 1.0, 5.0, ((0, 16),), jnp.float32),
        "plan_step": jax.random.randint(streams_of[4], (1,), 0, 2 * WARM).astype(jnp.int32),
        "ln1_gain": jnp.clip(1.0 + 0.1 * jax.random.normal(streams_of[5], (D,), jnp.float32), 0.5, 1.5).astype(jnp.bfloat16),
        "w_qkv": gaussian(streams_of[6], (D, 3 * D), D ** -0.5, 0.1875, ((0, 32),)),
        "w_out": gaussian(streams_of[7], (D, D), (D // 16) ** -0.5, 0.75, ((0, 32),)),
        "ln2_gain": jnp.clip(1.0 + 0.1 * jax.random.normal(streams_of[8], (D,), jnp.float32), 0.5, 1.5).astype(jnp.bfloat16),
        "w_up": gaussian(streams_of[9], (D, FF), D ** -0.5, 0.1875, ((0, 32),)),
        "w_down": gaussian(streams_of[10], (FF, D), FF ** -0.5, 0.09375, ((0, 32),)),
        "w_latent": gaussian(streams_of[11], (D, 2 * LATENT), (4 * D) ** -0.5, 0.09375, ((0, 32),)),
        "w_decode": gaussian(streams_of[12], (LATENT, D), LATENT ** -0.5, 0.25, ((0, 32),)),
        "decode_bias": gaussian(streams_of[13], (D,), 0.5, 3.0, ((0, 32),)),
        "comp_mean": gaussian(streams_of[14], (COMPS, LATENT), 1.0, 4.0, ((1, 32),)),
        "comp_logvar": jnp.clip(jax.random.uniform(streams_of[15], (COMPS, LATENT), jnp.float32, -0.5, 0.5) * levels(streams_of[15], (COMPS, LATENT), ((1, 32),), -0.4, 0.0), -0.5, 0.5).astype(jnp.bfloat16),
    }


HIGHEST = lax.Precision.HIGHEST
FREE_BITS = 0.8
SOFTNESS = 0.2

@jax.custom_vjp
def low(v):
    return lax.optimization_barrier(v.astype(jnp.bfloat16)).astype(jnp.float32)

@jax.custom_vjp
def low_back(v):
    return v

def low_keep(v):
    return (low(v), None)

def low_pass(kept, grad):
    return (grad,)

def back_keep(v):
    return (v, None)

def back_low(kept, grad):
    return (low(grad),)
low.defvjp(low_keep, low_pass)
low_back.defvjp(back_keep, back_low)

def rounded(tensor):
    return low_back(low(tensor))

def matmul(left_side, right_side):
    return jnp.dot(left_side, right_side, precision=HIGHEST)

def layer_norm(tensor):
    centred = tensor - lax.optimization_barrier(jnp.mean(tensor, axis=-1, keepdims=True))
    return centred * lax.rsqrt(lax.optimization_barrier(jnp.mean(centred * centred, axis=-1, keepdims=True)) + 1e-05)

def attention(packed, segments):
    cell_count = packed.shape[0]
    model_width = packed.shape[1] // 3
    head_size = model_width // HEADS
    queries = packed[:, :model_width].reshape(cell_count, HEADS, head_size)
    key_rows = packed[:, model_width:2 * model_width].reshape(cell_count, HEADS, head_size)
    value_rows = packed[:, 2 * model_width:].reshape(cell_count, HEADS, head_size)
    scores = low_back(jnp.einsum('qhd,khd->hqk', queries, key_rows, precision=HIGHEST) * head_size ** (-0.5))
    same_slide = segments[:, None] == segments[None, :]
    scores = jnp.where(same_slide[None, :, :], scores, -1e+30)
    attn_weights = low(jax.nn.softmax(scores, axis=-1))
    mixed_rows = jnp.einsum('hqk,khd->qhd', attn_weights, value_rows, precision=HIGHEST)
    return mixed_rows.reshape(cell_count, model_width)

def phase_one(params, inputs, segments):
    gain_one, w_qkv, w_out, gain_two, w_up, w_down = params
    first_in = low(layer_norm(inputs) * gain_one)
    packed = rounded(matmul(first_in, w_qkv))
    mixed_rows = rounded(attention(packed, segments))
    middle = inputs + low_back(matmul(mixed_rows, w_out))
    second_in = low(layer_norm(middle) * gain_two)
    hidden = low(jax.nn.gelu(low_back(matmul(second_in, w_up)), approximate=False))
    return rounded(middle + low_back(matmul(hidden, w_down)))

def latent_piece(mean_part, logvar_part, noise_part, centre, spread):
    sample = mean_part + jnp.exp(0.5 * logvar_part) * noise_part
    gap = mean_part - centre
    diverge = 0.5 * (spread - logvar_part + (jnp.exp(logvar_part) + gap * gap) * jnp.exp(-spread) - 1.0)
    return (sample, diverge)

def phase_two(params, carried, mixture_block, noise_block):
    w_latent, w_decode, decode_bias, comp_mean, comp_logvar = params
    moments = low_back(matmul(carried, w_latent))
    centre = comp_mean[mixture_block]
    spread = comp_logvar[mixture_block]
    sample, diverge = latent_piece(moments[:, :LATENT], moments[:, LATENT:], noise_block, centre, spread)
    decoded = matmul(low(sample), w_decode) + decode_bias
    return (decoded, lax.optimization_barrier(jnp.sum(diverge, axis=0)))

def objective(params, inputs, cotangent, segment_ids, mixture_blocks, noise_blocks, kl_weight):
    first_params = params[:6]
    second_params = params[6:]

    def advance(running, block_data):
        inputs_block, cotangent_block, segment_block, mixture_block, noise_block = block_data
        carried = phase_one(first_params, inputs_block, segment_block)
        decoded, kl_part = phase_two(second_params, carried, mixture_block, noise_block)
        return ((running[0] + kl_part, running[1] + jnp.sum(decoded * cotangent_block)), decoded)
    start_state = (jnp.zeros((LATENT,), jnp.float32), jnp.zeros((), jnp.float32))
    (kl_total, recon), outputs = lax.scan(jax.checkpoint(advance), start_state, (inputs, cotangent, segment_ids, mixture_blocks, noise_blocks))
    kl_mean = kl_total / TOKENS
    floored = FREE_BITS + SOFTNESS * jax.nn.softplus((kl_mean - FREE_BITS) / SOFTNESS)
    return (recon + kl_weight * TOKENS * jnp.sum(floored), outputs)

def reference(layer_ends, segment_ids, mixture, noise, plan_step, ln1_gain, w_qkv, w_out, ln2_gain, w_up, w_down, w_latent, w_decode, decode_bias, comp_mean, comp_logvar):
    blocks = TOKENS // CELLS_MB
    ends_float = layer_ends.astype(jnp.float32)
    inputs = ends_float[0].reshape(blocks, CELLS_MB, D)
    cotangent = ends_float[1].reshape(blocks, CELLS_MB, D)
    mixture_blocks = mixture.reshape(blocks, CELLS_MB)
    noise_blocks = noise.astype(jnp.float32).reshape(blocks, CELLS_MB, LATENT)
    kl_weight = jnp.minimum(1.0, (plan_step[0] + 1).astype(jnp.float32) / WARM)
    params = tuple((weight.astype(jnp.float32) for weight in (ln1_gain, w_qkv, w_out, ln2_gain, w_up, w_down, w_latent, w_decode, decode_bias, comp_mean, comp_logvar)))

    def evaluate(param_set, data):
        return objective(param_set, data, cotangent, segment_ids, mixture_blocks, noise_blocks, kl_weight)
    objective_value, pull_back, outputs = jax.vjp(evaluate, params, inputs, has_aux=True)
    weight_grads, data_grad = pull_back(jnp.ones((), jnp.float32))
    result_ends = jnp.stack([data_grad.reshape(TOKENS, D), low(outputs).reshape(TOKENS, D)])
    return (result_ends, weight_grads[0], weight_grads[1], weight_grads[2], weight_grads[3], weight_grads[4], weight_grads[5], weight_grads[6], weight_grads[7], weight_grads[8], weight_grads[9], weight_grads[10])
```

```python
import functools

import jax
import jax.numpy as jnp
from jax import lax
from jax.experimental import pallas as pl
from jax.experimental.pallas import tpu as pltpu
from jax.sharding import PartitionSpec as P

HEADS = 16
WARM = 1000
HIGHEST = lax.Precision.HIGHEST
FREE_BITS = 0.8
SOFTNESS = 0.2
NEGATIVE = -1e30
EVERY = ("dp", "pipe")
LOW = jnp.bfloat16
FULL = jnp.float32


def after(value, *others):
    return lax.optimization_barrier((value,) + others)[0]


def swap_bits(mask):
    return (mask & 1) * 2 + (mask >> 1)


def send(value, even, odd):
    count = lax.axis_size("dp") * lax.axis_size("pipe")
    pairs = [(i, i ^ (odd if i & 1 else even)) for i in range(count)]
    return lax.ppermute(value, EVERY, pairs)


def send_core(value):
    return send(value, 1, 1)


def far_masks():
    return range(1, lax.axis_size("dp") // 4)


def far_exchange(value, mask):
    return send(value, mask * 8, mask * 8)


def near_first(value):
    return send(value, 2, 4)


def near_second(value):
    return send(value, 4, 2)


def place():
    return jnp.stack([lax.axis_index("dp"), lax.axis_index("pipe")]).astype(jnp.int32)


def slot_owner(place_ref, slot, far, other_core):
    turn, step = divmod(slot, far)
    core = place_ref[1]
    if other_core:
        core = 1 - core
    near = jnp.where(core == 0, turn, swap_bits(turn))
    return (place_ref[0] ^ (4 * step)) ^ near, core


def copy_through(copies, sems):
    into = [pltpu.make_async_copy(src, mid, sems.at[0, i]) for i, (src, mid, _) in enumerate(copies)]
    out = [pltpu.make_async_copy(mid, dst, sems.at[1, i]) for i, (_, mid, dst) in enumerate(copies)]
    for one in into:
        one.start()
    for one, two in zip(into, out):
        one.wait()
        two.start()
    for two in out:
        two.wait()


def unpack(parts, pieces):
    half, rows, cols = parts[0].shape
    far = half // 2
    count = half * 2

    def kernel(place_ref, own_a, own_b, other_a, other_b, *rest):
        outs = rest[: len(pieces)]
        middles, sems = rest[len(pieces) : -1], rest[-1]
        copies = []
        for refs, other in (((own_a, own_b), False), ((other_a, other_b), True)):
            for slot in range(count):
                dp_index, core = slot_owner(place_ref, slot, far, other)
                source = refs[slot // half].at[slot % half]
                for (row, height, col, width), middle, out in zip(pieces, middles, outs):
                    copies.append(
                        (
                            source.at[pl.ds(row, height), pl.ds(col, width)],
                            middle.at[dp_index, core],
                            out.at[dp_index, core],
                        )
                    )
        copy_through(copies, sems)

    anywhere = pl.BlockSpec(memory_space=pl.ANY)
    shapes = [(count, 2, p[1], p[3]) for p in pieces]
    size = 4 * count * rows * cols
    outs = pl.pallas_call(
        kernel,
        out_shape=[jax.ShapeDtypeStruct(shape, LOW) for shape in shapes],
        in_specs=[pl.BlockSpec(memory_space=pltpu.SMEM)] + [anywhere] * 4,
        out_specs=[anywhere] * len(pieces),
        scratch_shapes=[pltpu.VMEM(shape, LOW) for shape in shapes]
        + [pltpu.SemaphoreType.DMA((2, 2 * count * len(pieces)))],
        compiler_params=pltpu.CompilerParams(vmem_limit_bytes=size + (2 << 20)),
        cost_estimate=pl.CostEstimate(flops=0, bytes_accessed=2 * size, transcendentals=0),
        name="unpack",
    )(place(), *parts)
    return [o.reshape(count * 2 * p[1], p[3]) for o, p in zip(outs, pieces)]


def pack(grads, pieces, far):
    count = far * 4
    rows = max(p[0] + p[1] for p in pieces)
    cols = max(p[2] + p[3] for p in pieces)
    shaped = [g.reshape(count, 2, p[1], p[3]) for g, p in zip(grads, pieces)]

    def kernel(place_ref, *rest):
        ins = rest[: len(pieces)]
        outs, middles, sems = rest[len(pieces) : -3], rest[-3:-1], rest[-1]
        copies = []
        for out, middle, other in zip(outs, middles, (False, True)):
            for slot in range(count):
                dp_index, core = slot_owner(place_ref, slot, far, other)
                for (row, height, col, width), source in zip(pieces, ins):
                    copies.append(
                        (
                            source.at[dp_index, core],
                            middle.at[slot, pl.ds(row, height), pl.ds(col, width)],
                            out.at[slot, pl.ds(row, height), pl.ds(col, width)],
                        )
                    )
        copy_through(copies, sems)

    anywhere = pl.BlockSpec(memory_space=pl.ANY)
    size = 4 * count * rows * cols
    return pl.pallas_call(
        kernel,
        out_shape=[jax.ShapeDtypeStruct((count, rows, cols), LOW)] * 2,
        in_specs=[pl.BlockSpec(memory_space=pltpu.SMEM)] + [anywhere] * len(pieces),
        out_specs=[anywhere] * 2,
        scratch_shapes=[pltpu.VMEM((count, rows, cols), LOW)] * 2
        + [pltpu.SemaphoreType.DMA((2, 2 * count * len(pieces)))],
        compiler_params=pltpu.CompilerParams(vmem_limit_bytes=size + (2 << 20)),
        cost_estimate=pl.CostEstimate(flops=0, bytes_accessed=2 * size, transcendentals=0),
        name="pack",
    )(place(), *shaped)


def gather(shard, pieces):
    if shard.shape[0] % 16:
        whole = lax.all_gather(shard, EVERY, axis=0, tiled=False)
        return [
            whole[:, p[0] : p[0] + p[1], p[2] : p[2] + p[3]].reshape(-1, p[3]) for p in pieces
        ]
    block = shard[None]
    far = jnp.concatenate([block] + [far_exchange(block, m) for m in far_masks()], axis=0)
    eight = jnp.concatenate([far, near_first(far)], axis=0)
    rest = near_second(eight)
    return unpack((eight, rest, send_core(eight), send_core(rest)), pieces)


def add_low(one, two):
    return (one.astype(FULL) + two.astype(FULL)).astype(LOW)


def scatter(grads, pieces, rows):
    if rows % 16:
        count = lax.axis_size("dp") * 2
        height = max(p[0] + p[1] for p in pieces)
        columns = max(p[2] + p[3] for p in pieces)
        whole = jnp.zeros((count, height, columns), LOW)
        for grad, p in zip(grads, pieces):
            whole = whole.at[:, p[0] : p[0] + p[1], p[2] : p[2] + p[3]].set(
                grad.reshape(count, p[1], p[3])
            )
        return lax.psum_scatter(whole, EVERY, scatter_dimension=0, tiled=True)[0].astype(FULL)
    far = lax.axis_size("dp") // 4
    own, other = pack(grads, pieces, far)
    got = send_core(other)
    half = 2 * far
    outgoing = add_low(own[half:], got[half:])
    kept = add_low(own[:half], got[:half])
    got = near_second(outgoing)
    outgoing = add_low(kept[far:], got[far:])
    kept = add_low(kept[:far], got[:far])
    got = near_first(outgoing)
    total = kept.astype(FULL) + got.astype(FULL)
    low = total.astype(LOW)
    result = total[0]
    for mask in far_masks():
        result = result + far_exchange(low[mask : mask + 1], mask)[0].astype(FULL)
    return result


def sum_everywhere(value):
    bit = 1
    count = lax.axis_size("dp") * 2
    while bit < count:
        value = value + send(value, bit, bit)
        bit *= 2
    return value


def matmul(left_side, right_side):
    return jnp.dot(left_side, right_side, preferred_element_type=FULL)


def left_product(left_side, right_side):
    return lax.dot_general(
        left_side, right_side, (((0,), (0,)), ((), ())), preferred_element_type=FULL
    )


def right_product(left_side, right_side):
    return lax.dot_general(
        left_side, right_side, (((1,), (1,)), ((), ())), preferred_element_type=FULL
    )


def norm_parts(tensor):
    centred = tensor - jnp.mean(tensor, axis=-1, keepdims=True)
    scale = lax.rsqrt(jnp.mean(centred * centred, axis=-1, keepdims=True) + 1e-05)
    return centred * scale, scale


def norm_back(normed, scale, grad, gain):
    inner = grad * gain
    return scale * (
        inner
        - jnp.mean(inner, axis=-1, keepdims=True)
        - normed * jnp.mean(inner * normed, axis=-1, keepdims=True)
    )


def head_lanes(value, head, size):
    lane = lax.broadcasted_iota(jnp.int32, value.shape, 1)
    return jnp.where((lane // size) == head, value, jnp.zeros_like(value))


def attention_forward(packed, segments):
    cells, three = packed.shape
    width = three // 3
    size = width // HEADS
    pair = 128 // size
    steps = HEADS // pair

    def kernel(seg_col, seg_row, q_ref, k_ref, v_ref, out_ref, attn_ref):
        same = seg_col[...] == seg_row[...]
        queries, keys = q_ref[...], k_ref[...]
        values = jnp.transpose(v_ref[...])
        outs = []
        for head in range(pair):
            scores = right_product(head_lanes(keys, head, size), queries) * size ** (-0.5)
            scores = jnp.where(same, scores, NEGATIVE)
            powers = jnp.exp(scores - jnp.max(scores, axis=0, keepdims=True))
            attn = powers * (1.0 / jnp.sum(powers, axis=0, keepdims=True))
            attn_ref[head] = attn
            outs.append(matmul(values[head * size : (head + 1) * size], attn.astype(LOW)))
        out_ref[...] = jnp.transpose(jnp.concatenate(outs, axis=0)).astype(LOW)

    return pl.pallas_call(
        kernel,
        grid=(steps,),
        in_specs=[
            pl.BlockSpec((cells, 1), lambda i: (0, 0)),
            pl.BlockSpec((1, cells), lambda i: (0, 0)),
            pl.BlockSpec((cells, 128), lambda i: (0, i)),
            pl.BlockSpec((cells, 128), lambda i: (0, i + steps)),
            pl.BlockSpec((cells, 128), lambda i: (0, i + 2 * steps)),
        ],
        out_specs=[
            pl.BlockSpec((cells, 128), lambda i: (0, i)),
            pl.BlockSpec((pair, cells, cells), lambda i: (i, 0, 0)),
        ],
        out_shape=[
            jax.ShapeDtypeStruct((cells, width), LOW),
            jax.ShapeDtypeStruct((HEADS, cells, cells), FULL),
        ],
        compiler_params=pltpu.CompilerParams(vmem_limit_bytes=32 << 20),
        cost_estimate=pl.CostEstimate(
            flops=4 * cells * cells * width, bytes_accessed=24 << 20, transcendentals=cells * cells * HEADS
        ),
        name="attention_forward",
    )(segments[:, None], segments[None, :], packed, packed, packed)


def attention_backward(packed, attn, grad_mixed):
    cells, three = packed.shape
    width = three // 3
    size = width // HEADS
    pair = 128 // size
    steps = HEADS // pair

    def kernel(q_ref, k_ref, v_ref, g_ref, attn_ref, out_ref):
        queries, keys, values, grad = q_ref[...], k_ref[...], v_ref[...], g_ref[...]
        keys_t = jnp.transpose(keys)
        grad_q, grad_k, grad_v = [], 0.0, 0.0
        for head in range(pair):
            attn = attn_ref[head]
            grad_attn = right_product(head_lanes(values, head, size), grad)
            inner = jnp.sum(grad_attn * attn, axis=0, keepdims=True)
            grad_scores = (attn * (grad_attn - inner)).astype(LOW)
            grad_q.append(matmul(keys_t[head * size : (head + 1) * size], grad_scores))
            grad_k += head_lanes(matmul(grad_scores, queries), head, size)
            grad_v += head_lanes(matmul(attn.astype(LOW), grad), head, size)
        scale = size ** (-0.5)
        out_ref[0] = (jnp.transpose(jnp.concatenate(grad_q, axis=0)) * scale).astype(LOW)
        out_ref[1] = (grad_k * scale).astype(LOW)
        out_ref[2] = grad_v.astype(LOW)

    return pl.pallas_call(
        kernel,
        grid=(steps,),
        in_specs=[
            pl.BlockSpec((cells, 128), lambda i: (0, i)),
            pl.BlockSpec((cells, 128), lambda i: (0, i + steps)),
            pl.BlockSpec((cells, 128), lambda i: (0, i + 2 * steps)),
            pl.BlockSpec((cells, 128), lambda i: (0, i)),
            pl.BlockSpec((pair, cells, cells), lambda i: (i, 0, 0)),
        ],
        out_specs=pl.BlockSpec((3, cells, 128), lambda i: (0, 0, i)),
        out_shape=jax.ShapeDtypeStruct((3, cells, width), LOW),
        compiler_params=pltpu.CompilerParams(vmem_limit_bytes=32 << 20),
        cost_estimate=pl.CostEstimate(
            flops=10 * cells * cells * width, bytes_accessed=24 << 20, transcendentals=0
        ),
        name="attention_backward",
    )(packed, packed, packed, grad_mixed, attn)


def local(
    layer_ends,
    segment_ids,
    mixture,
    noise,
    plan_step,
    ln1_gain,
    w_qkv,
    w_out,
    ln2_gain,
    w_up,
    w_down,
    w_latent,
    w_decode,
    decode_bias,
    comp_mean,
    comp_logvar,
):
    core = lax.axis_index("pipe")
    cells = segment_ids.shape[1]
    devices = lax.axis_size("dp") * 2
    width = layer_ends.shape[2]
    latent = noise.shape[1]
    comps = comp_mean.shape[0]
    total_cells = cells * devices

    rows = w_qkv.shape[0]
    small = jnp.concatenate(
        [ln1_gain, ln2_gain, decode_bias, comp_mean.reshape(-1), comp_logvar.reshape(-1)]
    )
    small_count = small.shape[0]
    small = jnp.pad(small, (0, rows * 128 - small_count)).reshape(rows, 128)
    qkv_cols, out_cols, up_cols = w_qkv.shape[1], w_out.shape[1], w_up.shape[1]
    first_pieces = (
        (0, rows, 0, qkv_cols),
        (0, rows, qkv_cols, out_cols),
        (0, rows, qkv_cols + out_cols, 128),
    )
    up_pieces = ((0, rows, 0, up_cols),)
    down_rows, decode_rows = w_down.shape[0], w_decode.shape[0]
    down_pieces = ((0, down_rows, 0, width),)
    last_pieces = ((0, rows, 0, width), (rows, decode_rows, 0, width))
    qkv, out_proj, small_all = gather(
        jnp.concatenate([w_qkv, w_out, small], axis=1), first_pieces
    )
    (up,) = gather(w_up, up_pieces)
    (down,) = gather(w_down, down_pieces)
    to_latent, decode = gather(jnp.concatenate([w_latent, w_decode], axis=0), last_pieces)
    small_all = small_all.reshape(devices, rows * 128)
    piece = rows * 3
    gain_one = small_all[:, :rows].reshape(-1).astype(FULL)
    gain_two = small_all[:, rows : 2 * rows].reshape(-1).astype(FULL)
    bias = small_all[:, 2 * rows : 3 * rows].reshape(-1).astype(FULL)
    comp_cols = latent // devices

    def comp_table(start):
        flat = small_all[:, start : start + comps * comp_cols].reshape(devices, comps, comp_cols)
        return flat.transpose(1, 0, 2).reshape(comps, latent)

    means = comp_table(piece)
    spreads = comp_table(piece + comps * comp_cols)

    def my_rows(tensor, which):
        return lax.dynamic_slice_in_dim(tensor, which * cells, cells, axis=0)

    kept = my_rows(layer_ends[0], core)
    got = send_core(my_rows(layer_ends[0], 1 - core))
    inputs_low = jnp.where(core == 0, kept, got)
    cotangent = jnp.where(core == 0, got, kept)
    segments = lax.dynamic_index_in_dim(segment_ids, core, keepdims=False)
    mixture_rows = my_rows(mixture, core)
    noise_rows = my_rows(noise, core)

    inputs = inputs_low.astype(FULL)
    normed_one, scale_one = norm_parts(inputs)
    first_in = (normed_one * gain_one).astype(LOW)
    packed = matmul(first_in, qkv).astype(LOW)
    mixed, attn = attention_forward(packed, segments)
    middle = inputs + matmul(mixed, out_proj)
    normed_two, scale_two = norm_parts(middle)
    second_in = (normed_two * gain_two).astype(LOW)
    up_proj = matmul(second_in, up)
    gate = 0.5 * (1.0 + lax.erf(up_proj * (0.5**0.5)))
    hidden = (up_proj * gate).astype(LOW)
    slope = gate + up_proj * jnp.exp(-0.5 * up_proj * up_proj) * (0.5 / jnp.pi) ** 0.5
    carried = (middle + matmul(hidden, down)).astype(LOW)
    moments = matmul(carried, to_latent)
    mean_part, logvar = moments[:, :latent], moments[:, latent:]
    choose = mixture_rows[:, None] == jnp.arange(comps, dtype=jnp.int32)[None, :]
    centre = matmul(choose.astype(LOW), means)
    spread = matmul(choose.astype(LOW), spreads)
    deviation = jnp.exp(0.5 * logvar)
    sample = (mean_part + deviation * noise_rows).astype(LOW)
    gap = mean_part - centre
    shrink = jnp.exp(-spread)
    variance = jnp.exp(logvar)
    diverge = 0.5 * (spread - logvar + (variance + gap * gap) * shrink - 1.0)
    kl_sum = sum_everywhere(jnp.sum(diverge, axis=0))
    decoded = (matmul(sample, decode) + bias).astype(LOW)

    kl_weight = jnp.minimum(1.0, (plan_step[0] + 1).astype(FULL) / WARM)
    coef = kl_weight * jax.nn.sigmoid((kl_sum / total_cells - FREE_BITS) / SOFTNESS)
    grad_decode = left_product(sample, cotangent).astype(LOW)
    grad_bias = jnp.sum(cotangent.astype(FULL), axis=0)
    grad_sample = right_product(cotangent, decode)
    grad_centre = coef * (-(gap * shrink))
    grad_spread = coef * (1.0 - (variance + gap * gap) * shrink) * 0.5
    grad_mu = grad_sample - grad_centre
    grad_logvar = grad_sample * noise_rows * deviation * 0.5 + coef * (variance * shrink - 1.0) * 0.5
    grad_moments = jnp.concatenate([grad_mu, grad_logvar], axis=1).astype(LOW)
    chosen = choose.astype(FULL)
    table = (((0,), (0,)), ((), ()))
    grad_mean = lax.dot_general(chosen, grad_centre, table, precision=HIGHEST)
    grad_spreads = lax.dot_general(chosen, grad_spread, table, precision=HIGHEST)
    grad_latent = left_product(carried, grad_moments).astype(LOW)
    grad_carried = right_product(grad_moments, to_latent).astype(LOW)
    last_sum = scatter([grad_latent, grad_decode], last_pieces, rows + decode_rows)

    grad_down = left_product(hidden, grad_carried).astype(LOW)
    down_sum = scatter([grad_down], down_pieces, down_rows)
    grad_up_proj = (right_product(grad_carried, down) * slope).astype(LOW)
    grad_up = left_product(second_in, grad_up_proj).astype(LOW)
    up_sum = scatter([grad_up], up_pieces, rows)
    grad_second = right_product(grad_up_proj, up)
    grad_gain_two = jnp.sum(normed_two * grad_second, axis=0)
    grad_middle = grad_carried.astype(FULL) + norm_back(normed_two, scale_two, grad_second, gain_two)
    grad_branch = grad_middle.astype(LOW)
    grad_out = left_product(mixed, grad_branch).astype(LOW)
    grad_mixed = right_product(grad_branch, out_proj).astype(LOW)
    grad_packed = attention_backward(packed, attn, grad_mixed)
    grad_packed = jnp.concatenate([grad_packed[0], grad_packed[1], grad_packed[2]], axis=1)
    grad_qkv = left_product(first_in, grad_packed).astype(LOW)
    grad_first = right_product(grad_packed, qkv)
    grad_gain_one = jnp.sum(normed_one * grad_first, axis=0)
    grad_inputs = grad_middle + norm_back(normed_one, scale_one, grad_first, gain_one)

    def comp_rows(tensor):
        return tensor.reshape(comps, devices, comp_cols).transpose(1, 0, 2).reshape(devices, -1)

    small_grads = jnp.concatenate(
        [
            grad_gain_one.reshape(devices, rows),
            grad_gain_two.reshape(devices, rows),
            grad_bias.reshape(devices, rows),
            comp_rows(grad_mean),
            comp_rows(grad_spreads),
        ],
        axis=1,
    )
    small_grads = jnp.pad(small_grads, ((0, 0), (0, rows * 128 - small_count)))
    small_grads = small_grads.astype(LOW).reshape(devices * rows, 128)
    first_sum = scatter([grad_qkv, grad_out, small_grads], first_pieces, rows)

    decoded_there = send_core(decoded)
    inputs_there = send_core(grad_inputs)
    result = jnp.where(
        core == 0,
        jnp.concatenate([grad_inputs, inputs_there], axis=0),
        jnp.concatenate([decoded_there, decoded], axis=0).astype(FULL),
    )[None]
    small_sum = first_sum[:, qkv_cols + out_cols :].reshape(-1)
    comp_size = comps * comp_cols
    return (
        result,
        small_sum[:rows],
        first_sum[:, :qkv_cols],
        first_sum[:, qkv_cols : qkv_cols + out_cols],
        small_sum[rows : 2 * rows],
        up_sum,
        down_sum,
        last_sum[:rows],
        last_sum[rows:],
        small_sum[2 * rows : 3 * rows],
        small_sum[piece : piece + comp_size].reshape(comps, comp_cols),
        small_sum[piece + comp_size : piece + 2 * comp_size].reshape(comps, comp_cols),
    )


def solution(mesh):
    split = P(EVERY)
    wide = P(EVERY, None)
    tall = P(None, EVERY)
    ends = P("pipe", "dp", None)
    return jax.shard_map(
        local,
        mesh=mesh,
        in_specs=(
            ends,
            P("dp", None),
            P("dp"),
            P("dp", None),
            P(),
            split,
            wide,
            wide,
            split,
            wide,
            wide,
            wide,
            wide,
            split,
            tall,
            tall,
        ),
        out_specs=(ends, split, wide, wide, split, wide, wide, wide, wide, split, tall, tall),
        check_vma=False,
    )
```

```python
import functools

import jax
import jax.numpy as jnp
from jax import lax
from jax.experimental import pallas as pl
from jax.experimental.pallas import tpu as pltpu
from jax.sharding import PartitionSpec as P

HEADS = 16
WARM = 1000
FREE_BITS = 0.8
SOFTNESS = 0.2
NEGATIVE = -1e30
EVERY = ("dp", "pipe")
LOW = jnp.bfloat16
FULL = jnp.float32


def hold(*values):
    return lax.optimization_barrier(values)


def swap_bits(mask):
    return (mask & 1) * 2 + (mask >> 1)


def send(value, even, odd):
    count = lax.axis_size("dp") * lax.axis_size("pipe")
    pairs = [(i, i ^ (odd if i & 1 else even)) for i in range(count)]
    return lax.ppermute(value, EVERY, pairs)


def send_core(value):
    return send(value, 1, 1)


def far_masks():
    return range(1, lax.axis_size("dp") // 4)


def far_exchange(value, mask):
    return send(value, mask * 8, mask * 8)


def near_first(value):
    return send(value, 2, 4)


def near_second(value):
    return send(value, 4, 2)


def place():
    return jnp.stack([lax.axis_index("dp"), lax.axis_index("pipe")]).astype(jnp.int32)


def slot_owner(where, slot, far, other_core, far_first):
    turn, step = (slot // far, slot % far) if far_first else (slot % 4, slot // 4)
    core = where[1]
    if other_core:
        core = 1 - core
    near = jnp.where(core == 0, turn, swap_bits(turn))
    return (where[0] ^ (4 * step)) ^ near, core


def slot_of(where, dp_index, core, far, far_first):
    apart = dp_index ^ where[0]
    step, near = apart // 4, apart % 4
    turn = jnp.where(core == 0, near, swap_bits(near))
    slot = turn * far + step if far_first else step * 4 + turn
    return slot + jnp.where(core == where[1], 0, 4 * far)


def tables():
    far = lax.axis_size("dp") // 4
    slots = jnp.arange(4 * far)
    rows = []
    for far_first in (True, False):
        for other in (False, True):
            owner, core = slot_owner(place(), slots, far, other, far_first)
            rows.append(owner * 2 + core)
    blocks = jnp.arange(8 * far)
    back = slot_of(place(), blocks // 2, blocks % 2, far, True) % (4 * far)
    return jnp.concatenate(rows + [back]).astype(jnp.int32)


class Rows:
    def __init__(self, own, other, piece, far_first=True):
        self.piece = row, height, col, width = piece
        self.count = sum(part.shape[0] for part in own)
        self.base = 0 if far_first else 2 * self.count
        self.shape = (2 * self.count * height, width)
        self.slots = height % 16 == 0
        if self.slots:
            self.operands = list(own) + list(other)
        else:
            every = jnp.concatenate(list(own) + list(other), axis=0)
            index = jnp.arange(2 * self.count)
            picked = slot_of(place(), index // 2, index % 2, self.count // 4, far_first)
            picked = jnp.take(every, picked, axis=0)
            self.operands = [picked[:, row : row + height, col : col + width].reshape(self.shape)]

    def region(self, table, step):
        height = 8 * self.piece[1]
        start = ((table[0] // 8) ^ step) * height
        return pl.ds(pl.multiple_of(start, height), height)

    def start(self, table, refs, target, sems, by_step=False, columns=None):
        row, height, col, width = self.piece
        first, width = columns or (0, width)
        columns = pl.ds(first, width)
        far = self.count // 4
        if not self.slots:
            for step in range(far if by_step else 1):
                some = self.region(table, step) if by_step else pl.ds(0, self.shape[0])
                source = refs[0].at[some, columns]
                pltpu.make_async_copy(source, target.at[some, columns], sems.at[step]).start()
            return
        found = [ref.at[k] for ref in refs for k in range(ref.shape[0])]
        steps = [s % self.count % far if self.base == 0 else s % self.count // 4 for s in range(len(found))]
        for slot in sorted(range(len(found)), key=lambda s: steps[s]):
            block = pl.multiple_of(table[self.base + slot] * height, height)
            pltpu.make_async_copy(
                found[slot].at[pl.ds(row, height), pl.ds(col + first, width)],
                target.at[pl.ds(block, height), columns],
                sems.at[steps[slot] if by_step else 0],
            ).start()


def arrived(target, sem):
    pltpu.make_async_copy(target, target, sem).wait()


class Slots:
    def __init__(self, rows, cols, far_first=True):
        self.count = lax.axis_size("dp")
        self.base = 0 if far_first else 2 * self.count
        self.rows, self.cols = rows, cols

    def shapes(self):
        return [jax.ShapeDtypeStruct((self.count, self.rows, self.cols), LOW)] * 2

    def start(self, table, sources, outs, sem):
        for slot in range(2 * self.count):
            out = outs[slot // self.count].at[slot % self.count]
            for source, height, row, col in sources:
                block = pl.multiple_of(table[self.base + slot] * height, height)
                pltpu.make_async_copy(
                    source.at[pl.ds(block, height)],
                    out.at[pl.ds(row, height), pl.ds(col, source.shape[1])],
                    sem,
                ).start()


    def send(self, table, source, first_block, outs, sem):
        own_core = table[0] % 2
        for i in range(source.shape[0] // self.rows):
            slot = table[4 * self.count + first_block + i]
            part = source.at[pl.ds(i * self.rows, self.rows)]
            columns = pl.ds(0, source.shape[1])

            @pl.when(own_core == i % 2)
            def _():
                pltpu.make_async_copy(part, outs[0].at[slot, :, columns], sem).start()

            @pl.when(own_core != i % 2)
            def _():
                pltpu.make_async_copy(part, outs[1].at[slot, :, columns], sem).start()


ANYWHERE = pl.BlockSpec(memory_space=pl.ANY)
SCALARS = pl.BlockSpec(memory_space=pltpu.SMEM)
INSIDE = pl.BlockSpec(memory_space=pltpu.VMEM)


def whole(*shape):
    return pl.BlockSpec(shape, lambda *_: (0,) * len(shape))


def params(megabytes=60):
    return pltpu.CompilerParams(vmem_limit_bytes=megabytes << 20)


def cost(flops, bytes_accessed, transcendentals=0):
    return pl.CostEstimate(flops=1024, bytes_accessed=1024, transcendentals=0)


def region_columns(step, table):
    return (0, (table[0] // 8) ^ step)


def by_region(steps, in_specs, out_specs, scratch):
    return pltpu.PrefetchScalarGridSpec(
        num_scalar_prefetch=1,
        grid=(steps,),
        in_specs=in_specs,
        out_specs=out_specs,
        scratch_shapes=scratch,
    )


def first_kernel(table, normed, weight, small):
    cells, width = normed.shape
    cols, tile = weight.shape[1], 512
    parts = len(weight.operands)

    def kernel(table_ref, normed_ref, *rest):
        refs, rest = rest[:parts], rest[parts:]
        small_refs, rest = rest[: len(small.operands)], rest[len(small.operands) :]
        in_ref, packed_ref, small_ref, turned_ref, held, sems = rest
        step = pl.program_id(0)

        @pl.when(step == 0)
        def _():
            small.start(table_ref, small_refs, small_ref, sems.at[pl.ds(0, 1)])
            weight.start(table_ref, refs, held, sems.at[pl.ds(1, 1)], columns=(0, tile))
            weight.start(table_ref, refs, held, sems.at[pl.ds(2, 1)], columns=(tile, cols - tile))
            arrived(small_ref, sems.at[0])
            turned = jnp.transpose(small_ref[...].astype(FULL))
            turned_ref[...] = turned
            in_ref[...] = (normed_ref[...] * turned[0:1]).astype(LOW)
            arrived(held.at[:, pl.ds(0, tile)], sems.at[1])

        @pl.when(step == 1)
        def _():
            arrived(held.at[:, pl.ds(tile, cols - tile)], sems.at[2])

        columns = held[:, pl.ds(pl.multiple_of(step * tile, tile), tile)]
        packed_ref[...] = matmul(in_ref[...], columns).astype(LOW)

    return pl.pallas_call(
        kernel,
        grid=(cols // tile,),
        in_specs=[SCALARS, whole(cells, width)]
        + [ANYWHERE] * (parts + len(small.operands)),
        out_specs=[
            whole(cells, width),
            pl.BlockSpec((cells, tile), lambda i: (0, i)),
            whole(*small.shape),
            whole(128, small.shape[0]),
        ],
        out_shape=[
            jax.ShapeDtypeStruct((cells, width), LOW),
            jax.ShapeDtypeStruct((cells, cols), LOW),
            jax.ShapeDtypeStruct(small.shape, LOW),
            jax.ShapeDtypeStruct((128, small.shape[0]), FULL),
        ],
        scratch_shapes=[pltpu.VMEM(weight.shape, LOW), pltpu.SemaphoreType.DMA((3,))],
        compiler_params=params(),
        cost_estimate=cost(2 * cells * width * cols, 14 << 20),
        name="first",
    )(table, normed, *weight.operands, *small.operands)


def branch_kernel(table, mixed, inputs, turned, weight):
    cells, width = inputs.shape
    parts, tile = len(weight.operands), 256

    def kernel(table_ref, mixed_ref, in_ref, turned_ref, *rest):
        refs, (middle_ref, second_ref, held, sems) = rest[:parts], rest[parts:]

        @pl.when(pl.program_id(0) == 0)
        def _():
            weight.start(table_ref, refs, held, sems)
            arrived(held, sems.at[0])

        middle = in_ref[...] + matmul(mixed_ref[...], held[...])
        middle_ref[...] = middle
        second_ref[...] = (norm_parts(middle)[0] * turned_ref[1:2]).astype(LOW)

    cut = pl.BlockSpec((tile, width), lambda i: (i, 0))
    return pl.pallas_call(
        kernel,
        grid=(cells // tile,),
        in_specs=[SCALARS, cut, cut, pl.BlockSpec((8, width), lambda i: (0, 0))]
        + [ANYWHERE] * parts,
        out_specs=[cut, cut],
        out_shape=[
            jax.ShapeDtypeStruct((cells, width), FULL),
            jax.ShapeDtypeStruct((cells, width), LOW),
        ],
        scratch_shapes=[pltpu.VMEM(weight.shape, LOW), pltpu.SemaphoreType.DMA((1,))],
        compiler_params=params(),
        cost_estimate=cost(2 * cells * width * width, 9 << 20),
        name="branch",
    )(table, mixed, inputs, turned, *weight.operands)


def up_kernel(table, second_in, weight):
    cells, width = second_in.shape
    cols, tile = weight.shape[1], 512
    parts = len(weight.operands)

    def kernel(table_ref, in_ref, *rest):
        refs, (hidden_ref, slope_ref, held, sems) = rest[:parts], rest[parts:]
        step = pl.program_id(0)

        @pl.when(step == 0)
        def _():
            weight.start(table_ref, refs, held, sems.at[pl.ds(0, 1)], columns=(0, tile))
            weight.start(table_ref, refs, held, sems.at[pl.ds(1, 1)], columns=(tile, cols - tile))
            arrived(held.at[:, pl.ds(0, tile)], sems.at[0])

        @pl.when(step == 1)
        def _():
            arrived(held.at[:, pl.ds(tile, cols - tile)], sems.at[1])

        columns = held[:, pl.ds(pl.multiple_of(step * tile, tile), tile)]
        up_proj = matmul(in_ref[...], columns)
        gate = 0.5 + 0.5 * lax.erf(up_proj * (0.5**0.5))
        hidden_ref[...] = (up_proj * gate).astype(LOW)
        bell = jnp.exp(-0.5 * up_proj * up_proj) * (0.5 / jnp.pi) ** 0.5
        slope_ref[...] = (gate + up_proj * bell).astype(LOW)

    return pl.pallas_call(
        kernel,
        grid=(cols // tile,),
        in_specs=[SCALARS, whole(cells, width)] + [ANYWHERE] * parts,
        out_specs=[pl.BlockSpec((cells, tile), lambda i: (0, i))] * 2,
        out_shape=[
            jax.ShapeDtypeStruct((cells, cols), LOW),
            jax.ShapeDtypeStruct((cells, cols), LOW),
        ],
        scratch_shapes=[pltpu.VMEM(weight.shape, LOW), pltpu.SemaphoreType.DMA((2,))],
        compiler_params=params(),
        cost_estimate=cost(2 * cells * width * cols, 22 << 20, 2 * cells * cols),
        name="up",
    )(table, second_in, *weight.operands)


def latent_kernel(table, hidden, middle, noise, centre, spread, down, to_latent):
    cells, width = middle.shape
    latent = noise.shape[1]
    parts, more = len(down.operands), len(to_latent.operands)
    steps = down.count // 4
    tile = hidden.shape[1] // steps

    def kernel(table_ref, hidden_ref, mid_ref, noise_ref, centre_ref, spread_ref, *rest):
        refs, rest = rest[:parts], rest[parts:]
        latent_refs, rest = rest[:more], rest[more:]
        carried_ref, moments_ref, sample_ref, kl_ref, total, held, latent_held, sems = rest
        step = pl.program_id(0)

        @pl.when(step == 0)
        def _():
            down.start(table_ref, refs, held, sems, True)
            to_latent.start(table_ref, latent_refs, latent_held, sems.at[pl.ds(steps, 1)])
            total[...] = mid_ref[...]

        some = held.at[down.region(table_ref, step)]
        arrived(some, sems.at[step])
        total[...] += matmul(hidden_ref[...], some[...])

        @pl.when(step == steps - 1)
        def _():
            carried_ref[...] = total[...].astype(LOW)
            arrived(latent_held, sems.at[steps])
            moments_ref[...] = matmul(carried_ref[...], latent_held[...])
            mean_part, logvar = moments_ref[:, :latent], moments_ref[:, latent:]
            sample_ref[...] = (mean_part + jnp.exp(0.5 * logvar) * noise_ref[...]).astype(LOW)
            gap, far = mean_part - centre_ref[...], spread_ref[...]
            diverge = 0.5 * (far - logvar + (jnp.exp(logvar) + gap * gap) * jnp.exp(-far) - 1.0)
            kl_ref[...] = jnp.sum(diverge, axis=0, keepdims=True)

    return pl.pallas_call(
        kernel,
        grid_spec=by_region(
            steps,
            [pl.BlockSpec((cells, tile), region_columns), whole(cells, width)]
            + [whole(cells, latent)] * 3
            + [ANYWHERE] * (parts + more),
            [whole(cells, width), whole(cells, 2 * latent), whole(cells, latent), whole(1, latent)],
            [
                pltpu.VMEM((cells, width), FULL),
                pltpu.VMEM(down.shape, LOW),
                pltpu.VMEM(to_latent.shape, LOW),
                pltpu.SemaphoreType.DMA((steps + 1,)),
            ],
        ),
        out_shape=[
            jax.ShapeDtypeStruct((cells, width), LOW),
            jax.ShapeDtypeStruct((cells, 2 * latent), FULL),
            jax.ShapeDtypeStruct((cells, latent), LOW),
            jax.ShapeDtypeStruct((1, latent), FULL),
        ],
        compiler_params=params(),
        cost_estimate=cost(2 * cells * width * (hidden.shape[1] + width), 20 << 20),
        name="latent",
    )(table, hidden, middle, noise, centre, spread, *down.operands, *to_latent.operands)


def decode_kernel(table, sample, cotangent, turned, decode):
    cells, width = cotangent.shape
    latent = sample.shape[1]
    parts = len(decode.operands)

    def kernel(table_ref, sample_ref, dy_ref, turned_ref, *rest):
        refs, (out_ref, grad_ref, back_ref, bias_ref, held, sem) = rest[:parts], rest[parts:]
        decode.start(table_ref, refs, held, sem)
        grad_ref[...] = left_product(sample_ref[...], dy_ref[...]).astype(LOW)
        bias_ref[...] = jnp.sum(dy_ref[...].astype(FULL), axis=0, keepdims=True)
        arrived(held, sem.at[0])
        back_ref[...] = right_product(dy_ref[...], held[...])
        out_ref[...] = (matmul(sample_ref[...], held[...]) + turned_ref[2:3]).astype(LOW)

    return pl.pallas_call(
        kernel,
        in_specs=[SCALARS] + [INSIDE] * 3 + [ANYWHERE] * parts,
        out_specs=[INSIDE] * 4,
        out_shape=[
            jax.ShapeDtypeStruct((cells, width), LOW),
            jax.ShapeDtypeStruct((latent, width), LOW),
            jax.ShapeDtypeStruct((cells, latent), FULL),
            jax.ShapeDtypeStruct((1, width), FULL),
        ],
        scratch_shapes=[pltpu.VMEM(decode.shape, LOW), pltpu.SemaphoreType.DMA((1,))],
        compiler_params=params(),
        cost_estimate=cost(6 * cells * width * latent, 8 << 20),
        name="decode",
    )(table, sample, cotangent, turned, *decode.operands)


def factors_kernel(back, moments, noise, centre, spread, choose):
    cells, latent = noise.shape
    comps = choose.shape[1]

    def kernel(back_ref, mom_ref, noise_ref, centre_ref, spread_ref, choose_ref, plain_ref, factor_ref, comp_ref):
        mean_part, logvar = mom_ref[:, :latent], mom_ref[:, latent:]
        gap, shrink = mean_part - centre_ref[...], jnp.exp(-spread_ref[...])
        ratio = jnp.exp(logvar) * shrink
        moved = gap * shrink
        factor_ref[:, :latent] = moved
        factor_ref[:, latent:] = (ratio - 1.0) * 0.5
        for i, value in enumerate((-moved, (1.0 - (ratio + gap * moved)) * 0.5)):
            high = value.astype(LOW)
            rest = (value - high.astype(FULL)).astype(LOW)
            chosen = choose_ref[...]
            comp_ref[i] = left_product(chosen, high) + left_product(chosen, rest)
        back = back_ref[...]
        plain_ref[:, :latent] = back
        plain_ref[:, latent:] = back * noise_ref[...] * jnp.exp(0.5 * logvar) * 0.5

    return pl.pallas_call(
        kernel,
        in_specs=[INSIDE] * 6,
        out_specs=[INSIDE] * 3,
        out_shape=[
            jax.ShapeDtypeStruct((cells, 2 * latent), FULL),
            jax.ShapeDtypeStruct((cells, 2 * latent), FULL),
            jax.ShapeDtypeStruct((2, comps, latent), FULL),
        ],
        compiler_params=params(),
        cost_estimate=cost(200 * cells * latent, 10 << 20),
        name="factors",
    )(back, moments, noise, centre, spread, choose)


def plain_slots(slots, grads):
    far = slots.count // 4
    results = []
    for other in (False, True):
        owner, core = slot_owner(place(), jnp.arange(slots.count), far, other, slots.base == 0)
        result = jnp.zeros((slots.count, slots.rows, slots.cols), LOW)
        for grad, height, row, col in grads:
            blocks = grad.reshape(slots.count, 2, height, grad.shape[1])
            blocks = jnp.take(blocks[:, core], owner, axis=0)
            result = result.at[:, row : row + height, col : col + grad.shape[1]].set(blocks)
        results.append(result)
    return results


def moments_kernel(table, kl_weight, total, kl_sum, plain, factor, carried, comp, grad_decode, to_latent, slots):
    cells, width = carried.shape
    latent = kl_sum.shape[1]
    parts = len(to_latent.operands)
    height = to_latent.piece[1]
    decode_height = grad_decode.shape[0] // (2 * slots.count)
    direct = height % 16 == 0 and decode_height % 16 == 0

    def kernel(table_ref, weight_ref, kl_ref, plain_ref, factor_ref, carried_ref, comp_ref, gd_ref, *rest):
        refs, rest = rest[:parts], rest[parts:]
        gc_ref, comp_out, *rest = rest
        outs, rest = rest[: 2 if direct else 1], rest[2 if direct else 1 :]
        held, grads, sums, sems = rest
        to_latent.start(table_ref, refs, held, sems.at[pl.ds(0, 1)])
        mean = kl_ref[...] * (1.0 / total)
        coef = weight_ref[0] * jax.nn.sigmoid((mean - FREE_BITS) * (1.0 / SOFTNESS))
        for i in range(2):
            some = pl.ds(i * latent, latent)
            comp_out[i] = comp_ref[i] * coef
            grads[:, some] = (plain_ref[:, some] + factor_ref[:, some] * coef).astype(LOW)
        sums[...] = left_product(carried_ref[...], grads[...]).astype(LOW)
        if direct:
            slots.start(
                table_ref, [(sums, height, 0, 0), (gd_ref, decode_height, height, 0)], outs, sems.at[1]
            )
        else:
            outs[0][...] = sums[...]
        arrived(held, sems.at[0])
        gc_ref[...] = right_product(grads[...], held[...]).astype(LOW)
        if direct:
            arrived(outs[0], sems.at[1])
            arrived(outs[1], sems.at[1])

    results = pl.pallas_call(
        kernel,
        in_specs=[SCALARS, SCALARS] + [INSIDE] * 6 + [ANYWHERE] * parts,
        out_specs=[INSIDE] * 2 + ([ANYWHERE] * 2 if direct else [INSIDE]),
        out_shape=[
            jax.ShapeDtypeStruct((cells, width), LOW),
            jax.ShapeDtypeStruct(comp.shape, FULL),
        ]
        + (slots.shapes() if direct else [jax.ShapeDtypeStruct((width, 2 * latent), LOW)]),
        scratch_shapes=[
            pltpu.VMEM(to_latent.shape, LOW),
            pltpu.VMEM((cells, 2 * latent), LOW),
            pltpu.VMEM((width, 2 * latent), LOW),
            pltpu.SemaphoreType.DMA((2,)),
        ],
        compiler_params=params(),
        cost_estimate=cost(8 * cells * width * latent, 16 << 20),
        name="moments",
    )(table, kl_weight, kl_sum, plain, factor, carried, comp, grad_decode, *to_latent.operands)
    if direct:
        return results
    grads = [(results[2], height, 0, 0), (grad_decode, decode_height, height, 0)]
    return list(results[:2]) + plain_slots(slots, grads)


def weight_grad(table, left, rights, slots, height, name, extra=()):
    cells, rows = left.shape
    each = rights[0].shape[1]
    cols = each * len(rights)
    direct = height % 16 == 0
    tile = 512 if cols <= 1024 else 256
    steps = rows // tile
    extra = list(extra)

    def product(left_ref, right_refs, target):
        turned = jnp.transpose(left_ref[...])
        for i, right_ref in enumerate(right_refs):
            target[:, pl.ds(i * each, each)] = matmul(turned, right_ref[...]).astype(LOW)

    def kernel(table_ref, left_ref, *rest):
        right_refs, rest = rest[: len(rights)], rest[len(rights) :]
        if not direct:
            product(left_ref, right_refs, rest[0])
            return
        more, (own, other, sums, sems) = rest[: len(extra)], rest[len(extra) :]
        step = pl.program_id(0)

        @pl.when(step == 0)
        def _():
            for ref, one in zip(more, extra):
                slots.start(table_ref, [(ref, one[1], one[2], one[3])], (own, other), sems.at[2])

        current = lax.rem(step, 2)

        @pl.when(step >= 2)
        def _():
            arrived(sums.at[current], sems.at[current])

        product(left_ref, right_refs, sums.at[current])
        slots.send(table_ref, sums.at[current], step * (tile // height), (own, other), sems.at[current])

        @pl.when(step == steps - 1)
        def _():
            arrived(sums.at[0], sems.at[0])
            arrived(sums.at[1], sems.at[1])
            for ref in more:
                arrived(ref, sems.at[2])

    results = pl.pallas_call(
        kernel,
        grid=(steps,),
        in_specs=[SCALARS, pl.BlockSpec((cells, tile), lambda i: (0, i))]
        + [whole(cells, each)] * len(rights)
        + [whole(*one[0].shape) for one in (extra if direct else [])],
        out_specs=[ANYWHERE] * 2 if direct else [pl.BlockSpec((tile, cols), lambda i: (i, 0))],
        out_shape=slots.shapes() if direct else [jax.ShapeDtypeStruct((rows, cols), LOW)],
        scratch_shapes=[pltpu.VMEM((2, tile, cols), LOW), pltpu.SemaphoreType.DMA((3,))]
        if direct
        else [],
        compiler_params=params(),
        cost_estimate=cost(2 * cells * rows * cols, 2 * rows * cols),
        name=name,
    )(table, left, *rights, *[one[0] for one in (extra if direct else [])])
    if direct:
        return results
    return plain_slots(slots, [(results[0], height, 0, 0)] + extra)


def up_back_kernel(table, grad_carried, slope, down):
    cells, width = grad_carried.shape
    cols = slope.shape[1]
    parts = len(down.operands)
    steps = down.count // 4
    tile = cols // steps

    def kernel(table_ref, grad_ref, slope_ref, *rest):
        refs, (out_ref, held, sems) = rest[:parts], rest[parts:]
        step = pl.program_id(0)

        @pl.when(step == 0)
        def _():
            down.start(table_ref, refs, held, sems, True)

        some = held.at[down.region(table_ref, step)]
        arrived(some, sems.at[step])
        out_ref[...] = (right_product(grad_ref[...], some[...]) * slope_ref[...]).astype(LOW)

    return pl.pallas_call(
        kernel,
        grid_spec=by_region(
            steps,
            [whole(cells, width), pl.BlockSpec((cells, tile), region_columns)]
            + [ANYWHERE] * parts,
            pl.BlockSpec((cells, tile), region_columns),
            [pltpu.VMEM(down.shape, LOW), pltpu.SemaphoreType.DMA((steps,))],
        ),
        out_shape=jax.ShapeDtypeStruct((cells, cols), LOW),
        compiler_params=params(),
        cost_estimate=cost(2 * cells * width * cols, 22 << 20),
        name="up_back",
    )(table, grad_carried, slope, *down.operands)


def middle_back_kernel(table, grad_up_proj, grad_carried, middle, turned, up, out_proj):
    cells, width = grad_carried.shape
    cols = grad_up_proj.shape[1]
    parts, more = len(up.operands), len(out_proj.operands)

    def kernel(table_ref, gu_ref, gc_ref, mid_ref, turned_ref, *rest):
        refs, rest = rest[:parts], rest[parts:]
        out_refs, rest = rest[:more], rest[more:]
        gm_ref, gb_ref, gx_ref, gain_ref, gu_held, second, held, out_held, sems = rest
        loading = pltpu.make_async_copy(gu_ref, gu_held, sems.at[2])
        loading.start()
        up.start(table_ref, refs, held, sems)
        out_proj.start(table_ref, out_refs, out_held, sems.at[pl.ds(1, 1)])
        loading.wait()
        arrived(held, sems.at[0])
        for column in range(0, width, 512):
            some = pl.ds(column, 512)
            second[:, some] = right_product(gu_held[...], held[some])
        normed, scale = norm_parts(mid_ref[...])
        grad_second = second[...]
        gain_ref[...] = jnp.sum(normed * grad_second, axis=0, keepdims=True)
        back = norm_back(normed, scale, grad_second, turned_ref[1:2])
        grad_middle = gc_ref[...].astype(FULL) + back
        gm_ref[...] = grad_middle
        gb_ref[...] = grad_middle.astype(LOW)
        arrived(out_held, sems.at[1])
        gx_ref[...] = right_product(gb_ref[...], out_held[...]).astype(LOW)

    return pl.pallas_call(
        kernel,
        in_specs=[SCALARS, ANYWHERE] + [INSIDE] * 3 + [ANYWHERE] * (parts + more),
        out_specs=[INSIDE] * 4,
        out_shape=[
            jax.ShapeDtypeStruct((cells, width), FULL),
            jax.ShapeDtypeStruct((cells, width), LOW),
            jax.ShapeDtypeStruct((cells, width), LOW),
            jax.ShapeDtypeStruct((1, width), FULL),
        ],
        scratch_shapes=[
            pltpu.VMEM((cells, cols), LOW),
            pltpu.VMEM((cells, width), FULL),
            pltpu.VMEM(up.shape, LOW),
            pltpu.VMEM(out_proj.shape, LOW),
            pltpu.SemaphoreType.DMA((3,)),
        ],
        compiler_params=params(),
        cost_estimate=cost(2 * cells * width * (cols + width), 22 << 20),
        name="middle_back",
    )(table, grad_up_proj, grad_carried, middle, turned, *up.operands, *out_proj.operands)


def input_back_kernel(table, grad_packed, grad_middle, inputs, turned, weight):
    cells, width = inputs.shape
    parts = len(weight.operands)

    def kernel(table_ref, gq_ref, gk_ref, gv_ref, gm_ref, in_ref, turned_ref, *rest):
        refs, (gx_ref, gain_ref, first, held, sems) = rest[:parts], rest[parts:]
        weight.start(table_ref, refs, held, sems)
        normed, scale = norm_parts(in_ref[...])
        arrived(held, sems.at[0])
        for column in range(0, width, 512):
            some = pl.ds(column, 512)
            first[:, some] = sum(
                right_product(ref[...], held[some, i * width : (i + 1) * width])
                for i, ref in enumerate((gq_ref, gk_ref, gv_ref))
            )
        grad_first = first[...]
        gain_ref[...] = jnp.sum(normed * grad_first, axis=0, keepdims=True)
        gx_ref[...] = gm_ref[...] + norm_back(normed, scale, grad_first, turned_ref[0:1])

    return pl.pallas_call(
        kernel,
        in_specs=[SCALARS] + [INSIDE] * 6 + [ANYWHERE] * parts,
        out_specs=[INSIDE] * 2,
        out_shape=[
            jax.ShapeDtypeStruct((cells, width), FULL),
            jax.ShapeDtypeStruct((1, width), FULL),
        ],
        scratch_shapes=[
            pltpu.VMEM((cells, width), FULL),
            pltpu.VMEM(weight.shape, LOW),
            pltpu.SemaphoreType.DMA((1,)),
        ],
        compiler_params=params(),
        cost_estimate=cost(6 * cells * width * width, 18 << 20),
        name="input_back",
    )(table, *grad_packed, grad_middle, inputs, turned, *weight.operands)


def small_block(columns, rest):
    rows = rest.shape[0]
    gap = jnp.zeros((rows, 16 - len(columns)), rest.dtype)
    end = jnp.zeros((rows, 112 - rest.shape[1]), rest.dtype)
    return jnp.concatenate([*columns, gap, rest, end], axis=1)


def join(*parts):
    return jnp.concatenate(parts, axis=0)


def far_start(block):
    return [far_exchange(block, mask) for mask in far_masks()]


def add_low(one, two):
    return (one.astype(FULL) + two.astype(FULL)).astype(LOW)


def add_all(first, others):
    total = first.astype(FULL)
    for one in others:
        total = total + one.astype(FULL)
    return total


def far_slots(value, size):
    return [far_exchange(value[m * size : (m + 1) * size], m) for m in far_masks()]


def matmul(left_side, right_side):
    return jnp.dot(left_side, right_side, preferred_element_type=FULL)


def left_product(left_side, right_side):
    return lax.dot_general(
        left_side, right_side, (((0,), (0,)), ((), ())), preferred_element_type=FULL
    )


def right_product(left_side, right_side):
    return lax.dot_general(
        left_side, right_side, (((1,), (1,)), ((), ())), preferred_element_type=FULL
    )


def norm_parts(tensor):
    centred = tensor - jnp.mean(tensor, axis=-1, keepdims=True)
    scale = lax.rsqrt(jnp.mean(centred * centred, axis=-1, keepdims=True) + 1e-05)
    return centred * scale, scale


def norm_back(normed, scale, grad, gain):
    inner = grad * gain
    return scale * (
        inner
        - jnp.mean(inner, axis=-1, keepdims=True)
        - normed * jnp.mean(inner * normed, axis=-1, keepdims=True)
    )


def head_lanes(value, head, size):
    lane = lax.broadcasted_iota(jnp.int32, value.shape, 1)
    return jnp.where((lane // size) == head, value, jnp.zeros_like(value))


def attention_forward(packed, segments):
    cells, three = packed.shape
    width = three // 3
    size = width // HEADS
    pair = 128 // size
    steps = HEADS // pair

    def kernel(seg_col, seg_row, q_ref, k_ref, v_ref, out_ref, attn_ref):
        same = seg_col[...] == seg_row[...]
        queries, keys = q_ref[...], k_ref[...]
        values = jnp.transpose(v_ref[...])
        outs = []
        for head in range(pair):
            scores = right_product(head_lanes(keys, head, size), queries) * size ** (-0.5)
            scores = jnp.where(same, scores, NEGATIVE)
            powers = jnp.exp(scores - jnp.max(scores, axis=0, keepdims=True))
            attn = powers * (1.0 / jnp.sum(powers, axis=0, keepdims=True))
            attn_low = attn.astype(LOW)
            attn_ref[head] = attn_low
            outs.append(matmul(values[head * size : (head + 1) * size], attn_low))
        out_ref[...] = jnp.transpose(jnp.concatenate(outs, axis=0)).astype(LOW)

    return pl.pallas_call(
        kernel,
        grid=(steps,),
        in_specs=[
            pl.BlockSpec((cells, 1), lambda i: (0, 0)),
            pl.BlockSpec((1, cells), lambda i: (0, 0)),
            pl.BlockSpec((cells, 128), lambda i: (0, i)),
            pl.BlockSpec((cells, 128), lambda i: (0, i + steps)),
            pl.BlockSpec((cells, 128), lambda i: (0, i + 2 * steps)),
        ],
        out_specs=[
            pl.BlockSpec((cells, 128), lambda i: (0, i)),
            pl.BlockSpec((pair, cells, cells), lambda i: (i, 0, 0)),
        ],
        out_shape=[
            jax.ShapeDtypeStruct((cells, width), LOW),
            jax.ShapeDtypeStruct((HEADS, cells, cells), LOW),
        ],
        compiler_params=params(),
        cost_estimate=cost(4 * cells * cells * width, 24 << 20),
        name="attention_forward",
    )(segments[:, None], segments[None, :], packed, packed, packed)


def attention_backward(packed, attn, grad_mixed):
    cells, three = packed.shape
    width = three // 3
    size = width // HEADS
    pair = 128 // size
    steps = HEADS // pair

    def kernel(q_ref, k_ref, v_ref, g_ref, attn_ref, gq_ref, gk_ref, gv_ref):
        queries, keys, values, grad = q_ref[...], k_ref[...], v_ref[...], g_ref[...]
        keys_t = jnp.transpose(keys)
        grad_q, grad_k, grad_v = [], 0.0, 0.0
        for head in range(pair):
            attn_low = attn_ref[head]
            attn = attn_low.astype(FULL)
            grad_attn = right_product(head_lanes(values, head, size), grad)
            inner = jnp.sum(grad_attn * attn, axis=0, keepdims=True)
            grad_scores = (attn * (grad_attn - inner)).astype(LOW)
            grad_q.append(matmul(keys_t[head * size : (head + 1) * size], grad_scores))
            grad_k += head_lanes(matmul(grad_scores, queries), head, size)
            grad_v += head_lanes(matmul(attn_low, grad), head, size)
        scale = size ** (-0.5)
        gq_ref[...] = (jnp.transpose(jnp.concatenate(grad_q, axis=0)) * scale).astype(LOW)
        gk_ref[...] = (grad_k * scale).astype(LOW)
        gv_ref[...] = grad_v.astype(LOW)

    return pl.pallas_call(
        kernel,
        grid=(steps,),
        in_specs=[
            pl.BlockSpec((cells, 128), lambda i: (0, i)),
            pl.BlockSpec((cells, 128), lambda i: (0, i + steps)),
            pl.BlockSpec((cells, 128), lambda i: (0, i + 2 * steps)),
            pl.BlockSpec((cells, 128), lambda i: (0, i)),
            pl.BlockSpec((pair, cells, cells), lambda i: (i, 0, 0)),
        ],
        out_specs=[pl.BlockSpec((cells, 128), lambda i: (0, i))] * 3,
        out_shape=[jax.ShapeDtypeStruct((cells, width), LOW)] * 3,
        compiler_params=params(),
        cost_estimate=cost(10 * cells * cells * width, 24 << 20),
        name="attention_backward",
    )(packed, packed, packed, grad_mixed, attn)


def local(
    layer_ends,
    segment_ids,
    mixture,
    noise,
    plan_step,
    ln1_gain,
    w_qkv,
    w_out,
    ln2_gain,
    w_up,
    w_down,
    w_latent,
    w_decode,
    decode_bias,
    comp_mean,
    comp_logvar,
):
    core = lax.axis_index("pipe")
    cells = segment_ids.shape[1]
    devices = lax.axis_size("dp") * 2
    width = layer_ends.shape[2]
    latent = noise.shape[1]
    comps = comp_mean.shape[0]
    total_cells = cells * devices

    rows = w_qkv.shape[0]
    comp_cols = latent // devices
    lanes = 2 * comps * comp_cols // rows
    small = jnp.concatenate([comp_mean.reshape(-1), comp_logvar.reshape(-1)]).reshape(rows, lanes)
    columns = [ln1_gain[:, None], ln2_gain[:, None], decode_bias[:, None]]
    small = small_block(columns, small)
    qkv_cols, out_cols, up_cols = w_qkv.shape[1], w_out.shape[1], w_up.shape[1]
    first_pieces = (
        (0, rows, 0, qkv_cols),
        (0, rows, qkv_cols, out_cols),
        (0, rows, qkv_cols + out_cols, 128),
    )
    up_pieces = ((0, rows, 0, up_cols),)
    down_rows, decode_rows = w_down.shape[0], w_decode.shape[0]
    down_pieces = ((0, down_rows, 0, width),)
    last_pieces = ((0, rows, 0, width), (rows, decode_rows, 0, width))
    first_block = jnp.concatenate([w_qkv, w_out, small], axis=1)[None]
    up_block, down_block = w_up[None], w_down[None]
    last_block = jnp.concatenate([w_latent, w_decode], axis=0)[None]

    def my_rows(tensor, which):
        return lax.dynamic_slice_in_dim(tensor, which * cells, cells, axis=0)

    kept = my_rows(layer_ends[0], core)
    going = my_rows(layer_ends[0], 1 - core)
    segments = lax.dynamic_index_in_dim(segment_ids, core, keepdims=False)
    mixture_rows = my_rows(mixture, core)
    noise_rows = my_rows(noise, core)

    table = tables()
    first_far = far_start(first_block)
    got = send_core(going)
    last_near = near_first(last_block)
    got, last_near = hold(got, last_near)
    inputs = jnp.where(core == 0, kept, got).astype(FULL)
    cotangent = jnp.where(core == 0, got, kept)
    normed_one, scale_one = norm_parts(inputs)
    last_two = join(last_block, last_near)
    last_more = near_second(last_two)
    last_more, normed_one, up_block, *first_far = hold(
        last_more, normed_one, up_block, *first_far
    )
    last_four = join(last_two, last_more)

    first_four = join(first_block, *first_far)
    first_m1, first_m2 = near_first(first_four), near_second(first_four)
    up_far = far_start(up_block)
    first_m1, first_m2, *up_far = hold(first_m1, first_m2, *up_far)

    first_m3 = near_second(first_m1)
    first_c0, first_c1, first_c2 = [send_core(one) for one in (first_four, first_m1, first_m2)]
    first_m3, first_c0, first_c1, first_c2, down_block, *up_far = hold(
        first_m3, first_c0, first_c1, first_c2, down_block, *up_far
    )

    up_four = join(up_block, *up_far)
    first_c3, up_four, down_block = hold(send_core(first_m3), up_four, down_block)
    up_m1, up_m2 = near_first(up_four), near_second(up_four)
    down_far = far_start(down_block)
    first_parts = [first_four, first_m1, first_m2, first_m3], [first_c0, first_c1, first_c2, first_c3]
    qkv, out_proj, small_rows = [Rows(*first_parts, piece) for piece in first_pieces]
    first_in, packed, small_all, turned = first_kernel(table, normed_one, qkv, small_rows)
    mixed, attn = attention_forward(packed, segments)
    up_m1, up_m2, mixed, last_four, *down_far = hold(up_m1, up_m2, mixed, last_four, *down_far)

    up_m3 = near_second(up_m1)
    down_four = join(down_block, *down_far)
    down_m1 = near_first(down_four)
    up_c0 = send_core(up_four)
    last_early, last_late = [1, 2], list(far_masks())[2:]
    last_far = {mask: far_exchange(last_four, mask) for mask in last_early}
    middle, second_in = branch_kernel(table, mixed, inputs, turned, out_proj)
    small_all = small_all.reshape(devices, rows, 128)[:, :, 16 : 16 + lanes]
    small_all = small_all.reshape(devices, 2, comps, comp_cols).transpose(1, 2, 0, 3)
    means, spreads = small_all.reshape(2, comps, latent)
    choose = mixture_rows[:, None] == jnp.arange(comps, dtype=jnp.int32)[None, :]
    centre = matmul(choose.astype(LOW), means)
    spread = matmul(choose.astype(LOW), spreads)
    early = [last_far[mask] for mask in last_early]
    up_m3, down_m1, up_c0, second_in, centre, spread, up_m1, up_m2, last_four, *early = hold(
        up_m3, down_m1, up_c0, second_in, centre, spread, up_m1, up_m2, last_four, *early
    )
    last_far.update(zip(last_early, early))

    down_m2, down_m3 = near_second(down_four), near_second(down_m1)
    up_c1, up_c2, up_c3 = [send_core(one) for one in (up_m1, up_m2, up_m3)]
    up_c1, up_c2, up_c3, last_four, down_four, down_m1 = hold(
        up_c1, up_c2, up_c3, last_four, down_four, down_m1
    )
    last_far.update((mask, far_exchange(last_four, mask)) for mask in last_late)
    up = Rows([up_four, up_m1, up_m2, up_m3], [up_c0, up_c1, up_c2, up_c3], up_pieces[0])
    hidden, slope = up_kernel(table, second_in, up)
    down_c0, down_c1 = send_core(down_four), send_core(down_m1)
    late = [last_far[mask] for mask in last_late]
    down_m2, down_m3, down_c0, down_c1, hidden, *late = hold(
        down_m2, down_m3, down_c0, down_c1, hidden, *late
    )
    last_far.update(zip(last_late, late))

    last_all = join(last_four, *[last_far[mask] for mask in far_masks()])
    last_there = send_core(last_all)
    down_c2, down_c3 = send_core(down_m2), send_core(down_m3)
    last_there, down_c2, down_c3 = hold(last_there, down_c2, down_c3)
    to_latent, decode = [Rows([last_all], [last_there], piece, False) for piece in last_pieces]
    down = Rows(
        [down_four, down_m1, down_m2, down_m3], [down_c0, down_c1, down_c2, down_c3], down_pieces[0]
    )
    carried, moments, sample, kl_part = latent_kernel(
        table, hidden, middle, noise_rows, centre, spread, down, to_latent
    )
    kl_sum = kl_part + send_core(kl_part)
    kl_sum, sample = hold(kl_sum, sample)
    decoded, grad_decode, grad_sample, grad_bias = decode_kernel(
        table, sample, cotangent, turned, decode
    )
    kl_near = [send(kl_sum, bit, bit) for bit in (2, 4, 6)]
    kl_sum = sum(kl_near, kl_sum)
    kl_sum, grad_sample, decoded = hold(kl_sum, grad_sample, decoded)
    kl_far = [far_exchange(kl_sum, mask) for mask in far_masks()]
    plain, factor, comp = factors_kernel(
        grad_sample, moments, noise_rows, centre, spread, choose.astype(LOW)
    )
    kl_sum = sum(kl_far, kl_sum)
    kl_sum, grad_decode, plain, factor, grad_bias, decoded = hold(
        kl_sum, grad_decode, plain, factor, grad_bias, decoded
    )
    decoded_there = send_core(decoded)

    far = lax.axis_size("dp") // 4
    kl_weight = jnp.minimum(1.0, (plan_step + 1).astype(FULL) / WARM)
    grad_carried, comp, last_own, last_other = moments_kernel(
        table,
        kl_weight,
        total_cells,
        kl_sum,
        plain,
        factor,
        carried,
        comp,
        grad_decode,
        to_latent,
        Slots(rows + decode_rows, width),
    )
    last_own, last_other, grad_carried, hidden = hold(last_own, last_other, grad_carried, hidden)
    last_got = send_core(last_other)
    down_own, down_other = weight_grad(
        table, hidden, [grad_carried], Slots(down_rows, width), down_rows, "grad_down"
    )
    last_got, down_own, down_other, grad_carried = hold(
        last_got, down_own, down_other, grad_carried
    )

    down_got = send_core(down_other)
    turns = [slice(turn * far, (turn + 1) * far) for turn in range(4)]
    last_m3, last_m2 = [near_second(add_low(last_own[t], last_got[t])) for t in (turns[3], turns[2])]
    grad_up_proj = up_back_kernel(table, grad_carried, slope, down)
    down_got, grad_up_proj, last_m3, last_m2 = hold(down_got, grad_up_proj, last_m3, last_m2)

    down_m3, down_m2 = [near_second(add_low(down_own[t], down_got[t])) for t in (turns[3], turns[2])]
    last_m1 = near_first(add_all(last_own[turns[1]], [last_got[turns[1]], last_m3]).astype(LOW))
    grad_middle, grad_branch, grad_mixed, grad_gain_two = middle_back_kernel(
        table, grad_up_proj, grad_carried, middle, turned, up, out_proj
    )
    up_own, up_other = weight_grad(
        table, second_in, [grad_up_proj], Slots(rows, up_cols), rows, "grad_up"
    )
    down_m3, down_m2, last_m1, up_own, up_other, grad_mixed = hold(
        down_m3, down_m2, last_m1, up_own, up_other, grad_mixed
    )

    up_got = send_core(up_other)
    down_m1 = near_first(add_all(down_own[turns[1]], [down_got[turns[1]], down_m3]).astype(LOW))
    last_low = add_all(last_own[turns[0]], [last_got[turns[0]], last_m2, last_m1]).astype(LOW)
    last_far = far_slots(last_low, 1)
    grad_out = left_product(mixed, grad_branch).astype(LOW)
    grad_packed = attention_backward(packed, attn, grad_mixed)
    up_got, down_m1, grad_out, *grad_packed = hold(
        up_got, down_m1, grad_out, *grad_packed, *last_far
    )
    grad_packed, last_far = grad_packed[:3], grad_packed[3:]

    up_m3, up_m2 = [near_second(add_low(up_own[t], up_got[t])) for t in (turns[3], turns[2])]
    down_low = add_all(down_own[turns[0]], [down_got[turns[0]], down_m2, down_m1]).astype(LOW)
    down_far = far_slots(down_low, 1)
    grad_inputs, grad_gain_one = input_back_kernel(
        table, grad_packed, grad_middle, inputs, turned, qkv
    )
    up_m3, up_m2, grad_inputs, grad_gain_one, grad_packed_q, *down_far = hold(
        up_m3, up_m2, grad_inputs, grad_gain_one, grad_packed[0], *down_far
    )
    grad_packed = [grad_packed_q, *grad_packed[1:]]

    up_m1 = near_first(add_all(up_own[turns[1]], [up_got[turns[1]], up_m3]).astype(LOW))
    tables_grad = comp.reshape(2, comps, devices, comp_cols)
    tables_grad = tables_grad.transpose(2, 0, 1, 3).reshape(devices * rows, lanes)
    columns = [one.reshape(width, 1) for one in (grad_gain_one, grad_gain_two, grad_bias)]
    small_grads = small_block(columns, tables_grad).astype(LOW)
    first_own, first_other = weight_grad(
        table,
        first_in,
        grad_packed,
        Slots(rows, qkv_cols + out_cols + 128),
        rows,
        "grad_qkv",
        [(grad_out, rows, 0, qkv_cols), (small_grads, rows, 0, qkv_cols + out_cols)],
    )
    up_m1, first_own, first_other = hold(up_m1, first_own, first_other)

    first_got = send_core(first_other)
    up_low = add_all(up_own[turns[0]], [up_got[turns[0]], up_m2, up_m1]).astype(LOW)
    first_got, up_low, grad_inputs = hold(first_got, up_low, grad_inputs)

    first_m3, first_m2 = [
        near_second(add_low(first_own[t], first_got[t])) for t in (turns[3], turns[2])
    ]
    up_far = far_slots(up_low, 1)
    down_sum = add_all(down_low[0], [one[0] for one in down_far])
    last_sum = add_all(last_low[0], [one[0] for one in last_far])
    first_m3, first_m2, down_sum, last_sum, *up_far = hold(
        first_m3, first_m2, down_sum, last_sum, *up_far
    )

    first_m1 = near_first(add_all(first_own[turns[1]], [first_got[turns[1]], first_m3]).astype(LOW))
    inputs_there = send_core(grad_inputs)
    result = jnp.where(
        core == 0,
        jnp.concatenate([grad_inputs, inputs_there], axis=0),
        jnp.concatenate([decoded_there, decoded], axis=0).astype(FULL),
    )[None]
    up_sum = add_all(up_low[0], [one[0] for one in up_far])
    first_m1, result, up_sum = hold(first_m1, result, up_sum)

    first_low = add_all(first_own[turns[0]], [first_got[turns[0]], first_m2, first_m1]).astype(LOW)
    first_far = far_slots(first_low, 1)
    first_sum = add_all(first_low[0], [one[0] for one in first_far])
    small_sum = first_sum[:, qkv_cols + out_cols :]
    comp_mean_sum, comp_logvar_sum = small_sum[:, 16 : 16 + lanes].reshape(2, comps, comp_cols)
    return (
        result,
        small_sum[:, 0],
        first_sum[:, :qkv_cols],
        first_sum[:, qkv_cols : qkv_cols + out_cols],
        small_sum[:, 1],
        up_sum,
        down_sum,
        last_sum[:rows],
        last_sum[rows:],
        small_sum[:, 2],
        comp_mean_sum,
        comp_logvar_sum,
    )


def solution(mesh):
    split = P(EVERY)
    wide = P(EVERY, None)
    tall = P(None, EVERY)
    ends = P("pipe", "dp", None)
    return jax.shard_map(
        local,
        mesh=mesh,
        in_specs=(
            ends,
            P("dp", None),
            P("dp"),
            P("dp", None),
            P(),
            split,
            wide,
            wide,
            split,
            wide,
            wide,
            wide,
            wide,
            split,
            tall,
            tall,
        ),
        out_specs=(ends, split, wide, wide, split, wide, wide, wide, wide, split, tall, tall),
        check_vma=False,
    )
```

```python
import functools

import jax
import jax.numpy as jnp
from jax import lax
from jax.experimental import pallas as pl
from jax.experimental.pallas import tpu as pltpu
from jax.sharding import PartitionSpec as P

HEADS = 16
WARM = 1000
FREE_BITS = 0.8
SOFTNESS = 0.2
NEGATIVE = -1e30
EVERY = ("dp", "pipe")
LOW = jnp.bfloat16
FULL = jnp.float32


def hold(*values):
    return lax.optimization_barrier(values)


def swap_bits(mask):
    return (mask & 1) * 2 + (mask >> 1)


def send(value, even, odd):
    count = lax.axis_size("dp") * lax.axis_size("pipe")
    pairs = [(i, i ^ (odd if i & 1 else even)) for i in range(count)]
    return lax.ppermute(value, EVERY, pairs)


def send_core(value):
    return send(value, 1, 1)


def far_masks():
    return range(1, lax.axis_size("dp") // 4)


def far_exchange(value, mask):
    return send(value, mask * 8, mask * 8)


def near_first(value):
    return send(value, 2, 4)


def near_second(value):
    return send(value, 4, 2)


def place():
    return jnp.stack([lax.axis_index("dp"), lax.axis_index("pipe")]).astype(jnp.int32)


def slot_owner(where, slot, far, other_core, far_first):
    turn, step = (slot // far, slot % far) if far_first else (slot % 4, slot // 4)
    core = where[1]
    if other_core:
        core = 1 - core
    near = jnp.where(core == 0, turn, swap_bits(turn))
    return (where[0] ^ (4 * step)) ^ near, core


def slot_of(where, dp_index, core, far, far_first):
    apart = dp_index ^ where[0]
    step, near = apart // 4, apart % 4
    turn = jnp.where(core == 0, near, swap_bits(near))
    slot = turn * far + step if far_first else step * 4 + turn
    return slot + jnp.where(core == where[1], 0, 4 * far)


def tables():
    far = lax.axis_size("dp") // 4
    slots = jnp.arange(4 * far)
    rows = []
    for far_first in (True, False):
        for other in (False, True):
            owner, core = slot_owner(place(), slots, far, other, far_first)
            rows.append(owner * 2 + core)
    blocks = jnp.arange(8 * far)
    back = slot_of(place(), blocks // 2, blocks % 2, far, True) % (4 * far)
    return jnp.concatenate(rows + [back]).astype(jnp.int32)


class Rows:
    def __init__(self, own, other, piece, far_first=True):
        self.piece = row, height, col, width = piece
        self.count = sum(part.shape[0] for part in own)
        self.base = 0 if far_first else 2 * self.count
        self.shape = (2 * self.count * height, width)
        self.slots = height % 16 == 0
        if self.slots:
            self.operands = list(own) + list(other)
        else:
            every = jnp.concatenate(list(own) + list(other), axis=0)
            index = jnp.arange(2 * self.count)
            picked = slot_of(place(), index // 2, index % 2, self.count // 4, far_first)
            picked = jnp.take(every, picked, axis=0)
            self.operands = [picked[:, row : row + height, col : col + width].reshape(self.shape)]

    def region(self, table, step):
        height = 8 * self.piece[1]
        start = ((table[0] // 8) ^ step) * height
        return pl.ds(pl.multiple_of(start, height), height)

    def start(self, table, refs, target, sems, by_step=False, columns=None):
        row, height, col, width = self.piece
        first, width = columns or (0, width)
        columns = pl.ds(first, width)
        far = self.count // 4
        if not self.slots:
            for step in range(far if by_step else 1):
                some = self.region(table, step) if by_step else pl.ds(0, self.shape[0])
                source = refs[0].at[some, columns]
                pltpu.make_async_copy(source, target.at[some, columns], sems.at[step]).start()
            return
        found = [ref.at[k] for ref in refs for k in range(ref.shape[0])]
        steps = [s % self.count % far if self.base == 0 else s % self.count // 4 for s in range(len(found))]
        for slot in sorted(range(len(found)), key=lambda s: steps[s]):
            block = pl.multiple_of(table[self.base + slot] * height, height)
            pltpu.make_async_copy(
                found[slot].at[pl.ds(row, height), pl.ds(col + first, width)],
                target.at[pl.ds(block, height), columns],
                sems.at[steps[slot] if by_step else 0],
            ).start()


def arrived(target, sem):
    pltpu.make_async_copy(target, target, sem).wait()


class Slots:
    def __init__(self, rows, cols, far_first=True):
        self.count = lax.axis_size("dp")
        self.base = 0 if far_first else 2 * self.count
        self.rows, self.cols = rows, cols

    def shapes(self):
        return [jax.ShapeDtypeStruct((self.count // 2, self.rows, self.cols), LOW)] * 4

    def start(self, table, sources, outs, sem):
        half = self.count // 2
        for slot in range(2 * self.count):
            out = outs[slot // half].at[slot % half]
            for source, height, row, col in sources:
                block = pl.multiple_of(table[self.base + slot] * height, height)
                pltpu.make_async_copy(
                    source.at[pl.ds(block, height)],
                    out.at[pl.ds(row, height), pl.ds(col, source.shape[1])],
                    sem,
                ).start()

    def send(self, table, source, first_block, outs, sem):
        half = self.count // 2
        own_core = table[0] % 2
        columns = pl.ds(0, source.shape[1])
        for i in range(source.shape[0] // self.rows):
            slot = table[4 * self.count + first_block + i]
            part = source.at[pl.ds(i * self.rows, self.rows)]
            which = 2 * jnp.where(own_core == i % 2, 0, 1) + slot // half
            for k, out in enumerate(outs):

                @pl.when(which == k)
                def _():
                    target = out.at[lax.rem(slot, half), :, columns]
                    pltpu.make_async_copy(part, target, sem).start()


ANYWHERE = pl.BlockSpec(memory_space=pl.ANY)
FAR_AWAY = pl.BlockSpec(memory_space=pltpu.HBM)
SCALARS = pl.BlockSpec(memory_space=pltpu.SMEM)
INSIDE = pl.BlockSpec(memory_space=pltpu.VMEM)


def whole(*shape):
    return pl.BlockSpec(shape, lambda *_: (0,) * len(shape))


def params(megabytes=60):
    return pltpu.CompilerParams(vmem_limit_bytes=megabytes << 20)


def cost(flops, bytes_accessed, transcendentals=0):
    return pl.CostEstimate(flops=1024, bytes_accessed=1024, transcendentals=0)


def region_columns(step, table):
    return (0, (table[0] // 8) ^ step)


def by_region(steps, in_specs, out_specs, scratch):
    return pltpu.PrefetchScalarGridSpec(
        num_scalar_prefetch=1,
        grid=(steps,),
        in_specs=in_specs,
        out_specs=out_specs,
        scratch_shapes=scratch,
    )


def first_kernel(table, normed, weight, small):
    cells, width = normed.shape
    cols, tile = weight.shape[1], 512
    parts = len(weight.operands)

    def kernel(table_ref, normed_ref, *rest):
        refs, rest = rest[:parts], rest[parts:]
        small_refs, rest = rest[: len(small.operands)], rest[len(small.operands) :]
        in_ref, packed_ref, small_ref, turned_ref, held, sems = rest
        step = pl.program_id(0)

        @pl.when(step == 0)
        def _():
            small.start(table_ref, small_refs, small_ref, sems.at[pl.ds(0, 1)])
            weight.start(table_ref, refs, held, sems.at[pl.ds(1, 1)], columns=(0, tile))
            weight.start(table_ref, refs, held, sems.at[pl.ds(2, 1)], columns=(tile, cols - tile))
            arrived(small_ref, sems.at[0])
            turned = jnp.transpose(small_ref[...].astype(FULL))
            turned_ref[...] = turned
            in_ref[...] = (normed_ref[...] * turned[0:1]).astype(LOW)
            arrived(held.at[:, pl.ds(0, tile)], sems.at[1])

        @pl.when(step == 1)
        def _():
            arrived(held.at[:, pl.ds(tile, cols - tile)], sems.at[2])

        columns = held[:, pl.ds(pl.multiple_of(step * tile, tile), tile)]
        packed_ref[...] = matmul(in_ref[...], columns).astype(LOW)

    return pl.pallas_call(
        kernel,
        grid=(cols // tile,),
        in_specs=[SCALARS, whole(cells, width)]
        + [ANYWHERE] * (parts + len(small.operands)),
        out_specs=[
            whole(cells, width),
            pl.BlockSpec((cells, tile), lambda i: (0, i)),
            whole(*small.shape),
            whole(128, small.shape[0]),
        ],
        out_shape=[
            jax.ShapeDtypeStruct((cells, width), LOW),
            jax.ShapeDtypeStruct((cells, cols), LOW),
            jax.ShapeDtypeStruct(small.shape, LOW),
            jax.ShapeDtypeStruct((128, small.shape[0]), FULL),
        ],
        scratch_shapes=[pltpu.VMEM(weight.shape, LOW), pltpu.SemaphoreType.DMA((3,))],
        compiler_params=params(),
        cost_estimate=cost(2 * cells * width * cols, 14 << 20),
        name="first",
    )(table, normed, *weight.operands, *small.operands)


def branch_kernel(table, mixed, inputs, turned, weight):
    cells, width = inputs.shape
    parts, tile = len(weight.operands), 256

    def kernel(table_ref, mixed_ref, in_ref, turned_ref, *rest):
        refs, (middle_ref, second_ref, held, sems) = rest[:parts], rest[parts:]

        @pl.when(pl.program_id(0) == 0)
        def _():
            weight.start(table_ref, refs, held, sems)
            arrived(held, sems.at[0])

        middle = in_ref[...] + matmul(mixed_ref[...], held[...])
        middle_ref[...] = middle
        second_ref[...] = (norm_parts(middle)[0] * turned_ref[1:2]).astype(LOW)

    cut = pl.BlockSpec((tile, width), lambda i: (i, 0))
    return pl.pallas_call(
        kernel,
        grid=(cells // tile,),
        in_specs=[SCALARS, cut, cut, pl.BlockSpec((8, width), lambda i: (0, 0))]
        + [ANYWHERE] * parts,
        out_specs=[cut, cut],
        out_shape=[
            jax.ShapeDtypeStruct((cells, width), FULL),
            jax.ShapeDtypeStruct((cells, width), LOW),
        ],
        scratch_shapes=[pltpu.VMEM(weight.shape, LOW), pltpu.SemaphoreType.DMA((1,))],
        compiler_params=params(),
        cost_estimate=cost(2 * cells * width * width, 9 << 20),
        name="branch",
    )(table, mixed, inputs, turned, *weight.operands)


def up_kernel(table, second_in, weight):
    cells, width = second_in.shape
    cols, tile = weight.shape[1], 512
    parts = len(weight.operands)

    def kernel(table_ref, in_ref, *rest):
        refs, (hidden_ref, slope_ref, held, sems) = rest[:parts], rest[parts:]
        step = pl.program_id(0)

        @pl.when(step == 0)
        def _():
            weight.start(table_ref, refs, held, sems.at[pl.ds(0, 1)], columns=(0, tile))
            weight.start(table_ref, refs, held, sems.at[pl.ds(1, 1)], columns=(tile, cols - tile))
            arrived(held.at[:, pl.ds(0, tile)], sems.at[0])

        @pl.when(step == 1)
        def _():
            arrived(held.at[:, pl.ds(tile, cols - tile)], sems.at[1])

        columns = held[:, pl.ds(pl.multiple_of(step * tile, tile), tile)]
        up_proj = matmul(in_ref[...], columns)
        gate = 0.5 + 0.5 * lax.erf(up_proj * (0.5**0.5))
        hidden_ref[...] = (up_proj * gate).astype(LOW)
        bell = jnp.exp(-0.5 * up_proj * up_proj) * (0.5 / jnp.pi) ** 0.5
        slope_ref[...] = (gate + up_proj * bell).astype(LOW)

    return pl.pallas_call(
        kernel,
        grid=(cols // tile,),
        in_specs=[SCALARS, whole(cells, width)] + [FAR_AWAY] * parts,
        out_specs=[pl.BlockSpec((cells, tile), lambda i: (0, i))] * 2,
        out_shape=[
            jax.ShapeDtypeStruct((cells, cols), LOW),
            jax.ShapeDtypeStruct((cells, cols), LOW),
        ],
        scratch_shapes=[pltpu.VMEM(weight.shape, LOW), pltpu.SemaphoreType.DMA((2,))],
        compiler_params=params(22),
        cost_estimate=cost(2 * cells * width * cols, 22 << 20, 2 * cells * cols),
        name="up",
    )(table, second_in, *weight.operands)


def latent_kernel(table, hidden, middle, noise, choose, comp_tables, down, to_latent):
    cells, width = middle.shape
    latent = noise.shape[1]
    parts, more = len(down.operands), len(to_latent.operands)
    steps = down.count // 4
    tile = hidden.shape[1] // steps

    def kernel(table_ref, hidden_ref, mid_ref, noise_ref, choose_ref, tables_ref, *rest):
        refs, rest = rest[:parts], rest[parts:]
        latent_refs, rest = rest[:more], rest[more:]
        carried_ref, moments_ref, sample_ref, kl_ref, total, held, latent_held, sems = rest
        step = pl.program_id(0)

        @pl.when(step == 0)
        def _():
            down.start(table_ref, refs, held, sems, True)
            to_latent.start(table_ref, latent_refs, latent_held, sems.at[pl.ds(steps, 1)])
            total[...] = mid_ref[...]

        some = held.at[down.region(table_ref, step)]
        arrived(some, sems.at[step])
        total[...] += matmul(hidden_ref[...], some[...])

        @pl.when(step == steps - 1)
        def _():
            carried_ref[...] = total[...].astype(LOW)
            arrived(latent_held, sems.at[steps])
            moments_ref[...] = matmul(carried_ref[...], latent_held[...])
            mean_part, logvar = moments_ref[:, :latent], moments_ref[:, latent:]
            sample_ref[...] = (mean_part + jnp.exp(0.5 * logvar) * noise_ref[...]).astype(LOW)
            gap = mean_part - matmul(choose_ref[...], tables_ref[0])
            far = matmul(choose_ref[...], tables_ref[1])
            diverge = 0.5 * (far - logvar + (jnp.exp(logvar) + gap * gap) * jnp.exp(-far) - 1.0)
            kl_ref[...] = jnp.sum(diverge, axis=0, keepdims=True)

    return pl.pallas_call(
        kernel,
        grid_spec=by_region(
            steps,
            [pl.BlockSpec((cells, tile), region_columns), whole(cells, width)]
            + [whole(cells, latent), whole(*choose.shape), whole(*comp_tables.shape)]
            + [FAR_AWAY] * (parts + more),
            [whole(cells, width), whole(cells, 2 * latent), whole(cells, latent), whole(1, latent)],
            [
                pltpu.VMEM((cells, width), FULL),
                pltpu.VMEM(down.shape, LOW),
                pltpu.VMEM(to_latent.shape, LOW),
                pltpu.SemaphoreType.DMA((steps + 1,)),
            ],
        ),
        out_shape=[
            jax.ShapeDtypeStruct((cells, width), LOW),
            jax.ShapeDtypeStruct((cells, 2 * latent), FULL),
            jax.ShapeDtypeStruct((cells, latent), LOW),
            jax.ShapeDtypeStruct((1, latent), FULL),
        ],
        compiler_params=params(30),
        cost_estimate=cost(2 * cells * width * (hidden.shape[1] + width), 20 << 20),
        name="latent",
    )(table, hidden, middle, noise, choose, comp_tables, *down.operands, *to_latent.operands)


def decode_kernel(table, sample, cotangent, turned, decode):
    cells, width = cotangent.shape
    latent = sample.shape[1]
    parts = len(decode.operands)

    def kernel(table_ref, sample_ref, dy_ref, turned_ref, *rest):
        refs, (out_ref, grad_ref, back_ref, bias_ref, held, sem) = rest[:parts], rest[parts:]
        decode.start(table_ref, refs, held, sem)
        grad_ref[...] = left_product(sample_ref[...], dy_ref[...]).astype(LOW)
        bias_ref[...] = jnp.sum(dy_ref[...].astype(FULL), axis=0, keepdims=True)
        arrived(held, sem.at[0])
        back_ref[...] = right_product(dy_ref[...], held[...])
        out_ref[...] = (matmul(sample_ref[...], held[...]) + turned_ref[2:3]).astype(LOW)

    return pl.pallas_call(
        kernel,
        in_specs=[SCALARS] + [INSIDE] * 3 + [FAR_AWAY] * parts,
        out_specs=[INSIDE] * 4,
        out_shape=[
            jax.ShapeDtypeStruct((cells, width), LOW),
            jax.ShapeDtypeStruct((latent, width), LOW),
            jax.ShapeDtypeStruct((cells, latent), FULL),
            jax.ShapeDtypeStruct((1, width), FULL),
        ],
        scratch_shapes=[pltpu.VMEM(decode.shape, LOW), pltpu.SemaphoreType.DMA((1,))],
        compiler_params=params(16),
        cost_estimate=cost(6 * cells * width * latent, 8 << 20),
        name="decode",
    )(table, sample, cotangent, turned, *decode.operands)


def factors_kernel(back, moments, noise, choose, comp_tables):
    cells, latent = noise.shape
    comps = choose.shape[1]

    def kernel(back_ref, mom_ref, noise_ref, choose_ref, tables_ref, plain_ref, factor_ref, comp_ref):
        mean_part, logvar = mom_ref[:, :latent], mom_ref[:, latent:]
        gap = mean_part - matmul(choose_ref[...], tables_ref[0])
        shrink = jnp.exp(-matmul(choose_ref[...], tables_ref[1]))
        ratio = jnp.exp(logvar) * shrink
        moved = gap * shrink
        factor_ref[:, :latent] = moved
        factor_ref[:, latent:] = (ratio - 1.0) * 0.5
        for i, value in enumerate((-moved, (1.0 - (ratio + gap * moved)) * 0.5)):
            high = value.astype(LOW)
            rest = (value - high.astype(FULL)).astype(LOW)
            chosen = choose_ref[...]
            comp_ref[i] = left_product(chosen, high) + left_product(chosen, rest)
        back = back_ref[...]
        plain_ref[:, :latent] = back
        plain_ref[:, latent:] = back * noise_ref[...] * jnp.exp(0.5 * logvar) * 0.5

    return pl.pallas_call(
        kernel,
        in_specs=[INSIDE] * 5,
        out_specs=[INSIDE] * 3,
        out_shape=[
            jax.ShapeDtypeStruct((cells, 2 * latent), FULL),
            jax.ShapeDtypeStruct((cells, 2 * latent), FULL),
            jax.ShapeDtypeStruct((2, comps, latent), FULL),
        ],
        compiler_params=params(16),
        cost_estimate=cost(200 * cells * latent, 10 << 20),
        name="factors",
    )(back, moments, noise, choose, comp_tables)


def plain_slots(slots, grads):
    far = slots.count // 4
    results = []
    for other in (False, True):
        owner, core = slot_owner(place(), jnp.arange(slots.count), far, other, slots.base == 0)
        result = jnp.zeros((slots.count, slots.rows, slots.cols), LOW)
        for grad, height, row, col in grads:
            blocks = grad.reshape(slots.count, 2, height, grad.shape[1])
            blocks = jnp.take(blocks[:, core], owner, axis=0)
            result = result.at[:, row : row + height, col : col + grad.shape[1]].set(blocks)
        results += [result[: slots.count // 2], result[slots.count // 2 :]]
    return results


def moments_kernel(table, kl_weight, total, kl_sum, plain, factor, carried, comp, grad_decode, to_latent, slots):
    cells, width = carried.shape
    latent = kl_sum.shape[1]
    parts = len(to_latent.operands)
    height = to_latent.piece[1]
    decode_height = grad_decode.shape[0] // (2 * slots.count)
    direct = height % 16 == 0 and decode_height % 16 == 0

    def kernel(table_ref, weight_ref, kl_ref, plain_ref, factor_ref, carried_ref, comp_ref, gd_ref, *rest):
        refs, rest = rest[:parts], rest[parts:]
        gc_ref, comp_out, *rest = rest
        outs, rest = rest[: 4 if direct else 1], rest[4 if direct else 1 :]
        held, grads, sums, sems = rest
        to_latent.start(table_ref, refs, held, sems.at[pl.ds(0, 1)])
        mean = kl_ref[...] * (1.0 / total)
        coef = weight_ref[0] * jax.nn.sigmoid((mean - FREE_BITS) * (1.0 / SOFTNESS))
        for i in range(2):
            some = pl.ds(i * latent, latent)
            comp_out[i] = comp_ref[i] * coef
            grads[:, some] = (plain_ref[:, some] + factor_ref[:, some] * coef).astype(LOW)
        sums[...] = left_product(carried_ref[...], grads[...]).astype(LOW)
        if direct:
            slots.start(
                table_ref, [(sums, height, 0, 0), (gd_ref, decode_height, height, 0)], outs, sems.at[1]
            )
        else:
            outs[0][...] = sums[...]
        arrived(held, sems.at[0])
        gc_ref[...] = right_product(grads[...], held[...]).astype(LOW)
        if direct:
            for out in outs:
                arrived(out, sems.at[1])

    results = pl.pallas_call(
        kernel,
        in_specs=[SCALARS, SCALARS] + [INSIDE] * 6 + [FAR_AWAY] * parts,
        out_specs=[INSIDE] * 2 + ([FAR_AWAY] * 4 if direct else [INSIDE]),
        out_shape=[
            jax.ShapeDtypeStruct((cells, width), LOW),
            jax.ShapeDtypeStruct(comp.shape, FULL),
        ]
        + (slots.shapes() if direct else [jax.ShapeDtypeStruct((width, 2 * latent), LOW)]),
        scratch_shapes=[
            pltpu.VMEM(to_latent.shape, LOW),
            pltpu.VMEM((cells, 2 * latent), LOW),
            pltpu.VMEM((width, 2 * latent), LOW),
            pltpu.SemaphoreType.DMA((2,)),
        ],
        compiler_params=params(24),
        cost_estimate=cost(8 * cells * width * latent, 16 << 20),
        name="moments",
    )(table, kl_weight, kl_sum, plain, factor, carried, comp, grad_decode, *to_latent.operands)
    if direct:
        return results
    grads = [(results[2], height, 0, 0), (grad_decode, decode_height, height, 0)]
    return list(results[:2]) + plain_slots(slots, grads)


def weight_grad(table, left, rights, slots, height, name, extra=()):
    cells, rows = left.shape
    each = rights[0].shape[1]
    cols = each * len(rights)
    direct = height % 16 == 0
    tile = 512 if cols <= 1024 else 256
    steps = rows // tile
    extra = list(extra)

    def product(left_ref, right_refs, target):
        for i, right_ref in enumerate(right_refs):
            block = left_product(left_ref[...], right_ref[...])
            target[:, pl.ds(i * each, each)] = block.astype(LOW)

    def kernel(table_ref, left_ref, *rest):
        right_refs, rest = rest[: len(rights)], rest[len(rights) :]
        if not direct:
            product(left_ref, right_refs, rest[0])
            return
        more, rest = rest[: len(extra)], rest[len(extra) :]
        outs, (sums, sems) = rest[:4], rest[4:]
        step = pl.program_id(0)

        @pl.when(step == 0)
        def _():
            for ref, one in zip(more, extra):
                slots.start(table_ref, [(ref, one[1], one[2], one[3])], outs, sems.at[2])

        current = lax.rem(step, 2)

        @pl.when(step >= 2)
        def _():
            arrived(sums.at[current], sems.at[current])

        product(left_ref, right_refs, sums.at[current])
        slots.send(table_ref, sums.at[current], step * (tile // height), outs, sems.at[current])

        @pl.when(step == steps - 1)
        def _():
            arrived(sums.at[0], sems.at[0])
            arrived(sums.at[1], sems.at[1])
            for ref in more:
                arrived(ref, sems.at[2])

    results = pl.pallas_call(
        kernel,
        grid=(steps,),
        in_specs=[SCALARS, pl.BlockSpec((cells, tile), lambda i: (0, i))]
        + [whole(cells, each)] * len(rights)
        + [whole(*one[0].shape) for one in (extra if direct else [])],
        out_specs=[ANYWHERE] * 4 if direct else [pl.BlockSpec((tile, cols), lambda i: (i, 0))],
        out_shape=slots.shapes() if direct else [jax.ShapeDtypeStruct((rows, cols), LOW)],
        scratch_shapes=[pltpu.VMEM((2, tile, cols), LOW), pltpu.SemaphoreType.DMA((3,))]
        if direct
        else [],
        compiler_params=params(28),
        cost_estimate=cost(2 * cells * rows * cols, 2 * rows * cols),
        name=name,
    )(table, left, *rights, *[one[0] for one in (extra if direct else [])])
    if direct:
        return results
    return plain_slots(slots, [(results[0], height, 0, 0)] + extra)


def up_back_kernel(table, grad_carried, slope, down):
    cells, width = grad_carried.shape
    cols = slope.shape[1]
    parts = len(down.operands)
    steps = down.count // 4
    tile = cols // steps

    def kernel(table_ref, grad_ref, slope_ref, *rest):
        refs, (out_ref, held, sems) = rest[:parts], rest[parts:]
        step = pl.program_id(0)

        @pl.when(step == 0)
        def _():
            down.start(table_ref, refs, held, sems, True)

        some = held.at[down.region(table_ref, step)]
        arrived(some, sems.at[step])
        out_ref[...] = (right_product(grad_ref[...], some[...]) * slope_ref[...]).astype(LOW)

    return pl.pallas_call(
        kernel,
        grid_spec=by_region(
            steps,
            [whole(cells, width), pl.BlockSpec((cells, tile), region_columns)]
            + [FAR_AWAY] * parts,
            pl.BlockSpec((cells, tile), region_columns),
            [pltpu.VMEM(down.shape, LOW), pltpu.SemaphoreType.DMA((steps,))],
        ),
        out_shape=jax.ShapeDtypeStruct((cells, cols), LOW),
        compiler_params=params(24),
        cost_estimate=cost(2 * cells * width * cols, 22 << 20),
        name="up_back",
    )(table, grad_carried, slope, *down.operands)


def middle_back_kernel(table, grad_up_proj, grad_carried, middle, mixed, turned, up, out_proj):
    cells, width = grad_carried.shape
    cols = grad_up_proj.shape[1]
    parts, more = len(up.operands), len(out_proj.operands)

    def kernel(table_ref, gu_ref, gc_ref, mid_ref, mixed_ref, turned_ref, *rest):
        refs, rest = rest[:parts], rest[parts:]
        out_refs, rest = rest[:more], rest[more:]
        gm_ref, go_ref, gx_ref, gain_ref, gu_held, second, held, out_held, sems = rest
        loading = pltpu.make_async_copy(gu_ref, gu_held, sems.at[2])
        loading.start()
        up.start(table_ref, refs, held, sems)
        out_proj.start(table_ref, out_refs, out_held, sems.at[pl.ds(1, 1)])
        loading.wait()
        arrived(held, sems.at[0])
        for column in range(0, width, 512):
            some = pl.ds(column, 512)
            second[:, some] = right_product(gu_held[...], held[some])
        normed, scale = norm_parts(mid_ref[...])
        grad_second = second[...]
        gain_ref[...] = jnp.sum(normed * grad_second, axis=0, keepdims=True)
        back = norm_back(normed, scale, grad_second, turned_ref[1:2])
        grad_middle = gc_ref[...].astype(FULL) + back
        gm_ref[...] = grad_middle
        branch = grad_middle.astype(LOW)
        go_ref[...] = left_product(mixed_ref[...], branch).astype(LOW)
        arrived(out_held, sems.at[1])
        gx_ref[...] = right_product(branch, out_held[...]).astype(LOW)

    return pl.pallas_call(
        kernel,
        in_specs=[SCALARS, ANYWHERE] + [INSIDE] * 4 + [ANYWHERE] * (parts + more),
        out_specs=[INSIDE] * 4,
        out_shape=[
            jax.ShapeDtypeStruct((cells, width), FULL),
            jax.ShapeDtypeStruct((width, width), LOW),
            jax.ShapeDtypeStruct((cells, width), LOW),
            jax.ShapeDtypeStruct((1, width), FULL),
        ],
        scratch_shapes=[
            pltpu.VMEM((cells, cols), LOW),
            pltpu.VMEM((cells, width), FULL),
            pltpu.VMEM(up.shape, LOW),
            pltpu.VMEM(out_proj.shape, LOW),
            pltpu.SemaphoreType.DMA((3,)),
        ],
        compiler_params=params(),
        cost_estimate=cost(2 * cells * width * (cols + width), 22 << 20),
        name="middle_back",
    )(table, grad_up_proj, grad_carried, middle, mixed, turned, *up.operands, *out_proj.operands)


def input_back_kernel(table, grad_packed, grad_middle, inputs, turned, small, columns, weight):
    cells, width = inputs.shape
    parts = len(weight.operands)

    def kernel(table_ref, gq_ref, gk_ref, gv_ref, gm_ref, in_ref, turned_ref, small_ref, *rest):
        column_refs, rest = rest[: len(columns)], rest[len(columns) :]
        refs, (gx_ref, small_out, first, held, sems) = rest[:parts], rest[parts:]
        weight.start(table_ref, refs, held, sems)
        normed, scale = norm_parts(in_ref[...].astype(FULL))
        arrived(held, sems.at[0])
        for column in range(0, width, 512):
            some = pl.ds(column, 512)
            first[:, some] = sum(
                right_product(ref[...], held[some, i * width : (i + 1) * width])
                for i, ref in enumerate((gq_ref, gk_ref, gv_ref))
            )
        grad_first = first[...]
        gain = jnp.sum(normed * grad_first, axis=0, keepdims=True)
        lane = lax.broadcasted_iota(jnp.int32, (width, 128), 1)
        block = small_ref[...]
        for k, one in enumerate((gain, *[ref[...] for ref in column_refs])):
            one = jnp.transpose(jnp.broadcast_to(one, (128, width)))
            block = jnp.where(lane == k, one, block)
        small_out[...] = block.astype(LOW)
        gx_ref[...] = gm_ref[...] + norm_back(normed, scale, grad_first, turned_ref[0:1])

    return pl.pallas_call(
        kernel,
        in_specs=[SCALARS] + [INSIDE] * (7 + len(columns)) + [FAR_AWAY] * parts,
        out_specs=[INSIDE] * 2,
        out_shape=[
            jax.ShapeDtypeStruct((cells, width), FULL),
            jax.ShapeDtypeStruct((width, 128), LOW),
        ],
        scratch_shapes=[
            pltpu.VMEM((cells, width), FULL),
            pltpu.VMEM(weight.shape, LOW),
            pltpu.SemaphoreType.DMA((1,)),
        ],
        compiler_params=params(26),
        cost_estimate=cost(6 * cells * width * width, 18 << 20),
        name="input_back",
    )(table, *grad_packed, grad_middle, inputs, turned, small, *columns, *weight.operands)


def small_block(columns, rest):
    rows = rest.shape[0]
    gap = jnp.zeros((rows, 16 - len(columns)), rest.dtype)
    end = jnp.zeros((rows, 112 - rest.shape[1]), rest.dtype)
    return jnp.concatenate([*columns, gap, rest, end], axis=1)


def join(*parts):
    return jnp.concatenate(parts, axis=0)


def far_start(block):
    return [far_exchange(block, mask) for mask in far_masks()]


def add_low(one, two):
    return (one.astype(FULL) + two.astype(FULL)).astype(LOW)


def add_slots(size, *terms):
    parts = [array[first : first + size] for array, first in terms]
    return add_all(parts[0], parts[1:]).astype(LOW)


def both_cores(slots, got, turn, far):
    return add_slots(far, *[(pair[turn // 2], turn % 2 * far) for pair in (slots, got)])


def add_all(first, others):
    total = first.astype(FULL)
    for one in others:
        total = total + one.astype(FULL)
    return total


def far_slots(value, size):
    return [far_exchange(value[m * size : (m + 1) * size], m) for m in far_masks()]


def matmul(left_side, right_side):
    return jnp.dot(left_side, right_side, preferred_element_type=FULL)


def left_product(left_side, right_side):
    return lax.dot_general(
        left_side, right_side, (((0,), (0,)), ((), ())), preferred_element_type=FULL
    )


def right_product(left_side, right_side):
    return lax.dot_general(
        left_side, right_side, (((1,), (1,)), ((), ())), preferred_element_type=FULL
    )


def norm_parts(tensor):
    centred = tensor - jnp.mean(tensor, axis=-1, keepdims=True)
    scale = lax.rsqrt(jnp.mean(centred * centred, axis=-1, keepdims=True) + 1e-05)
    return centred * scale, scale


def norm_back(normed, scale, grad, gain):
    inner = grad * gain
    return scale * (
        inner
        - jnp.mean(inner, axis=-1, keepdims=True)
        - normed * jnp.mean(inner * normed, axis=-1, keepdims=True)
    )


def head_lanes(value, head, size):
    lane = lax.broadcasted_iota(jnp.int32, value.shape, 1)
    return jnp.where((lane // size) == head, value, jnp.zeros_like(value))


def attention_forward(packed, seg_col, seg_row, first, last, earlier=()):
    cells, three = packed.shape
    width = three // 3
    size = width // HEADS
    pair = 128 // size
    steps = HEADS // pair

    def kernel(seg_col, seg_row, q_ref, k_ref, v_ref, *rest):
        out_ref, attn_ref = rest[-2:]
        same = seg_col[...] == seg_row[...]
        queries, keys = q_ref[...], k_ref[...]
        values = jnp.transpose(v_ref[...])
        outs = []
        for head in range(pair):
            scores = right_product(head_lanes(keys, head, size), queries) * size ** (-0.5)
            scores = jnp.where(same, scores, NEGATIVE)
            powers = jnp.exp(scores - jnp.max(scores, axis=0, keepdims=True))
            attn = powers * (1.0 / jnp.sum(powers, axis=0, keepdims=True))
            attn_low = attn.astype(LOW)
            attn_ref[head] = attn_low
            outs.append(matmul(values[head * size : (head + 1) * size], attn_low))
        out_ref[...] = jnp.transpose(jnp.concatenate(outs, axis=0)).astype(LOW)

    return pl.pallas_call(
        kernel,
        grid=(last - first,),
        in_specs=[
            pl.BlockSpec((cells, 1), lambda i: (0, 0)),
            pl.BlockSpec((1, cells), lambda i: (0, 0)),
            pl.BlockSpec((cells, 128), lambda i: (0, i + first)),
            pl.BlockSpec((cells, 128), lambda i: (0, i + first + steps)),
            pl.BlockSpec((cells, 128), lambda i: (0, i + first + 2 * steps)),
        ]
        + [ANYWHERE] * len(earlier),
        out_specs=[
            pl.BlockSpec((cells, 128), lambda i: (0, i + first)),
            pl.BlockSpec((pair, cells, cells), lambda i: (i + first, 0, 0)),
        ],
        out_shape=[
            jax.ShapeDtypeStruct((cells, width), LOW),
            jax.ShapeDtypeStruct((HEADS, cells, cells), LOW),
        ],
        input_output_aliases={5 + i: i for i in range(len(earlier))},
        compiler_params=params(),
        cost_estimate=cost(4 * cells * cells * width, 24 << 20),
        name="attention_forward",
    )(seg_col, seg_row, packed, packed, packed, *earlier)


def attention_backward(packed, attn, mixed, grad_mixed):
    cells, three = packed.shape
    width = three // 3
    size = width // HEADS
    pair = 128 // size
    steps = HEADS // pair

    def kernel(q_ref, k_ref, v_ref, g_ref, mixed_ref, attn_ref, gq_ref, gk_ref, gv_ref):
        queries, keys, values, grad = q_ref[...], k_ref[...], v_ref[...], g_ref[...]
        keys_t = jnp.transpose(keys)
        inner = jnp.transpose(grad).astype(FULL) * jnp.transpose(mixed_ref[...]).astype(FULL)
        grad_q, grad_k, grad_v = [], 0.0, 0.0
        for head in range(pair):
            attn_low = attn_ref[head]
            attn = attn_low.astype(FULL)
            grad_attn = right_product(head_lanes(values, head, size), grad)
            some = slice(head * size, (head + 1) * size)
            grad_scores = attn * (grad_attn - jnp.sum(inner[some], axis=0, keepdims=True))
            grad_scores = grad_scores.astype(LOW)
            grad_q.append(matmul(keys_t[some], grad_scores))
            grad_k += head_lanes(matmul(grad_scores, queries), head, size)
            grad_v += head_lanes(matmul(attn_low, grad), head, size)
        scale = size ** (-0.5)
        gq_ref[...] = (jnp.transpose(jnp.concatenate(grad_q, axis=0)) * scale).astype(LOW)
        gk_ref[...] = (grad_k * scale).astype(LOW)
        gv_ref[...] = grad_v.astype(LOW)

    return pl.pallas_call(
        kernel,
        grid=(steps,),
        in_specs=[
            pl.BlockSpec((cells, 128), lambda i: (0, i)),
            pl.BlockSpec((cells, 128), lambda i: (0, i + steps)),
            pl.BlockSpec((cells, 128), lambda i: (0, i + 2 * steps)),
            pl.BlockSpec((cells, 128), lambda i: (0, i)),
            pl.BlockSpec((cells, 128), lambda i: (0, i)),
            pl.BlockSpec((pair, cells, cells), lambda i: (i, 0, 0)),
        ],
        out_specs=[pl.BlockSpec((cells, 128), lambda i: (0, i))] * 3,
        out_shape=[jax.ShapeDtypeStruct((cells, width), LOW)] * 3,
        compiler_params=params(),
        cost_estimate=cost(10 * cells * cells * width, 24 << 20),
        name="attention_backward",
    )(packed, packed, packed, grad_mixed, mixed, attn)


def local(
    layer_ends,
    segment_ids,
    mixture,
    noise,
    plan_step,
    ln1_gain,
    w_qkv,
    w_out,
    ln2_gain,
    w_up,
    w_down,
    w_latent,
    w_decode,
    decode_bias,
    comp_mean,
    comp_logvar,
):
    core = lax.axis_index("pipe")
    cells = segment_ids.shape[1]
    devices = lax.axis_size("dp") * 2
    width = layer_ends.shape[2]
    latent = noise.shape[1]
    comps = comp_mean.shape[0]
    total_cells = cells * devices

    rows = w_qkv.shape[0]
    comp_cols = latent // devices
    lanes = 2 * comps * comp_cols // rows
    small = jnp.concatenate([comp_mean.reshape(-1), comp_logvar.reshape(-1)]).reshape(rows, lanes)
    columns = [ln1_gain[:, None], ln2_gain[:, None], decode_bias[:, None]]
    small = small_block(columns, small)
    qkv_cols, out_cols, up_cols = w_qkv.shape[1], w_out.shape[1], w_up.shape[1]
    first_pieces = (
        (0, rows, 0, qkv_cols),
        (0, rows, qkv_cols, out_cols),
        (0, rows, qkv_cols + out_cols, 128),
    )
    up_pieces = ((0, rows, 0, up_cols),)
    down_rows, decode_rows = w_down.shape[0], w_decode.shape[0]
    down_pieces = ((0, down_rows, 0, width),)
    last_pieces = ((0, rows, 0, width), (rows, decode_rows, 0, width))
    first_block = jnp.concatenate([w_qkv, w_out, small], axis=1)[None]
    up_block, down_block = w_up[None], w_down[None]
    last_block = jnp.concatenate([w_latent, w_decode], axis=0)[None]

    def my_rows(tensor, which):
        return lax.dynamic_slice_in_dim(tensor, which * cells, cells, axis=0)

    kept = my_rows(layer_ends[0], core)
    going = my_rows(layer_ends[0], 1 - core)
    segments = lax.dynamic_index_in_dim(segment_ids, core, keepdims=False)
    mixture_rows = my_rows(mixture, core)
    noise_rows = my_rows(noise, core)

    table = tables()
    first_far = far_start(first_block)
    got = send_core(going)
    last_near = near_first(last_block)
    got, last_near, up_block, *first_far = hold(got, last_near, up_block, *first_far)
    inputs_low = jnp.where(core == 0, kept, got)
    inputs = inputs_low.astype(FULL)
    cotangent = jnp.where(core == 0, got, kept)
    normed_one, scale_one = norm_parts(inputs)
    last_two = join(last_block, last_near)

    first_four = join(first_block, *first_far)
    first_m1, first_m2 = near_first(first_four), near_second(first_four)
    up_far = far_start(up_block)
    seg_col, seg_row = segments[:, None], segments[None, :]
    choose = mixture_rows[:, None] == jnp.arange(comps, dtype=jnp.int32)[None, :]
    first_m1, first_m2, normed_one, last_two, table, seg_col, seg_row, *rest = hold(
        first_m1,
        first_m2,
        normed_one,
        last_two,
        table,
        seg_col,
        seg_row,
        choose.astype(LOW),
        noise_rows,
        down_block,
        *up_far,
    )
    choose, noise_rows, down_block, *up_far = rest

    first_m3 = near_second(first_m1)
    first_c0, first_c1, first_c2 = [send_core(one) for one in (first_four, first_m1, first_m2)]
    down_far = [far_exchange(down_block, 1)]
    first_m3, first_c0, first_c1, first_c2, down_block, *rest = hold(
        first_m3, first_c0, first_c1, first_c2, down_block, *down_far, *up_far
    )
    down_far, up_far = rest[:1], rest[1:]

    up_four = join(up_block, *up_far)
    first_c3, up_four, down_block = hold(send_core(first_m3), up_four, down_block)
    up_m1, up_m2 = near_first(up_four), near_second(up_four)
    last_more = near_second(last_two)
    down_far += [far_exchange(down_block, mask) for mask in far_masks() if mask > 1]
    first_parts = [first_four, first_m1, first_m2, first_m3], [first_c0, first_c1, first_c2, first_c3]
    qkv, out_proj, small_rows = [Rows(*first_parts, piece) for piece in first_pieces]
    first_in, packed, small_all, turned = first_kernel(table, normed_one, qkv, small_rows)
    pairs = HEADS * (width // HEADS) // 128
    some_heads = attention_forward(packed, seg_col, seg_row, 0, pairs // 2)
    up_m1, up_m2, last_more, packed, *rest = hold(
        up_m1, up_m2, last_more, packed, *some_heads, *down_far
    )
    some_heads, down_far = rest[:2], rest[2:]
    last_four = join(last_two, last_more)

    up_m3 = near_second(up_m1)
    down_four = join(down_block, *down_far)
    down_m1 = near_first(down_four)
    up_c0 = send_core(up_four)
    last_early, last_late = [1, 2], list(far_masks())[2:]
    last_far = {mask: far_exchange(last_four, mask) for mask in last_early}
    mixed, attn = attention_forward(packed, seg_col, seg_row, pairs // 2, pairs, some_heads)
    middle, second_in = branch_kernel(table, mixed, inputs, turned, out_proj)
    small_all = small_all.reshape(devices, rows, 128)[:, :, 16 : 16 + lanes]
    small_all = small_all.reshape(devices, 2, comps, comp_cols).transpose(1, 2, 0, 3)
    comp_tables = small_all.reshape(2, comps, latent)
    early = [last_far[mask] for mask in last_early]
    up_m3, down_m1, up_c0, second_in, comp_tables, up_m1, up_m2, last_four, *early = hold(
        up_m3, down_m1, up_c0, second_in, comp_tables, up_m1, up_m2, last_four, *early
    )
    last_far.update(zip(last_early, early))

    down_m2, down_m3 = near_second(down_four), near_second(down_m1)
    up_c1, up_c2, up_c3 = [send_core(one) for one in (up_m1, up_m2, up_m3)]
    up_c1, up_c2, up_c3, last_four, down_four, down_m1 = hold(
        up_c1, up_c2, up_c3, last_four, down_four, down_m1
    )
    last_far.update((mask, far_exchange(last_four, mask)) for mask in last_late)
    up = Rows([up_four, up_m1, up_m2, up_m3], [up_c0, up_c1, up_c2, up_c3], up_pieces[0])
    hidden, slope = up_kernel(table, second_in, up)
    down_c0, down_c1 = send_core(down_four), send_core(down_m1)
    late = [last_far[mask] for mask in last_late]
    down_m2, down_m3, down_c0, down_c1, hidden, *late = hold(
        down_m2, down_m3, down_c0, down_c1, hidden, *late
    )
    last_far.update(zip(last_late, late))

    last_all = join(last_four, *[last_far[mask] for mask in far_masks()])
    last_there = send_core(last_all)
    down_c2, down_c3 = send_core(down_m2), send_core(down_m3)
    last_there, down_c2, down_c3 = hold(last_there, down_c2, down_c3)
    to_latent, decode = [Rows([last_all], [last_there], piece, False) for piece in last_pieces]
    down = Rows(
        [down_four, down_m1, down_m2, down_m3], [down_c0, down_c1, down_c2, down_c3], down_pieces[0]
    )
    carried, moments, sample, kl_part = latent_kernel(
        table, hidden, middle, noise_rows, choose, comp_tables, down, to_latent
    )
    kl_sum = kl_part + send_core(kl_part)
    kl_sum, sample = hold(kl_sum, sample)
    decoded, grad_decode, grad_sample, grad_bias = decode_kernel(
        table, sample, cotangent, turned, decode
    )
    kl_near = [send(kl_sum, bit, bit) for bit in (2, 4, 6)]
    kl_sum = sum(kl_near, kl_sum)
    kl_sum, grad_sample, decoded = hold(kl_sum, grad_sample, decoded)
    kl_far = [far_exchange(kl_sum, mask) for mask in far_masks()]
    plain, factor, comp = factors_kernel(grad_sample, moments, noise_rows, choose, comp_tables)
    kl_sum = sum(kl_far, kl_sum)
    kl_sum, grad_decode, plain, factor, grad_bias, decoded = hold(
        kl_sum, grad_decode, plain, factor, grad_bias, decoded
    )

    far = lax.axis_size("dp") // 4
    kl_weight = jnp.minimum(1.0, (plan_step + 1).astype(FULL) / WARM)
    grad_carried, comp, *last_slots = moments_kernel(
        table,
        kl_weight,
        total_cells,
        kl_sum,
        plain,
        factor,
        carried,
        comp,
        grad_decode,
        to_latent,
        Slots(rows + decode_rows, width),
    )
    grad_carried, hidden, decoded, *last_slots = hold(grad_carried, hidden, decoded, *last_slots)
    decoded_there = send_core(decoded)
    last_got = [send_core(one) for one in last_slots[2:]]
    down_slots = weight_grad(
        table, hidden, [grad_carried], Slots(down_rows, width), down_rows, "grad_down"
    )
    grad_carried, decoded_there, *rest = hold(
        grad_carried, decoded_there, *last_got, *down_slots
    )
    last_got, down_slots = rest[:2], rest[2:]

    down_got = [send_core(one) for one in down_slots[2:]]
    last_3, last_2 = [both_cores(last_slots, last_got, turn, far) for turn in (3, 2)]
    last_m3, last_m2 = near_second(last_3), near_second(last_2)
    grad_up_proj = up_back_kernel(table, grad_carried, slope, down)
    grad_up_proj, last_m3, last_m2, *down_got = hold(grad_up_proj, last_m3, last_m2, *down_got)
    down_m3 = near_second(both_cores(down_slots, down_got, 3, far))
    up_slots = weight_grad(
        table, second_in, [grad_up_proj], Slots(rows, up_cols), rows, "grad_up"
    )
    down_0, down_1, down_2 = [both_cores(down_slots, down_got, turn, far) for turn in range(3)]
    down_m3, last_m3, down_0, down_1, down_2, *up_slots = hold(
        down_m3, last_m3, down_0, down_1, down_2, *up_slots
    )

    up_got = [send_core(one) for one in up_slots[2:]]
    down_m2 = near_second(down_2)
    last_m1 = near_first(add_slots(far, (last_slots[0], far), (last_got[0], far), (last_m3, 0)))
    grad_middle, grad_out, grad_mixed, grad_gain_two = middle_back_kernel(
        table, grad_up_proj, grad_carried, middle, mixed, turned, up, out_proj
    )
    tables_grad = comp.reshape(2, comps, devices, comp_cols)
    tables_grad = tables_grad.transpose(2, 0, 1, 3).reshape(devices * rows, lanes)
    small_grads = jnp.pad(tables_grad, ((0, 0), (16, 112 - lanes)))
    down_m2, last_m1, grad_mixed, grad_out, small_grads, *up_got = hold(
        down_m2, last_m1, grad_mixed, grad_out, small_grads, *up_got
    )

    up_m3 = near_second(both_cores(up_slots, up_got, 3, far))
    down_m1 = near_first(add_slots(far, (down_1, 0), (down_m3, 0)))
    grad_packed = attention_backward(packed, attn, mixed, grad_mixed)
    up_m3, down_m1, *grad_packed = hold(up_m3, down_m1, *grad_packed)

    up_m2 = near_second(both_cores(up_slots, up_got, 2, far))
    up_m1 = near_first(add_slots(far, (up_slots[0], far), (up_got[0], far), (up_m3, 0)))
    down_low = add_slots(far, (down_0, 0), (down_m2, 0), (down_m1, 0))
    down_far = far_slots(down_low, 1)
    grad_inputs, small_grads = input_back_kernel(
        table,
        grad_packed,
        grad_middle,
        inputs_low,
        turned,
        small_grads,
        [grad_gain_two, grad_bias],
        qkv,
    )
    first_slots = weight_grad(
        table,
        first_in,
        grad_packed,
        Slots(rows, qkv_cols + out_cols + 128),
        rows,
        "grad_qkv",
        [(grad_out, rows, 0, qkv_cols), (small_grads, rows, 0, qkv_cols + out_cols)],
    )
    up_m2, up_m1, grad_inputs, *rest = hold(up_m2, up_m1, grad_inputs, *first_slots, *down_far)
    first_slots, down_far = rest[:4], rest[4:]

    first_high = send_core(first_slots[3])
    up_low = add_slots(far, (up_slots[0], 0), (up_got[0], 0), (up_m2, 0), (up_m1, 0))
    first_high, up_low, *first_slots = hold(first_high, up_low, *first_slots)
    first_low = send_core(first_slots[2])
    first_got = [first_low, first_high]
    first_3, first_2 = [both_cores(first_slots, first_got, turn, far) for turn in (3, 2)]
    first_low, first_3, first_2, up_low = hold(first_low, first_3, first_2, up_low)

    first_m3, first_m2 = near_second(first_3), near_second(first_2)
    up_far = far_slots(up_low, 1)
    last_low = add_slots(far, (last_slots[0], 0), (last_got[0], 0), (last_m2, 0), (last_m1, 0))
    down_sum = add_all(down_low[0], [one[0] for one in down_far])
    first_m3, first_m2, down_sum, last_low, *up_far = hold(
        first_m3, first_m2, down_sum, last_low, *up_far
    )

    first_m1 = near_first(add_slots(far, (first_slots[0], far), (first_low, far), (first_m3, 0)))
    inputs_there = send_core(grad_inputs)
    up_sum = add_all(up_low[0], [one[0] for one in up_far])
    last_far = far_slots(last_low, 1)
    first_m1, inputs_there, up_sum, *last_far = hold(first_m1, inputs_there, up_sum, *last_far)
    last_sum = add_all(last_low[0], [one[0] for one in last_far])

    result = jnp.where(
        core == 0,
        jnp.concatenate([grad_inputs, inputs_there], axis=0),
        jnp.concatenate([decoded_there, decoded], axis=0).astype(FULL),
    )[None]
    first_all = add_slots(far, (first_slots[0], 0), (first_low, 0), (first_m2, 0), (first_m1, 0))
    first_far = far_slots(first_all, 1)
    first_sum = add_all(first_all[0], [one[0] for one in first_far])
    small_sum = first_sum[:, qkv_cols + out_cols :]
    comp_mean_sum, comp_logvar_sum = small_sum[:, 16 : 16 + lanes].reshape(2, comps, comp_cols)
    return (
        result,
        small_sum[:, 0],
        first_sum[:, :qkv_cols],
        first_sum[:, qkv_cols : qkv_cols + out_cols],
        small_sum[:, 1],
        up_sum,
        down_sum,
        last_sum[:rows],
        last_sum[rows:],
        small_sum[:, 2],
        comp_mean_sum,
        comp_logvar_sum,
    )


def solution(mesh):
    split = P(EVERY)
    wide = P(EVERY, None)
    tall = P(None, EVERY)
    ends = P("pipe", "dp", None)
    return jax.shard_map(
        local,
        mesh=mesh,
        in_specs=(
            ends,
            P("dp", None),
            P("dp"),
            P("dp", None),
            P(),
            split,
            wide,
            wide,
            split,
            wide,
            wide,
            wide,
            wide,
            split,
            tall,
            tall,
        ),
        out_specs=(ends, split, wide, wide, split, wide, wide, wide, wide, split, tall, tall),
        check_vma=False,
    )
```

```python
import functools

import jax
import jax.numpy as jnp
from jax import lax
from jax.experimental import pallas as pl
from jax.experimental.pallas import tpu as pltpu
from jax.sharding import PartitionSpec as P

HEADS = 16
WARM = 1000
FREE_BITS = 0.8
SOFTNESS = 0.2
NEGATIVE = -1e30
EVERY = ("dp", "pipe")
LOW = jnp.bfloat16
FULL = jnp.float32


def hold(*values):
    return lax.optimization_barrier(values)


def swap_bits(mask):
    return (mask & 1) * 2 + (mask >> 1)


def send(value, even, odd):
    count = lax.axis_size("dp") * lax.axis_size("pipe")
    pairs = [(i, i ^ (odd if i & 1 else even)) for i in range(count)]
    return lax.ppermute(value, EVERY, pairs)


def send_core(value):
    return send(value, 1, 1)


def far_masks():
    return range(1, lax.axis_size("dp") // 4)


def far_exchange(value, mask):
    return send(value, mask * 8, mask * 8)


def near_first(value):
    return send(value, 2, 4)


def near_second(value):
    return send(value, 4, 2)


def place():
    return jnp.stack([lax.axis_index("dp"), lax.axis_index("pipe")]).astype(jnp.int32)


def slot_owner(where, slot, far, other_core, far_first):
    turn, step = (slot // far, slot % far) if far_first else (slot % 4, slot // 4)
    core = where[1]
    if other_core:
        core = 1 - core
    near = jnp.where(core == 0, turn, swap_bits(turn))
    return (where[0] ^ (4 * step)) ^ near, core


def slot_of(where, dp_index, core, far, far_first):
    apart = dp_index ^ where[0]
    step, near = apart // 4, apart % 4
    turn = jnp.where(core == 0, near, swap_bits(near))
    slot = turn * far + step if far_first else step * 4 + turn
    return slot + jnp.where(core == where[1], 0, 4 * far)


def tables():
    far = lax.axis_size("dp") // 4
    slots = jnp.arange(4 * far)
    rows = []
    for far_first in (True, False):
        for other in (False, True):
            owner, core = slot_owner(place(), slots, far, other, far_first)
            rows.append(owner * 2 + core)
    blocks = jnp.arange(8 * far)
    back = slot_of(place(), blocks // 2, blocks % 2, far, True) % (4 * far)
    return jnp.concatenate(rows + [back]).astype(jnp.int32)


class Rows:
    def __init__(self, own, other, piece, far_first=True):
        self.piece = row, height, col, width = piece
        self.count = sum(part.shape[0] for part in own)
        self.base = 0 if far_first else 2 * self.count
        self.shape = (2 * self.count * height, width)
        self.slots = height % 16 == 0
        if self.slots:
            self.operands = list(own) + list(other)
        else:
            every = jnp.concatenate(list(own) + list(other), axis=0)
            index = jnp.arange(2 * self.count)
            picked = slot_of(place(), index // 2, index % 2, self.count // 4, far_first)
            picked = jnp.take(every, picked, axis=0)
            self.operands = [picked[:, row : row + height, col : col + width].reshape(self.shape)]

    def region(self, table, step, group=1):
        height = 8 * self.piece[1] * group
        start = ((table[0] // (8 * group)) ^ step) * height
        return pl.ds(pl.multiple_of(start, height), height)

    def start(self, table, refs, target, sems, group=0, columns=None):
        row, height, col, width = self.piece
        first, width = columns or (0, width)
        columns = pl.ds(first, width)
        far = self.count // 4
        if not self.slots:
            for step in range(far // group if group else 1):
                some = self.region(table, step, group) if group else pl.ds(0, self.shape[0])
                source = refs[0].at[some, columns]
                pltpu.make_async_copy(source, target.at[some, columns], sems.at[step]).start()
            return
        found = [ref.at[k] for ref in refs for k in range(ref.shape[0])]
        steps = [s % self.count % far if self.base == 0 else s % self.count // 4 for s in range(len(found))]
        for slot in sorted(range(len(found)), key=lambda s: steps[s]):
            block = pl.multiple_of(table[self.base + slot] * height, height)
            pltpu.make_async_copy(
                found[slot].at[pl.ds(row, height), pl.ds(col + first, width)],
                target.at[pl.ds(block, height), columns],
                sems.at[steps[slot] // group if group else 0],
            ).start()


def arrived(target, sem):
    pltpu.make_async_copy(target, target, sem).wait()


class Slots:
    def __init__(self, rows, cols, far_first=True):
        self.count = lax.axis_size("dp")
        self.base = 0 if far_first else 2 * self.count
        self.rows, self.cols = rows, cols

    def shapes(self):
        return [jax.ShapeDtypeStruct((self.count // 2, self.rows, self.cols), LOW)] * 4

    def start(self, table, sources, outs, sem):
        half = self.count // 2
        for slot in range(2 * self.count):
            out = outs[slot // half].at[slot % half]
            for source, height, row, col in sources:
                block = pl.multiple_of(table[self.base + slot] * height, height)
                pltpu.make_async_copy(
                    source.at[pl.ds(block, height)],
                    out.at[pl.ds(row, height), pl.ds(col, source.shape[1])],
                    sem,
                ).start()

    def send(self, table, source, first_block, outs, sem):
        half = self.count // 2
        own_core = table[0] % 2
        columns = pl.ds(0, source.shape[1])
        for i in range(source.shape[0] // self.rows):
            slot = table[4 * self.count + first_block + i]
            part = source.at[pl.ds(i * self.rows, self.rows)]
            which = 2 * jnp.where(own_core == i % 2, 0, 1) + slot // half
            for k, out in enumerate(outs):

                @pl.when(which == k)
                def _():
                    target = out.at[lax.rem(slot, half), :, columns]
                    pltpu.make_async_copy(part, target, sem).start()


ANYWHERE = pl.BlockSpec(memory_space=pl.ANY)
FAR_AWAY = pl.BlockSpec(memory_space=pltpu.HBM)
SCALARS = pl.BlockSpec(memory_space=pltpu.SMEM)
INSIDE = pl.BlockSpec(memory_space=pltpu.VMEM)


def whole(*shape):
    return pl.BlockSpec(shape, lambda *_: (0,) * len(shape))


def params(megabytes=60):
    return pltpu.CompilerParams(vmem_limit_bytes=megabytes << 20)


def cost(flops, bytes_accessed, transcendentals=0):
    return pl.CostEstimate(flops=1024, bytes_accessed=1024, transcendentals=0)


def region_columns(step, table):
    return (0, (table[0] // 8) ^ step)


def by_region(steps, in_specs, out_specs, scratch):
    return pltpu.PrefetchScalarGridSpec(
        num_scalar_prefetch=1,
        grid=(steps,),
        in_specs=in_specs,
        out_specs=out_specs,
        scratch_shapes=scratch,
    )


def first_kernel(table, normed, weight, small):
    cells, width = normed.shape
    cols, tile = weight.shape[1], 512
    parts = len(weight.operands)

    def kernel(table_ref, normed_ref, *rest):
        refs, rest = rest[:parts], rest[parts:]
        small_refs, rest = rest[: len(small.operands)], rest[len(small.operands) :]
        in_ref, packed_ref, small_ref, turned_ref, held, sems = rest
        step = pl.program_id(0)

        @pl.when(step == 0)
        def _():
            small.start(table_ref, small_refs, small_ref, sems.at[pl.ds(0, 1)])
            weight.start(table_ref, refs, held, sems.at[pl.ds(1, 1)], columns=(0, tile))
            weight.start(table_ref, refs, held, sems.at[pl.ds(2, 1)], columns=(tile, cols - tile))
            arrived(small_ref, sems.at[0])
            turned = jnp.transpose(small_ref[...].astype(FULL))
            turned_ref[...] = turned
            in_ref[...] = (normed_ref[...] * turned[0:1]).astype(LOW)
            arrived(held.at[:, pl.ds(0, tile)], sems.at[1])

        @pl.when(step == 1)
        def _():
            arrived(held.at[:, pl.ds(tile, cols - tile)], sems.at[2])

        columns = held[:, pl.ds(pl.multiple_of(step * tile, tile), tile)]
        packed_ref[...] = matmul(in_ref[...], columns).astype(LOW)

    return pl.pallas_call(
        kernel,
        grid=(cols // tile,),
        in_specs=[SCALARS, whole(cells, width)]
        + [ANYWHERE] * (parts + len(small.operands)),
        out_specs=[
            whole(cells, width),
            pl.BlockSpec((cells, tile), lambda i: (0, i)),
            whole(*small.shape),
            whole(128, small.shape[0]),
        ],
        out_shape=[
            jax.ShapeDtypeStruct((cells, width), LOW),
            jax.ShapeDtypeStruct((cells, cols), LOW),
            jax.ShapeDtypeStruct(small.shape, LOW),
            jax.ShapeDtypeStruct((128, small.shape[0]), FULL),
        ],
        scratch_shapes=[pltpu.VMEM(weight.shape, LOW), pltpu.SemaphoreType.DMA((3,))],
        compiler_params=params(),
        cost_estimate=cost(2 * cells * width * cols, 14 << 20),
        name="first",
    )(table, normed, *weight.operands, *small.operands)


def branch_kernel(table, mixed, inputs, turned, weight):
    cells, width = inputs.shape
    parts, tile = len(weight.operands), 256

    def kernel(table_ref, mixed_ref, in_ref, turned_ref, *rest):
        refs, (middle_ref, second_ref, held, sems) = rest[:parts], rest[parts:]

        @pl.when(pl.program_id(0) == 0)
        def _():
            weight.start(table_ref, refs, held, sems)
            arrived(held, sems.at[0])

        middle = in_ref[...] + matmul(mixed_ref[...], held[...])
        middle_ref[...] = middle
        second_ref[...] = (norm_parts(middle)[0] * turned_ref[1:2]).astype(LOW)

    cut = pl.BlockSpec((tile, width), lambda i: (i, 0))
    return pl.pallas_call(
        kernel,
        grid=(cells // tile,),
        in_specs=[SCALARS, cut, cut, pl.BlockSpec((8, width), lambda i: (0, 0))]
        + [ANYWHERE] * parts,
        out_specs=[cut, cut],
        out_shape=[
            jax.ShapeDtypeStruct((cells, width), FULL),
            jax.ShapeDtypeStruct((cells, width), LOW),
        ],
        scratch_shapes=[pltpu.VMEM(weight.shape, LOW), pltpu.SemaphoreType.DMA((1,))],
        compiler_params=params(),
        cost_estimate=cost(2 * cells * width * width, 9 << 20),
        name="branch",
    )(table, mixed, inputs, turned, *weight.operands)


def up_kernel(table, second_in, weight):
    cells, width = second_in.shape
    cols, tile = weight.shape[1], 512
    parts = len(weight.operands)

    def kernel(table_ref, in_ref, *rest):
        refs, (hidden_ref, slope_ref, held, sems) = rest[:parts], rest[parts:]
        step = pl.program_id(0)

        @pl.when(step == 0)
        def _():
            weight.start(table_ref, refs, held, sems.at[pl.ds(0, 1)], columns=(0, tile))
            weight.start(table_ref, refs, held, sems.at[pl.ds(1, 1)], columns=(tile, cols - tile))
            arrived(held.at[:, pl.ds(0, tile)], sems.at[0])

        @pl.when(step == 1)
        def _():
            arrived(held.at[:, pl.ds(tile, cols - tile)], sems.at[1])

        columns = held[:, pl.ds(pl.multiple_of(step * tile, tile), tile)]
        up_proj = matmul(in_ref[...], columns)
        gate = 0.5 + 0.5 * lax.erf(up_proj * (0.5**0.5))
        hidden_ref[...] = (up_proj * gate).astype(LOW)
        bell = jnp.exp(-0.5 * up_proj * up_proj) * (0.5 / jnp.pi) ** 0.5
        slope_ref[...] = (gate + up_proj * bell).astype(LOW)

    return pl.pallas_call(
        kernel,
        grid=(cols // tile,),
        in_specs=[SCALARS, whole(cells, width)] + [FAR_AWAY] * parts,
        out_specs=[pl.BlockSpec((cells, tile), lambda i: (0, i))] * 2,
        out_shape=[
            jax.ShapeDtypeStruct((cells, cols), LOW),
            jax.ShapeDtypeStruct((cells, cols), LOW),
        ],
        scratch_shapes=[pltpu.VMEM(weight.shape, LOW), pltpu.SemaphoreType.DMA((2,))],
        compiler_params=params(22),
        cost_estimate=cost(2 * cells * width * cols, 22 << 20, 2 * cells * cols),
        name="up",
    )(table, second_in, *weight.operands)


def half_specs(cells, height, cols, far, turns):
    slots = [turn * far + other * 4 * far for other in (0, 1) for turn in turns]

    def columns(slot):
        return pl.BlockSpec((cells, height), lambda step, table: (0, table[slot + step]))

    rows = pl.BlockSpec((1, height, cols), lambda step, table: (step, 0, 0))
    return [columns(slot) for slot in slots] + [rows] * len(slots)


def half_product(refs):
    half = len(refs) // 2
    left = jnp.concatenate([ref[...] for ref in refs[:half]], axis=1)
    return matmul(left, jnp.concatenate([ref[0] for ref in refs[half:]], axis=0))


def down_half(table, hidden, middle, parts, turns):
    cells, width = middle.shape
    far, height = parts[0].shape[:2]

    def kernel(table_ref, mid_ref, *rest):
        refs, total_ref = rest[:-1], rest[-1]

        @pl.when(pl.program_id(0) == 0)
        def _():
            total_ref[...] = mid_ref[...]

        total_ref[...] += half_product(refs)

    return pl.pallas_call(
        kernel,
        grid_spec=by_region(
            far,
            [whole(cells, width)] + half_specs(cells, height, width, far, turns),
            whole(cells, width),
            [],
        ),
        out_shape=jax.ShapeDtypeStruct((cells, width), FULL),
        compiler_params=params(24),
        cost_estimate=cost(0, 0),
        name="down_half",
    )(table, middle, *[hidden] * 4, *parts)


def latent_kernel(table, hidden, middle, noise, choose, comp_tables, down, to_latent, parts=None, turns=()):
    cells, width = middle.shape
    latent = noise.shape[1]
    mine, more = (8 if parts else 1 + len(down.operands)), len(to_latent.operands)
    steps = down.count // 4
    tile = hidden.shape[1] // steps

    def kernel(table_ref, mid_ref, noise_ref, choose_ref, tables_ref, *rest):
        refs, rest = rest[:mine], rest[mine:]
        latent_refs, rest = rest[:more], rest[more:]
        carried_ref, moments_ref, sample_ref, kl_ref, total, *held, latent_held, sems = rest
        step = pl.program_id(0)

        @pl.when(step == 0)
        def _():
            if not parts:
                down.start(table_ref, refs[1:], held[0], sems, 1)
            to_latent.start(table_ref, latent_refs, latent_held, sems.at[pl.ds(steps, 1)])
            total[...] = mid_ref[...]

        if parts:
            total[...] += half_product(refs)
        else:
            some = held[0].at[down.region(table_ref, step)]
            arrived(some, sems.at[step])
            total[...] += matmul(refs[0][...], some[...])

        @pl.when(step == steps - 1)
        def _():
            carried_ref[...] = total[...].astype(LOW)
            arrived(latent_held, sems.at[steps])
            moments_ref[...] = matmul(carried_ref[...], latent_held[...])
            mean_part, logvar = moments_ref[:, :latent], moments_ref[:, latent:]
            sample_ref[...] = (mean_part + jnp.exp(0.5 * logvar) * noise_ref[...]).astype(LOW)
            gap = mean_part - matmul(choose_ref[...], tables_ref[0])
            far = matmul(choose_ref[...], tables_ref[1])
            diverge = 0.5 * (far - logvar + (jnp.exp(logvar) + gap * gap) * jnp.exp(-far) - 1.0)
            kl_ref[...] = jnp.sum(diverge, axis=0, keepdims=True)

    return pl.pallas_call(
        kernel,
        grid_spec=by_region(
            steps,
            [whole(cells, width), whole(cells, latent), whole(*choose.shape)]
            + [whole(*comp_tables.shape)]
            + (
                half_specs(cells, tile // 8, width, steps, turns)
                if parts
                else [pl.BlockSpec((cells, tile), region_columns)] + [FAR_AWAY] * (mine - 1)
            )
            + [FAR_AWAY] * more,
            [whole(cells, width), whole(cells, 2 * latent), whole(cells, latent), whole(1, latent)],
            [
                pltpu.VMEM((cells, width), FULL),
                *([] if parts else [pltpu.VMEM(down.shape, LOW)]),
                pltpu.VMEM(to_latent.shape, LOW),
                pltpu.SemaphoreType.DMA((steps + 1,)),
            ],
        ),
        out_shape=[
            jax.ShapeDtypeStruct((cells, width), LOW),
            jax.ShapeDtypeStruct((cells, 2 * latent), FULL),
            jax.ShapeDtypeStruct((cells, latent), LOW),
            jax.ShapeDtypeStruct((1, latent), FULL),
        ],
        compiler_params=params(30),
        cost_estimate=cost(2 * cells * width * (hidden.shape[1] + width), 20 << 20),
        name="latent",
    )(
        table,
        middle,
        noise,
        choose,
        comp_tables,
        *([hidden] * 4 + parts if parts else [hidden, *down.operands]),
        *to_latent.operands,
    )


def decode_kernel(table, sample, cotangent, turned, decode):
    cells, width = cotangent.shape
    latent = sample.shape[1]
    parts = len(decode.operands)

    def kernel(table_ref, sample_ref, dy_ref, turned_ref, *rest):
        refs, (out_ref, grad_ref, back_ref, bias_ref, held, sem) = rest[:parts], rest[parts:]
        decode.start(table_ref, refs, held, sem)
        grad_ref[...] = left_product(sample_ref[...], dy_ref[...]).astype(LOW)
        bias_ref[...] = jnp.sum(dy_ref[...].astype(FULL), axis=0, keepdims=True)
        arrived(held, sem.at[0])
        back_ref[...] = right_product(dy_ref[...], held[...])
        out_ref[...] = (matmul(sample_ref[...], held[...]) + turned_ref[2:3]).astype(LOW)

    return pl.pallas_call(
        kernel,
        in_specs=[SCALARS] + [INSIDE] * 3 + [FAR_AWAY] * parts,
        out_specs=[INSIDE] * 4,
        out_shape=[
            jax.ShapeDtypeStruct((cells, width), LOW),
            jax.ShapeDtypeStruct((latent, width), LOW),
            jax.ShapeDtypeStruct((cells, latent), FULL),
            jax.ShapeDtypeStruct((1, width), FULL),
        ],
        scratch_shapes=[pltpu.VMEM(decode.shape, LOW), pltpu.SemaphoreType.DMA((1,))],
        compiler_params=params(16),
        cost_estimate=cost(6 * cells * width * latent, 8 << 20),
        name="decode",
    )(table, sample, cotangent, turned, *decode.operands)


def factors_kernel(back, moments, noise, choose, comp_tables):
    cells, latent = noise.shape
    comps = choose.shape[1]

    def kernel(back_ref, mom_ref, noise_ref, choose_ref, tables_ref, plain_ref, factor_ref, comp_ref):
        mean_part, logvar = mom_ref[:, :latent], mom_ref[:, latent:]
        gap = mean_part - matmul(choose_ref[...], tables_ref[0])
        shrink = jnp.exp(-matmul(choose_ref[...], tables_ref[1]))
        ratio = jnp.exp(logvar) * shrink
        moved = gap * shrink
        factor_ref[:, :latent] = moved
        factor_ref[:, latent:] = (ratio - 1.0) * 0.5
        for i, value in enumerate((-moved, (1.0 - (ratio + gap * moved)) * 0.5)):
            high = value.astype(LOW)
            rest = (value - high.astype(FULL)).astype(LOW)
            chosen = choose_ref[...]
            comp_ref[i] = left_product(chosen, high) + left_product(chosen, rest)
        back = back_ref[...]
        plain_ref[:, :latent] = back
        plain_ref[:, latent:] = back * noise_ref[...] * jnp.exp(0.5 * logvar) * 0.5

    return pl.pallas_call(
        kernel,
        in_specs=[INSIDE] * 5,
        out_specs=[INSIDE] * 3,
        out_shape=[
            jax.ShapeDtypeStruct((cells, 2 * latent), FULL),
            jax.ShapeDtypeStruct((cells, 2 * latent), FULL),
            jax.ShapeDtypeStruct((2, comps, latent), FULL),
        ],
        compiler_params=params(16),
        cost_estimate=cost(200 * cells * latent, 10 << 20),
        name="factors",
    )(back, moments, noise, choose, comp_tables)


def plain_slots(slots, grads):
    far = slots.count // 4
    results = []
    for other in (False, True):
        owner, core = slot_owner(place(), jnp.arange(slots.count), far, other, slots.base == 0)
        result = jnp.zeros((slots.count, slots.rows, slots.cols), LOW)
        for grad, height, row, col in grads:
            blocks = grad.reshape(slots.count, 2, height, grad.shape[1])
            blocks = jnp.take(blocks[:, core], owner, axis=0)
            result = result.at[:, row : row + height, col : col + grad.shape[1]].set(blocks)
        results += [result[: slots.count // 2], result[slots.count // 2 :]]
    return results


def moments_kernel(table, kl_weight, total, kl_sum, plain, factor, carried, comp, grad_decode, to_latent, slots):
    cells, width = carried.shape
    latent = kl_sum.shape[1]
    parts = len(to_latent.operands)
    height = to_latent.piece[1]
    decode_height = grad_decode.shape[0] // (2 * slots.count)
    direct = height % 16 == 0 and decode_height % 16 == 0

    def kernel(table_ref, weight_ref, kl_ref, plain_ref, factor_ref, carried_ref, comp_ref, gd_ref, *rest):
        refs, rest = rest[:parts], rest[parts:]
        gc_ref, comp_out, *rest = rest
        outs, rest = rest[: 4 if direct else 1], rest[4 if direct else 1 :]
        held, grads, sums, sems = rest
        to_latent.start(table_ref, refs, held, sems.at[pl.ds(0, 1)])
        mean = kl_ref[...] * (1.0 / total)
        coef = weight_ref[0] * jax.nn.sigmoid((mean - FREE_BITS) * (1.0 / SOFTNESS))
        for i in range(2):
            some = pl.ds(i * latent, latent)
            comp_out[i] = comp_ref[i] * coef
            grads[:, some] = (plain_ref[:, some] + factor_ref[:, some] * coef).astype(LOW)
        sums[...] = left_product(carried_ref[...], grads[...]).astype(LOW)
        if direct:
            slots.start(
                table_ref, [(sums, height, 0, 0), (gd_ref, decode_height, height, 0)], outs, sems.at[1]
            )
        else:
            outs[0][...] = sums[...]
        arrived(held, sems.at[0])
        gc_ref[...] = right_product(grads[...], held[...]).astype(LOW)
        if direct:
            for out in outs:
                arrived(out, sems.at[1])

    results = pl.pallas_call(
        kernel,
        in_specs=[SCALARS, SCALARS] + [INSIDE] * 6 + [FAR_AWAY] * parts,
        out_specs=[INSIDE] * 2 + ([FAR_AWAY] * 4 if direct else [INSIDE]),
        out_shape=[
            jax.ShapeDtypeStruct((cells, width), LOW),
            jax.ShapeDtypeStruct(comp.shape, FULL),
        ]
        + (slots.shapes() if direct else [jax.ShapeDtypeStruct((width, 2 * latent), LOW)]),
        scratch_shapes=[
            pltpu.VMEM(to_latent.shape, LOW),
            pltpu.VMEM((cells, 2 * latent), LOW),
            pltpu.VMEM((width, 2 * latent), LOW),
            pltpu.SemaphoreType.DMA((2,)),
        ],
        compiler_params=params(24),
        cost_estimate=cost(8 * cells * width * latent, 16 << 20),
        name="moments",
    )(table, kl_weight, kl_sum, plain, factor, carried, comp, grad_decode, *to_latent.operands)
    if direct:
        return results
    grads = [(results[2], height, 0, 0), (grad_decode, decode_height, height, 0)]
    return list(results[:2]) + plain_slots(slots, grads)


def weight_grad(table, left, rights, slots, height, name, extra=()):
    cells, rows = left.shape
    each = rights[0].shape[1]
    cols = each * len(rights)
    direct = height % 16 == 0
    tile = 512 if cols <= 1024 else 256
    steps = rows // tile
    extra = list(extra)

    def product(left_ref, right_refs, target):
        for i, right_ref in enumerate(right_refs):
            block = left_product(left_ref[...], right_ref[...])
            target[:, pl.ds(i * each, each)] = block.astype(LOW)

    def kernel(table_ref, left_ref, *rest):
        right_refs, rest = rest[: len(rights)], rest[len(rights) :]
        if not direct:
            product(left_ref, right_refs, rest[0])
            return
        more, rest = rest[: len(extra)], rest[len(extra) :]
        outs, (sums, sems) = rest[:4], rest[4:]
        step = pl.program_id(0)

        @pl.when(step == 0)
        def _():
            for ref, one in zip(more, extra):
                slots.start(table_ref, [(ref, one[1], one[2], one[3])], outs, sems.at[2])

        current = lax.rem(step, 2)

        @pl.when(step >= 2)
        def _():
            arrived(sums.at[current], sems.at[current])

        product(left_ref, right_refs, sums.at[current])
        slots.send(table_ref, sums.at[current], step * (tile // height), outs, sems.at[current])

        @pl.when(step == steps - 1)
        def _():
            arrived(sums.at[0], sems.at[0])
            arrived(sums.at[1], sems.at[1])
            for ref in more:
                arrived(ref, sems.at[2])

    results = pl.pallas_call(
        kernel,
        grid=(steps,),
        in_specs=[SCALARS, pl.BlockSpec((cells, tile), lambda i: (0, i))]
        + [whole(cells, each)] * len(rights)
        + [whole(*one[0].shape) for one in (extra if direct else [])],
        out_specs=[ANYWHERE] * 4 if direct else [pl.BlockSpec((tile, cols), lambda i: (i, 0))],
        out_shape=slots.shapes() if direct else [jax.ShapeDtypeStruct((rows, cols), LOW)],
        scratch_shapes=[pltpu.VMEM((2, tile, cols), LOW), pltpu.SemaphoreType.DMA((3,))]
        if direct
        else [],
        compiler_params=params(28),
        cost_estimate=cost(2 * cells * rows * cols, 2 * rows * cols),
        name=name,
    )(table, left, *rights, *[one[0] for one in (extra if direct else [])])
    if direct:
        return results
    return plain_slots(slots, [(results[0], height, 0, 0)] + extra)


def up_back_kernel(table, grad_carried, slope, down):
    cells, width = grad_carried.shape
    cols = slope.shape[1]
    parts = len(down.operands)
    steps = down.count // 4
    tile = cols // steps

    def kernel(table_ref, grad_ref, slope_ref, *rest):
        refs, (out_ref, held, sems) = rest[:parts], rest[parts:]
        step = pl.program_id(0)

        @pl.when(step == 0)
        def _():
            down.start(table_ref, refs, held, sems, 1)

        some = held.at[down.region(table_ref, step)]
        arrived(some, sems.at[step])
        out_ref[...] = (right_product(grad_ref[...], some[...]) * slope_ref[...]).astype(LOW)

    return pl.pallas_call(
        kernel,
        grid_spec=by_region(
            steps,
            [whole(cells, width), pl.BlockSpec((cells, tile), region_columns)]
            + [FAR_AWAY] * parts,
            pl.BlockSpec((cells, tile), region_columns),
            [pltpu.VMEM(down.shape, LOW), pltpu.SemaphoreType.DMA((steps,))],
        ),
        out_shape=jax.ShapeDtypeStruct((cells, cols), LOW),
        compiler_params=params(24),
        cost_estimate=cost(2 * cells * width * cols, 22 << 20),
        name="up_back",
    )(table, grad_carried, slope, *down.operands)


def middle_back_kernel(table, grad_up_proj, grad_carried, middle, mixed, turned, up, out_proj):
    cells, width = grad_carried.shape
    cols = grad_up_proj.shape[1]
    parts, more = len(up.operands), len(out_proj.operands)
    steps = up.count // 8

    def kernel(table_ref, gu_ref, gc_ref, mid_ref, mixed_ref, turned_ref, *rest):
        refs, rest = rest[:parts], rest[parts:]
        out_refs, rest = rest[:more], rest[more:]
        gm_ref, go_ref, gx_ref, gain_ref, gu_held, second, held, out_held, sems = rest
        loading = pltpu.make_async_copy(gu_ref, gu_held, sems.at[steps + 1])
        loading.start()
        up.start(table_ref, refs, held, sems, 2)
        out_proj.start(table_ref, out_refs, out_held, sems.at[pl.ds(steps, 1)])
        loading.wait()
        for step in range(steps):
            some = up.region(table_ref, step, 2)
            arrived(held.at[some], sems.at[step])
            second[:, some] = right_product(gu_held[...], held[some])
        normed, scale = norm_parts(mid_ref[...])
        grad_second = second[...]
        gain_ref[...] = jnp.sum(normed * grad_second, axis=0, keepdims=True)
        back = norm_back(normed, scale, grad_second, turned_ref[1:2])
        grad_middle = gc_ref[...].astype(FULL) + back
        gm_ref[...] = grad_middle
        branch = grad_middle.astype(LOW)
        go_ref[...] = left_product(mixed_ref[...], branch).astype(LOW)
        arrived(out_held, sems.at[steps])
        gx_ref[...] = right_product(branch, out_held[...]).astype(LOW)

    return pl.pallas_call(
        kernel,
        in_specs=[SCALARS, ANYWHERE] + [INSIDE] * 4 + [ANYWHERE] * (parts + more),
        out_specs=[INSIDE] * 4,
        out_shape=[
            jax.ShapeDtypeStruct((cells, width), FULL),
            jax.ShapeDtypeStruct((width, width), LOW),
            jax.ShapeDtypeStruct((cells, width), LOW),
            jax.ShapeDtypeStruct((1, width), FULL),
        ],
        scratch_shapes=[
            pltpu.VMEM((cells, cols), LOW),
            pltpu.VMEM((cells, width), FULL),
            pltpu.VMEM(up.shape, LOW),
            pltpu.VMEM(out_proj.shape, LOW),
            pltpu.SemaphoreType.DMA((steps + 2,)),
        ],
        compiler_params=params(50),
        cost_estimate=cost(2 * cells * width * (cols + width), 22 << 20),
        name="middle_back",
    )(table, grad_up_proj, grad_carried, middle, mixed, turned, *up.operands, *out_proj.operands)


def input_back_kernel(table, grad_packed, grad_middle, inputs, turned, small, columns, weight):
    cells, width = inputs.shape
    parts = len(weight.operands)
    steps = weight.count // 8

    def kernel(table_ref, gq_ref, gk_ref, gv_ref, gm_ref, in_ref, turned_ref, small_ref, *rest):
        column_refs, rest = rest[: len(columns)], rest[len(columns) :]
        refs, (gx_ref, small_out, first, held, sems) = rest[:parts], rest[parts:]
        weight.start(table_ref, refs, held, sems, 2)
        normed, scale = norm_parts(in_ref[...].astype(FULL))
        for step in range(steps):
            some = weight.region(table_ref, step, 2)
            arrived(held.at[some], sems.at[step])
            first[:, some] = sum(
                right_product(ref[...], held[some, i * width : (i + 1) * width])
                for i, ref in enumerate((gq_ref, gk_ref, gv_ref))
            )
        grad_first = first[...]
        gain = jnp.sum(normed * grad_first, axis=0, keepdims=True)
        lane = lax.broadcasted_iota(jnp.int32, (width, 128), 1)
        block = small_ref[...]
        for k, one in enumerate((gain, *[ref[...] for ref in column_refs])):
            one = jnp.transpose(jnp.broadcast_to(one, (128, width)))
            block = jnp.where(lane == k, one, block)
        small_out[...] = block.astype(LOW)
        gx_ref[...] = gm_ref[...] + norm_back(normed, scale, grad_first, turned_ref[0:1])

    return pl.pallas_call(
        kernel,
        in_specs=[SCALARS] + [INSIDE] * (7 + len(columns)) + [FAR_AWAY] * parts,
        out_specs=[INSIDE] * 2,
        out_shape=[
            jax.ShapeDtypeStruct((cells, width), FULL),
            jax.ShapeDtypeStruct((width, 128), LOW),
        ],
        scratch_shapes=[
            pltpu.VMEM((cells, width), FULL),
            pltpu.VMEM(weight.shape, LOW),
            pltpu.SemaphoreType.DMA((steps,)),
        ],
        compiler_params=params(44),
        cost_estimate=cost(6 * cells * width * width, 18 << 20),
        name="input_back",
    )(table, *grad_packed, grad_middle, inputs, turned, small, *columns, *weight.operands)


def small_block(columns, rest):
    rows = rest.shape[0]
    gap = jnp.zeros((rows, 16 - len(columns)), rest.dtype)
    end = jnp.zeros((rows, 112 - rest.shape[1]), rest.dtype)
    return jnp.concatenate([*columns, gap, rest, end], axis=1)


def join(*parts):
    _, rows, cols = parts[0].shape
    flat = jnp.concatenate([part.reshape(-1, cols) for part in parts], axis=0)
    return flat.reshape(-1, rows, cols)


def far_start(block):
    return [far_exchange(block, mask) for mask in far_masks()]


def add_low(one, two):
    return (one.astype(FULL) + two.astype(FULL)).astype(LOW)


def add_slots(size, *terms):
    parts = [array[first : first + size] for array, first in terms]
    return add_all(parts[0], parts[1:]).astype(LOW)


def both_cores(slots, got, turn, far):
    return add_slots(far, *[(pair[turn // 2], turn % 2 * far) for pair in (slots, got)])


def add_all(first, others):
    total = first.astype(FULL)
    for one in others:
        total = total + one.astype(FULL)
    return total


def odd_even(*terms):
    return [add_all(one[0], one[1:]).astype(LOW) for one in zip(*[(t[1::2], t[0::2]) for t in terms])]


def far_last(odd, even, bit):
    got = far_exchange(odd, bit)
    while even.shape[0] > 1:
        bit *= 2
        odd, even = odd_even(even, got)
        got = far_exchange(odd, bit)
    return even, got


def far_slots(value, size):
    return [far_exchange(value[m * size : (m + 1) * size], m) for m in far_masks()]


def matmul(left_side, right_side):
    return jnp.dot(left_side, right_side, preferred_element_type=FULL)


def left_product(left_side, right_side):
    return lax.dot_general(
        left_side, right_side, (((0,), (0,)), ((), ())), preferred_element_type=FULL
    )


def right_product(left_side, right_side):
    return lax.dot_general(
        left_side, right_side, (((1,), (1,)), ((), ())), preferred_element_type=FULL
    )


def norm_parts(tensor):
    centred = tensor - jnp.mean(tensor, axis=-1, keepdims=True)
    scale = lax.rsqrt(jnp.mean(centred * centred, axis=-1, keepdims=True) + 1e-05)
    return centred * scale, scale


def norm_back(normed, scale, grad, gain):
    inner = grad * gain
    return scale * (
        inner
        - jnp.mean(inner, axis=-1, keepdims=True)
        - normed * jnp.mean(inner * normed, axis=-1, keepdims=True)
    )


def head_lanes(value, head, size):
    lane = lax.broadcasted_iota(jnp.int32, value.shape, 1)
    return jnp.where((lane // size) == head, value, jnp.zeros_like(value))


def attention_forward(packed, seg_col, seg_row, first, last, earlier=()):
    cells, three = packed.shape
    width = three // 3
    size = width // HEADS
    pair = 128 // size
    steps = HEADS // pair

    def kernel(seg_col, seg_row, q_ref, k_ref, v_ref, *rest):
        out_ref, attn_ref = rest[-2:]
        same = seg_col[...] == seg_row[...]
        queries, keys = q_ref[...], k_ref[...]
        values = jnp.transpose(v_ref[...])
        outs = []
        for head in range(pair):
            scores = right_product(head_lanes(keys, head, size), queries) * size ** (-0.5)
            scores = jnp.where(same, scores, NEGATIVE)
            powers = jnp.exp(scores - jnp.max(scores, axis=0, keepdims=True))
            attn = powers * (1.0 / jnp.sum(powers, axis=0, keepdims=True))
            attn_low = attn.astype(LOW)
            attn_ref[head] = attn_low
            outs.append(matmul(values[head * size : (head + 1) * size], attn_low))
        out_ref[...] = jnp.transpose(jnp.concatenate(outs, axis=0)).astype(LOW)

    return pl.pallas_call(
        kernel,
        grid=(last - first,),
        in_specs=[
            pl.BlockSpec((cells, 1), lambda i: (0, 0)),
            pl.BlockSpec((1, cells), lambda i: (0, 0)),
            pl.BlockSpec((cells, 128), lambda i: (0, i + first)),
            pl.BlockSpec((cells, 128), lambda i: (0, i + first + steps)),
            pl.BlockSpec((cells, 128), lambda i: (0, i + first + 2 * steps)),
        ]
        + [ANYWHERE] * len(earlier),
        out_specs=[
            pl.BlockSpec((cells, 128), lambda i: (0, i + first)),
            pl.BlockSpec((pair, cells, cells), lambda i: (i + first, 0, 0)),
        ],
        out_shape=[
            jax.ShapeDtypeStruct((cells, width), LOW),
            jax.ShapeDtypeStruct((HEADS, cells, cells), LOW),
        ],
        input_output_aliases={5 + i: i for i in range(len(earlier))},
        compiler_params=params(),
        cost_estimate=cost(4 * cells * cells * width, 24 << 20),
        name="attention_forward",
    )(seg_col, seg_row, packed, packed, packed, *earlier)


def attention_backward(packed, attn, mixed, grad_mixed):
    cells, three = packed.shape
    width = three // 3
    size = width // HEADS
    pair = 128 // size
    steps = HEADS // pair

    def kernel(q_ref, k_ref, v_ref, g_ref, mixed_ref, attn_ref, gq_ref, gk_ref, gv_ref):
        queries, keys, values, grad = q_ref[...], k_ref[...], v_ref[...], g_ref[...]
        keys_t = jnp.transpose(keys)
        inner = jnp.transpose(grad).astype(FULL) * jnp.transpose(mixed_ref[...]).astype(FULL)
        grad_q, grad_k, grad_v = [], 0.0, 0.0
        for head in range(pair):
            attn_low = attn_ref[head]
            attn = attn_low.astype(FULL)
            grad_attn = right_product(head_lanes(values, head, size), grad)
            some = slice(head * size, (head + 1) * size)
            grad_scores = attn * (grad_attn - jnp.sum(inner[some], axis=0, keepdims=True))
            grad_scores = grad_scores.astype(LOW)
            grad_q.append(matmul(keys_t[some], grad_scores))
            grad_k += head_lanes(matmul(grad_scores, queries), head, size)
            grad_v += head_lanes(matmul(attn_low, grad), head, size)
        scale = size ** (-0.5)
        gq_ref[...] = (jnp.transpose(jnp.concatenate(grad_q, axis=0)) * scale).astype(LOW)
        gk_ref[...] = (grad_k * scale).astype(LOW)
        gv_ref[...] = grad_v.astype(LOW)

    return pl.pallas_call(
        kernel,
        grid=(steps,),
        in_specs=[
            pl.BlockSpec((cells, 128), lambda i: (0, i)),
            pl.BlockSpec((cells, 128), lambda i: (0, i + steps)),
            pl.BlockSpec((cells, 128), lambda i: (0, i + 2 * steps)),
            pl.BlockSpec((cells, 128), lambda i: (0, i)),
            pl.BlockSpec((cells, 128), lambda i: (0, i)),
            pl.BlockSpec((pair, cells, cells), lambda i: (i, 0, 0)),
        ],
        out_specs=[pl.BlockSpec((cells, 128), lambda i: (0, i))] * 3,
        out_shape=[jax.ShapeDtypeStruct((cells, width), LOW)] * 3,
        compiler_params=params(44),
        cost_estimate=cost(10 * cells * cells * width, 24 << 20),
        name="attention_backward",
    )(packed, packed, packed, grad_mixed, mixed, attn)


def local(
    layer_ends,
    segment_ids,
    mixture,
    noise,
    plan_step,
    ln1_gain,
    w_qkv,
    w_out,
    ln2_gain,
    w_up,
    w_down,
    w_latent,
    w_decode,
    decode_bias,
    comp_mean,
    comp_logvar,
):
    core = lax.axis_index("pipe")
    cells = segment_ids.shape[1]
    devices = lax.axis_size("dp") * 2
    width = layer_ends.shape[2]
    latent = noise.shape[1]
    comps = comp_mean.shape[0]
    total_cells = cells * devices

    rows = w_qkv.shape[0]
    comp_cols = latent // devices
    lanes = 2 * comps * comp_cols // rows
    small = jnp.concatenate([comp_mean.reshape(-1), comp_logvar.reshape(-1)]).reshape(rows, lanes)
    columns = [ln1_gain[:, None], ln2_gain[:, None], decode_bias[:, None]]
    small = small_block(columns, small)
    qkv_cols, out_cols, up_cols = w_qkv.shape[1], w_out.shape[1], w_up.shape[1]
    first_pieces = (
        (0, rows, 0, qkv_cols),
        (0, rows, qkv_cols, out_cols),
        (0, rows, qkv_cols + out_cols, 128),
    )
    up_pieces = ((0, rows, 0, up_cols),)
    down_rows, decode_rows = w_down.shape[0], w_decode.shape[0]
    down_pieces = ((0, down_rows, 0, width),)
    last_pieces = ((0, rows, 0, width), (rows, decode_rows, 0, width))
    first_block = jnp.concatenate([w_qkv, w_out, small], axis=1)[None]
    up_block, down_block = w_up[None], w_down[None]
    last_block = jnp.concatenate([w_latent, w_decode], axis=0)[None]

    def my_rows(tensor, which):
        return lax.dynamic_slice_in_dim(tensor, which * cells, cells, axis=0)

    kept = my_rows(layer_ends[0], core)
    going = my_rows(layer_ends[0], 1 - core)
    segments = lax.dynamic_index_in_dim(segment_ids, core, keepdims=False)
    mixture_rows = my_rows(mixture, core)
    noise_rows = my_rows(noise, core)

    table = tables()
    first_far = far_start(first_block)
    got = send_core(going)
    last_near = near_first(last_block)
    got, last_near, up_block, *first_far = hold(got, last_near, up_block, *first_far)
    inputs_low = jnp.where(core == 0, kept, got)
    inputs = inputs_low.astype(FULL)
    cotangent = jnp.where(core == 0, got, kept)
    normed_one, scale_one = norm_parts(inputs)
    last_two = join(last_block, last_near)

    first_four = join(first_block, *first_far)
    first_m1, first_m2 = near_first(first_four), near_second(first_four)
    up_far = far_start(up_block)
    seg_col, seg_row = segments[:, None], segments[None, :]
    choose = mixture_rows[:, None] == jnp.arange(comps, dtype=jnp.int32)[None, :]
    first_m1, first_m2, normed_one, last_two, table, seg_col, seg_row, *rest = hold(
        first_m1,
        first_m2,
        normed_one,
        last_two,
        table,
        seg_col,
        seg_row,
        choose.astype(LOW),
        noise_rows,
        down_block,
        *up_far,
    )
    choose, noise_rows, down_block, *up_far = rest

    first_m3 = near_second(first_m1)
    first_c0, first_c1, first_c2 = [send_core(one) for one in (first_four, first_m1, first_m2)]
    down_far = [far_exchange(down_block, 1)]
    first_m3, first_c0, first_c1, first_c2, down_block, *rest = hold(
        first_m3, first_c0, first_c1, first_c2, down_block, *down_far, *up_far
    )
    down_far, up_far = rest[:1], rest[1:]

    up_four = join(up_block, *up_far)
    first_c3, up_four, down_block = hold(send_core(first_m3), up_four, down_block)
    up_m1, up_m2 = near_first(up_four), near_second(up_four)
    last_more = near_second(last_two)
    down_far += [far_exchange(down_block, mask) for mask in far_masks() if mask > 1]
    first_parts = [first_four, first_m1, first_m2, first_m3], [first_c0, first_c1, first_c2, first_c3]
    qkv, out_proj, small_rows = [Rows(*first_parts, piece) for piece in first_pieces]
    first_in, packed, small_all, turned = first_kernel(table, normed_one, qkv, small_rows)
    pairs = HEADS * (width // HEADS) // 128
    some_heads = attention_forward(packed, seg_col, seg_row, 0, pairs // 2)
    up_m1, up_m2, last_more, packed, *rest = hold(
        up_m1, up_m2, last_more, packed, *some_heads, *down_far
    )
    some_heads, down_far = rest[:2], rest[2:]
    last_four = join(last_two, last_more)

    up_m3 = near_second(up_m1)
    down_four = join(down_block, *down_far)
    down_m1 = near_first(down_four)
    up_c0 = send_core(up_four)
    last_early, last_late = [1, 2], list(far_masks())[2:]
    last_far = {mask: far_exchange(last_four, mask) for mask in last_early}
    mixed, attn = attention_forward(packed, seg_col, seg_row, pairs // 2, pairs, some_heads)
    middle, second_in = branch_kernel(table, mixed, inputs, turned, out_proj)
    small_all = small_all.reshape(devices, rows, 128)[:, :, 16 : 16 + lanes]
    small_all = small_all.reshape(devices, 2, comps, comp_cols).transpose(1, 2, 0, 3)
    comp_tables = small_all.reshape(2, comps, latent)
    early = [last_far[mask] for mask in last_early]
    up_m3, down_m1, up_c0, second_in, comp_tables, up_m1, up_m2, last_four, *early = hold(
        up_m3, down_m1, up_c0, second_in, comp_tables, up_m1, up_m2, last_four, *early
    )
    last_far.update(zip(last_early, early))

    down_m2, down_m3 = near_second(down_four), near_second(down_m1)
    up_c1, up_c2, up_c3 = [send_core(one) for one in (up_m1, up_m2, up_m3)]
    up_c1, up_c2, up_c3, last_four, down_four, down_m1 = hold(
        up_c1, up_c2, up_c3, last_four, down_four, down_m1
    )
    last_far.update((mask, far_exchange(last_four, mask)) for mask in last_late)
    up = Rows([up_four, up_m1, up_m2, up_m3], [up_c0, up_c1, up_c2, up_c3], up_pieces[0])
    hidden, slope = up_kernel(table, second_in, up)
    down_c0, down_c1 = send_core(down_four), send_core(down_m1)
    late = [last_far[mask] for mask in last_late]
    down_m2, down_m3, down_c0, down_c1, hidden, *late = hold(
        down_m2, down_m3, down_c0, down_c1, hidden, *late
    )
    last_far.update(zip(last_late, late))

    last_all = join(last_four, *[last_far[mask] for mask in far_masks()])
    last_there = send_core(last_all)
    down_c2, down_c3 = send_core(down_m2), send_core(down_m3)
    in_halves = down_rows % 128 == 0
    if in_halves:
        middle_half = down_half(
            table, hidden, middle, [down_four, down_m1, down_c0, down_c1], (0, 1)
        )
        last_there, down_c2, down_c3, middle_half = hold(
            last_there, down_c2, down_c3, middle_half
        )
    else:
        last_there, down_c2, down_c3 = hold(last_there, down_c2, down_c3)
    to_latent, decode = [Rows([last_all], [last_there], piece, False) for piece in last_pieces]
    down = Rows(
        [down_four, down_m1, down_m2, down_m3], [down_c0, down_c1, down_c2, down_c3], down_pieces[0]
    )
    carried, moments, sample, kl_part = latent_kernel(
        table,
        hidden,
        middle_half if in_halves else middle,
        noise_rows,
        choose,
        comp_tables,
        down,
        to_latent,
        [down_m2, down_m3, down_c2, down_c3] if in_halves else None,
        (2, 3),
    )
    kl_sum = kl_part + send_core(kl_part)
    kl_sum, sample = hold(kl_sum, sample)
    decoded, grad_decode, grad_sample, grad_bias = decode_kernel(
        table, sample, cotangent, turned, decode
    )
    kl_near = [send(kl_sum, bit, bit) for bit in (2, 4, 6)]
    kl_sum = sum(kl_near, kl_sum)
    kl_sum, grad_sample, decoded = hold(kl_sum, grad_sample, decoded)
    kl_far = [far_exchange(kl_sum, mask) for mask in far_masks()]
    plain, factor, comp = factors_kernel(grad_sample, moments, noise_rows, choose, comp_tables)
    kl_sum = sum(kl_far, kl_sum)
    kl_sum, grad_decode, plain, factor, grad_bias, decoded = hold(
        kl_sum, grad_decode, plain, factor, grad_bias, decoded
    )

    far = lax.axis_size("dp") // 4
    kl_weight = jnp.minimum(1.0, (plan_step + 1).astype(FULL) / WARM)
    grad_carried, comp, *last_slots = moments_kernel(
        table,
        kl_weight,
        total_cells,
        kl_sum,
        plain,
        factor,
        carried,
        comp,
        grad_decode,
        to_latent,
        Slots(rows + decode_rows, width),
    )
    grad_carried, hidden, decoded, *last_slots = hold(grad_carried, hidden, decoded, *last_slots)
    decoded_there = send_core(decoded)
    last_got = [send_core(one) for one in last_slots[2:]]
    down_slots = weight_grad(
        table, hidden, [grad_carried], Slots(down_rows, width), down_rows, "grad_down"
    )
    grad_carried, decoded_there, *rest = hold(
        grad_carried, decoded_there, *last_got, *down_slots
    )
    last_got, down_slots = rest[:2], rest[2:]

    down_got = [send_core(one) for one in down_slots[2:]]
    last_3, last_2 = [both_cores(last_slots, last_got, turn, far) for turn in (3, 2)]
    last_m3, last_m2 = near_second(last_3), near_second(last_2)
    grad_up_proj = up_back_kernel(table, grad_carried, slope, down)
    grad_up_proj, last_m3, last_m2, *down_got = hold(grad_up_proj, last_m3, last_m2, *down_got)
    down_m3 = near_second(both_cores(down_slots, down_got, 3, far))
    up_slots = weight_grad(
        table, second_in, [grad_up_proj], Slots(rows, up_cols), rows, "grad_up"
    )
    down_0, down_1, down_2 = [both_cores(down_slots, down_got, turn, far) for turn in range(3)]
    tables_grad = comp.reshape(2, comps, devices, comp_cols)
    tables_grad = tables_grad.transpose(2, 0, 1, 3).reshape(devices * rows, lanes)
    small_grads = jnp.pad(tables_grad, ((0, 0), (16, 112 - lanes)))
    down_m3, last_m3, small_grads, down_0, down_1, down_2, *up_slots = hold(
        down_m3, last_m3, small_grads, down_0, down_1, down_2, *up_slots
    )

    up_got = [send_core(one) for one in up_slots[2:]]
    down_m2 = near_second(down_2)
    last_m1 = near_first(add_slots(far, (last_slots[0], far), (last_got[0], far), (last_m3, 0)))
    grad_middle, grad_out, grad_mixed, grad_gain_two = middle_back_kernel(
        table, grad_up_proj, grad_carried, middle, mixed, turned, up, out_proj
    )
    down_m2, last_m1, grad_mixed, grad_out, *up_got = hold(
        down_m2, last_m1, grad_mixed, grad_out, *up_got
    )

    up_m3 = near_second(both_cores(up_slots, up_got, 3, far))
    down_m1 = near_first(add_slots(far, (down_1, 0), (down_m3, 0)))
    grad_packed = attention_backward(packed, attn, mixed, grad_mixed)
    up_m3, down_m1, *grad_packed = hold(up_m3, down_m1, *grad_packed)

    up_m2 = near_second(both_cores(up_slots, up_got, 2, far))
    up_m1 = near_first(add_slots(far, (up_slots[0], far), (up_got[0], far), (up_m3, 0)))
    down_odd, down_even = odd_even(down_0, down_m2, down_m1)
    down_far = far_exchange(down_odd, 1)
    grad_inputs, small_grads = input_back_kernel(
        table,
        grad_packed,
        grad_middle,
        inputs_low,
        turned,
        small_grads,
        [grad_gain_two, grad_bias],
        qkv,
    )
    first_slots = weight_grad(
        table,
        first_in,
        grad_packed,
        Slots(rows, qkv_cols + out_cols + 128),
        rows,
        "grad_qkv",
        [(grad_out, rows, 0, qkv_cols), (small_grads, rows, 0, qkv_cols + out_cols)],
    )
    up_m2, up_m1, grad_inputs, down_far, *first_slots = hold(
        up_m2, up_m1, grad_inputs, down_far, *first_slots
    )

    first_high = send_core(first_slots[3])
    up_odd, up_even = odd_even(up_slots[0][:far], up_got[0][:far], up_m2, up_m1)
    first_high, up_odd, up_even, *first_slots = hold(first_high, up_odd, up_even, *first_slots)
    first_low = send_core(first_slots[2])
    first_got = [first_low, first_high]
    first_3, first_2 = [both_cores(first_slots, first_got, turn, far) for turn in (3, 2)]
    last_odd, last_even = odd_even(last_slots[0][:far], last_got[0][:far], last_m2, last_m1)
    down_odd, down_even = odd_even(down_even, down_far)
    first_low, first_3, first_2, last_odd, last_even, down_odd, down_even = hold(
        first_low, first_3, first_2, last_odd, last_even, down_odd, down_even
    )

    first_m3, first_m2 = near_second(first_3), near_second(first_2)
    up_far = far_exchange(up_odd, 1)
    last_far = far_exchange(last_odd, 1)
    down_even, down_far = far_last(down_odd, down_even, 2)
    first_m3, first_m2, up_far, last_far, down_far = hold(
        first_m3, first_m2, up_far, last_far, down_far
    )

    first_m1 = near_first(add_slots(far, (first_slots[0], far), (first_low, far), (first_m3, 0)))
    inputs_there = send_core(grad_inputs)
    up_odd, up_even = odd_even(up_even, up_far)
    last_odd, last_even = odd_even(last_even, last_far)
    up_even, up_far = far_last(up_odd, up_even, 2)
    last_even, last_far = far_last(last_odd, last_even, 2)
    down_sum = add_all(down_even[0], [down_far[0]])
    first_m1, inputs_there, down_sum, up_far, last_far = hold(
        first_m1, inputs_there, down_sum, up_far, last_far
    )
    up_sum = add_all(up_even[0], [up_far[0]])
    last_sum = add_all(last_even[0], [last_far[0]])

    result = jnp.where(
        core == 0,
        jnp.concatenate([grad_inputs, inputs_there], axis=0),
        jnp.concatenate([decoded_there, decoded], axis=0).astype(FULL),
    )[None]
    first_all = add_slots(far, (first_slots[0], 0), (first_low, 0), (first_m2, 0), (first_m1, 0))
    first_far = far_slots(first_all, 1)
    pieces = [first_all[0], *[one[0] for one in first_far]]

    def first_sum(start, size):
        parts = [one[:, start : start + size] for one in pieces]
        return add_all(parts[0], parts[1:])

    small_sum = first_sum(qkv_cols + out_cols, 128)
    comp_mean_sum, comp_logvar_sum = small_sum[:, 16 : 16 + lanes].reshape(2, comps, comp_cols)
    return (
        result,
        small_sum[:, 0],
        first_sum(0, qkv_cols),
        first_sum(qkv_cols, out_cols),
        small_sum[:, 1],
        up_sum,
        down_sum,
        last_sum[:rows],
        last_sum[rows:],
        small_sum[:, 2],
        comp_mean_sum,
        comp_logvar_sum,
    )


def solution(mesh):
    split = P(EVERY)
    wide = P(EVERY, None)
    tall = P(None, EVERY)
    ends = P("pipe", "dp", None)
    return jax.shard_map(
        local,
        mesh=mesh,
        in_specs=(
            ends,
            P("dp", None),
            P("dp"),
            P("dp", None),
            P(),
            split,
            wide,
            wide,
            split,
            wide,
            wide,
            wide,
            wide,
            split,
            tall,
            tall,
        ),
        out_specs=(ends, split, wide, wide, split, wide, wide, wide, wide, split, tall, tall),
        check_vma=False,
    )
```

```python
import functools

import jax
import jax.numpy as jnp
from jax import lax
from jax.experimental import pallas as pl
from jax.experimental.pallas import tpu as pltpu
from jax.sharding import PartitionSpec as P

HEADS = 16
WARM = 1000
FREE_BITS = 0.8
SOFTNESS = 0.2
NEGATIVE = -1e30
EVERY = ("dp", "pipe")
LOW = jnp.bfloat16
FULL = jnp.float32


def hold(*values):
    return lax.optimization_barrier(values)


def swap_bits(mask):
    return (mask & 1) * 2 + (mask >> 1)


def send(value, even, odd):
    count = lax.axis_size("dp") * lax.axis_size("pipe")
    pairs = [(i, i ^ (odd if i & 1 else even)) for i in range(count)]
    return lax.ppermute(value, EVERY, pairs)


def send_core(value):
    return send(value, 1, 1)


def far_masks():
    return range(1, lax.axis_size("dp") // 4)


def far_exchange(value, mask):
    return send(value, mask * 8, mask * 8)


def near_first(value):
    return send(value, 2, 4)


def near_second(value):
    return send(value, 4, 2)


def place():
    return jnp.stack([lax.axis_index("dp"), lax.axis_index("pipe")]).astype(jnp.int32)


def slot_owner(where, slot, far, other_core, far_first):
    turn, step = (slot // far, slot % far) if far_first else (slot % 4, slot // 4)
    core = where[1]
    if other_core:
        core = 1 - core
    near = jnp.where(core == 0, turn, swap_bits(turn))
    return (where[0] ^ (4 * step)) ^ near, core


def slot_of(where, dp_index, core, far, far_first):
    apart = dp_index ^ where[0]
    step, near = apart // 4, apart % 4
    turn = jnp.where(core == 0, near, swap_bits(near))
    slot = turn * far + step if far_first else step * 4 + turn
    return slot + jnp.where(core == where[1], 0, 4 * far)


def tables():
    far = lax.axis_size("dp") // 4
    slots = jnp.arange(4 * far)
    rows = []
    for far_first in (True, False):
        for other in (False, True):
            owner, core = slot_owner(place(), slots, far, other, far_first)
            rows.append(owner * 2 + core)
    blocks = jnp.arange(8 * far)
    back = slot_of(place(), blocks // 2, blocks % 2, far, True) % (4 * far)
    return jnp.concatenate(rows + [back]).astype(jnp.int32)


class Rows:
    def __init__(self, own, other, piece, far_first=True):
        self.piece = row, height, col, width = piece
        self.count = sum(part.shape[0] for part in own)
        self.base = 0 if far_first else 2 * self.count
        self.shape = (2 * self.count * height, width)
        self.slots = height % 16 == 0
        if self.slots:
            self.operands = list(own) + list(other)
        else:
            every = jnp.concatenate(list(own) + list(other), axis=0)
            index = jnp.arange(2 * self.count)
            picked = slot_of(place(), index // 2, index % 2, self.count // 4, far_first)
            picked = jnp.take(every, picked, axis=0)
            self.operands = [picked[:, row : row + height, col : col + width].reshape(self.shape)]

    def region(self, table, step, group=1):
        height = 8 * self.piece[1] * group
        start = ((table[0] // (8 * group)) ^ step) * height
        return pl.ds(pl.multiple_of(start, height), height)

    def start(self, table, refs, target, sems, group=0, columns=None):
        row, height, col, width = self.piece
        first, width = columns or (0, width)
        columns = pl.ds(first, width)
        far = self.count // 4
        if not self.slots:
            for step in range(far // group if group else 1):
                some = self.region(table, step, group) if group else pl.ds(0, self.shape[0])
                source = refs[0].at[some, columns]
                pltpu.make_async_copy(source, target.at[some, columns], sems.at[step]).start()
            return
        found = [ref.at[k] for ref in refs for k in range(ref.shape[0])]
        steps = [s % self.count % far if self.base == 0 else s % self.count // 4 for s in range(len(found))]
        for slot in sorted(range(len(found)), key=lambda s: steps[s]):
            block = pl.multiple_of(table[self.base + slot] * height, height)
            pltpu.make_async_copy(
                found[slot].at[pl.ds(row, height), pl.ds(col + first, width)],
                target.at[pl.ds(block, height), columns],
                sems.at[steps[slot] // group if group else 0],
            ).start()


def arrived(target, sem):
    pltpu.make_async_copy(target, target, sem).wait()


class Slots:
    def __init__(self, rows, cols, far_first=True):
        self.count = lax.axis_size("dp")
        self.base = 0 if far_first else 2 * self.count
        self.rows, self.cols = rows, cols

    def shapes(self):
        return [jax.ShapeDtypeStruct((self.count // 2, self.rows, self.cols), LOW)] * 4

    def start(self, table, sources, outs, sem):
        half = self.count // 2
        for slot in range(2 * self.count):
            out = outs[slot // half].at[slot % half]
            for source, height, row, col in sources:
                block = pl.multiple_of(table[self.base + slot] * height, height)
                pltpu.make_async_copy(
                    source.at[pl.ds(block, height)],
                    out.at[pl.ds(row, height), pl.ds(col, source.shape[1])],
                    sem,
                ).start()

    def send(self, table, source, first_block, outs, sem):
        half = self.count // 2
        own_core = table[0] % 2
        columns = pl.ds(0, source.shape[1])
        for i in range(source.shape[0] // self.rows):
            slot = table[4 * self.count + first_block + i]
            part = source.at[pl.ds(i * self.rows, self.rows)]
            which = 2 * jnp.where(own_core == i % 2, 0, 1) + slot // half
            for k, out in enumerate(outs):

                @pl.when(which == k)
                def _():
                    target = out.at[lax.rem(slot, half), :, columns]
                    pltpu.make_async_copy(part, target, sem).start()


ANYWHERE = pl.BlockSpec(memory_space=pl.ANY)
FAR_AWAY = pl.BlockSpec(memory_space=pltpu.HBM)
SCALARS = pl.BlockSpec(memory_space=pltpu.SMEM)
INSIDE = pl.BlockSpec(memory_space=pltpu.VMEM)


def whole(*shape):
    return pl.BlockSpec(shape, lambda *_: (0,) * len(shape))


def params(megabytes=60):
    return pltpu.CompilerParams(vmem_limit_bytes=megabytes << 20)


def cost(flops, bytes_accessed, transcendentals=0):
    return pl.CostEstimate(flops=1024, bytes_accessed=1024, transcendentals=0)


def region_columns(step, table):
    return (0, (table[0] // 8) ^ step)


def by_region(steps, in_specs, out_specs, scratch):
    return pltpu.PrefetchScalarGridSpec(
        num_scalar_prefetch=1,
        grid=(steps,),
        in_specs=in_specs,
        out_specs=out_specs,
        scratch_shapes=scratch,
    )


def first_kernel(table, normed, weight, small):
    cells, width = normed.shape
    cols, tile = weight.shape[1], 512
    parts = len(weight.operands)

    def kernel(table_ref, normed_ref, *rest):
        refs, rest = rest[:parts], rest[parts:]
        small_refs, rest = rest[: len(small.operands)], rest[len(small.operands) :]
        in_ref, packed_ref, small_ref, turned_ref, held, sems = rest
        step = pl.program_id(0)

        @pl.when(step == 0)
        def _():
            small.start(table_ref, small_refs, small_ref, sems.at[pl.ds(0, 1)])
            weight.start(table_ref, refs, held, sems.at[pl.ds(1, 1)], columns=(0, tile))
            weight.start(table_ref, refs, held, sems.at[pl.ds(2, 1)], columns=(tile, cols - tile))
            arrived(small_ref, sems.at[0])
            turned = jnp.transpose(small_ref[...].astype(FULL))
            turned_ref[...] = turned
            in_ref[...] = (normed_ref[...] * turned[0:1]).astype(LOW)
            arrived(held.at[:, pl.ds(0, tile)], sems.at[1])

        @pl.when(step == 1)
        def _():
            arrived(held.at[:, pl.ds(tile, cols - tile)], sems.at[2])

        columns = held[:, pl.ds(pl.multiple_of(step * tile, tile), tile)]
        packed_ref[...] = matmul(in_ref[...], columns).astype(LOW)

    return pl.pallas_call(
        kernel,
        grid=(cols // tile,),
        in_specs=[SCALARS, whole(cells, width)]
        + [ANYWHERE] * (parts + len(small.operands)),
        out_specs=[
            whole(cells, width),
            pl.BlockSpec((cells, tile), lambda i: (0, i)),
            whole(*small.shape),
            whole(128, small.shape[0]),
        ],
        out_shape=[
            jax.ShapeDtypeStruct((cells, width), LOW),
            jax.ShapeDtypeStruct((cells, cols), LOW),
            jax.ShapeDtypeStruct(small.shape, LOW),
            jax.ShapeDtypeStruct((128, small.shape[0]), FULL),
        ],
        scratch_shapes=[pltpu.VMEM(weight.shape, LOW), pltpu.SemaphoreType.DMA((3,))],
        compiler_params=params(),
        cost_estimate=cost(2 * cells * width * cols, 14 << 20),
        name="first",
    )(table, normed, *weight.operands, *small.operands)


def branch_kernel(table, mixed, inputs, turned, weight):
    cells, width = inputs.shape
    parts, tile = len(weight.operands), 256

    def kernel(table_ref, mixed_ref, in_ref, turned_ref, *rest):
        refs, (middle_ref, second_ref, held, sems) = rest[:parts], rest[parts:]

        @pl.when(pl.program_id(0) == 0)
        def _():
            weight.start(table_ref, refs, held, sems)
            arrived(held, sems.at[0])

        middle = in_ref[...] + matmul(mixed_ref[...], held[...])
        middle_ref[...] = middle
        second_ref[...] = (norm_parts(middle)[0] * turned_ref[1:2]).astype(LOW)

    cut = pl.BlockSpec((tile, width), lambda i: (i, 0))
    return pl.pallas_call(
        kernel,
        grid=(cells // tile,),
        in_specs=[SCALARS, cut, cut, pl.BlockSpec((8, width), lambda i: (0, 0))]
        + [ANYWHERE] * parts,
        out_specs=[cut, cut],
        out_shape=[
            jax.ShapeDtypeStruct((cells, width), FULL),
            jax.ShapeDtypeStruct((cells, width), LOW),
        ],
        scratch_shapes=[pltpu.VMEM(weight.shape, LOW), pltpu.SemaphoreType.DMA((1,))],
        compiler_params=params(),
        cost_estimate=cost(2 * cells * width * width, 9 << 20),
        name="branch",
    )(table, mixed, inputs, turned, *weight.operands)


def up_kernel(table, second_in, weight):
    cells, width = second_in.shape
    cols, tile = weight.shape[1], 512
    parts = len(weight.operands)

    def kernel(table_ref, in_ref, *rest):
        refs, (hidden_ref, slope_ref, held, sems) = rest[:parts], rest[parts:]
        step = pl.program_id(0)

        @pl.when(step == 0)
        def _():
            weight.start(table_ref, refs, held, sems.at[pl.ds(0, 1)], columns=(0, tile))
            weight.start(table_ref, refs, held, sems.at[pl.ds(1, 1)], columns=(tile, cols - tile))
            arrived(held.at[:, pl.ds(0, tile)], sems.at[0])

        @pl.when(step == 1)
        def _():
            arrived(held.at[:, pl.ds(tile, cols - tile)], sems.at[1])

        columns = held[:, pl.ds(pl.multiple_of(step * tile, tile), tile)]
        up_proj = matmul(in_ref[...], columns)
        gate = 0.5 + 0.5 * lax.erf(up_proj * (0.5**0.5))
        hidden_ref[...] = (up_proj * gate).astype(LOW)
        bell = jnp.exp(-0.5 * up_proj * up_proj) * (0.5 / jnp.pi) ** 0.5
        slope_ref[...] = (gate + up_proj * bell).astype(LOW)

    return pl.pallas_call(
        kernel,
        grid=(cols // tile,),
        in_specs=[SCALARS, whole(cells, width)] + [FAR_AWAY] * parts,
        out_specs=[pl.BlockSpec((cells, tile), lambda i: (0, i))] * 2,
        out_shape=[
            jax.ShapeDtypeStruct((cells, cols), LOW),
            jax.ShapeDtypeStruct((cells, cols), LOW),
        ],
        scratch_shapes=[pltpu.VMEM(weight.shape, LOW), pltpu.SemaphoreType.DMA((2,))],
        compiler_params=params(22),
        cost_estimate=cost(2 * cells * width * cols, 22 << 20, 2 * cells * cols),
        name="up",
    )(table, second_in, *weight.operands)


def half_specs(cells, height, cols, far, turns):
    slots = [turn * far + other * 4 * far for other in (0, 1) for turn in turns]

    def columns(slot):
        return pl.BlockSpec((cells, height), lambda step, table: (0, table[slot + step]))

    rows = pl.BlockSpec((1, height, cols), lambda step, table: (step, 0, 0))
    return [columns(slot) for slot in slots] + [rows] * len(slots)


def half_product(refs):
    half = len(refs) // 2
    left = jnp.concatenate([ref[...] for ref in refs[:half]], axis=1)
    return matmul(left, jnp.concatenate([ref[0] for ref in refs[half:]], axis=0))


def down_half(table, hidden, middle, parts, turns):
    cells, width = middle.shape
    far, height = parts[0].shape[:2]

    def kernel(table_ref, mid_ref, *rest):
        refs, total_ref = rest[:-1], rest[-1]

        @pl.when(pl.program_id(0) == 0)
        def _():
            total_ref[...] = mid_ref[...]

        total_ref[...] += half_product(refs)

    return pl.pallas_call(
        kernel,
        grid_spec=by_region(
            far,
            [whole(cells, width)] + half_specs(cells, height, width, far, turns),
            whole(cells, width),
            [],
        ),
        out_shape=jax.ShapeDtypeStruct((cells, width), FULL),
        compiler_params=params(24),
        cost_estimate=cost(0, 0),
        name="down_half",
    )(table, middle, *[hidden] * 4, *parts)


def latent_kernel(table, hidden, middle, noise, choose, comp_tables, down, to_latent, parts=None, turns=()):
    cells, width = middle.shape
    latent = noise.shape[1]
    mine, more = (8 if parts else 1 + len(down.operands)), len(to_latent.operands)
    steps = down.count // 4
    tile = hidden.shape[1] // steps

    def kernel(table_ref, mid_ref, noise_ref, choose_ref, tables_ref, *rest):
        refs, rest = rest[:mine], rest[mine:]
        latent_refs, rest = rest[:more], rest[more:]
        carried_ref, moments_ref, sample_ref, kl_ref, total, *held, latent_held, sems = rest
        step = pl.program_id(0)

        @pl.when(step == 0)
        def _():
            if not parts:
                down.start(table_ref, refs[1:], held[0], sems, 1)
            to_latent.start(table_ref, latent_refs, latent_held, sems.at[pl.ds(steps, 1)])
            total[...] = mid_ref[...]

        if parts:
            total[...] += half_product(refs)
        else:
            some = held[0].at[down.region(table_ref, step)]
            arrived(some, sems.at[step])
            total[...] += matmul(refs[0][...], some[...])

        @pl.when(step == steps - 1)
        def _():
            carried_ref[...] = total[...].astype(LOW)
            arrived(latent_held, sems.at[steps])
            moments_ref[...] = matmul(carried_ref[...], latent_held[...])
            mean_part, logvar = moments_ref[:, :latent], moments_ref[:, latent:]
            sample_ref[...] = (mean_part + jnp.exp(0.5 * logvar) * noise_ref[...]).astype(LOW)
            gap = mean_part - matmul(choose_ref[...], tables_ref[0])
            far = matmul(choose_ref[...], tables_ref[1])
            diverge = 0.5 * (far - logvar + (jnp.exp(logvar) + gap * gap) * jnp.exp(-far) - 1.0)
            kl_ref[...] = jnp.sum(diverge, axis=0, keepdims=True)

    return pl.pallas_call(
        kernel,
        grid_spec=by_region(
            steps,
            [whole(cells, width), whole(cells, latent), whole(*choose.shape)]
            + [whole(*comp_tables.shape)]
            + (
                half_specs(cells, tile // 8, width, steps, turns)
                if parts
                else [pl.BlockSpec((cells, tile), region_columns)] + [FAR_AWAY] * (mine - 1)
            )
            + [FAR_AWAY] * more,
            [whole(cells, width), whole(cells, 2 * latent), whole(cells, latent), whole(1, latent)],
            [
                pltpu.VMEM((cells, width), FULL),
                *([] if parts else [pltpu.VMEM(down.shape, LOW)]),
                pltpu.VMEM(to_latent.shape, LOW),
                pltpu.SemaphoreType.DMA((steps + 1,)),
            ],
        ),
        out_shape=[
            jax.ShapeDtypeStruct((cells, width), LOW),
            jax.ShapeDtypeStruct((cells, 2 * latent), FULL),
            jax.ShapeDtypeStruct((cells, latent), LOW),
            jax.ShapeDtypeStruct((1, latent), FULL),
        ],
        compiler_params=params(30),
        cost_estimate=cost(2 * cells * width * (hidden.shape[1] + width), 20 << 20),
        name="latent",
    )(
        table,
        middle,
        noise,
        choose,
        comp_tables,
        *([hidden] * 4 + parts if parts else [hidden, *down.operands]),
        *to_latent.operands,
    )


def decode_kernel(table, sample, cotangent, decode):
    cells, width = cotangent.shape
    latent = sample.shape[1]
    parts = len(decode.operands)

    def kernel(table_ref, sample_ref, dy_ref, *rest):
        refs, (grad_ref, back_ref, bias_ref, held, sem) = rest[:parts], rest[parts:]
        decode.start(table_ref, refs, held, sem)
        grad_ref[...] = left_product(sample_ref[...], dy_ref[...]).astype(LOW)
        bias_ref[...] = jnp.sum(dy_ref[...].astype(FULL), axis=0, keepdims=True)
        arrived(held, sem.at[0])
        back_ref[...] = right_product(dy_ref[...], held[...])

    return pl.pallas_call(
        kernel,
        in_specs=[SCALARS] + [INSIDE] * 2 + [FAR_AWAY] * parts,
        out_specs=[INSIDE] * 3,
        out_shape=[
            jax.ShapeDtypeStruct((latent, width), LOW),
            jax.ShapeDtypeStruct((cells, latent), FULL),
            jax.ShapeDtypeStruct((1, width), FULL),
        ],
        scratch_shapes=[pltpu.VMEM(decode.shape, LOW), pltpu.SemaphoreType.DMA((1,))],
        compiler_params=params(16),
        cost_estimate=cost(6 * cells * width * latent, 8 << 20),
        name="decode",
    )(table, sample, cotangent, *decode.operands)


def output_kernel(table, sample, turned, decode):
    cells = sample.shape[0]
    width = decode.shape[1]
    parts = len(decode.operands)

    def kernel(table_ref, sample_ref, turned_ref, *rest):
        refs, (out_ref, held, sem) = rest[:parts], rest[parts:]
        decode.start(table_ref, refs, held, sem)
        arrived(held, sem.at[0])
        out_ref[...] = (matmul(sample_ref[...], held[...]) + turned_ref[2:3]).astype(LOW)

    return pl.pallas_call(
        kernel,
        in_specs=[SCALARS] + [INSIDE] * 2 + [FAR_AWAY] * parts,
        out_specs=INSIDE,
        out_shape=jax.ShapeDtypeStruct((cells, width), LOW),
        scratch_shapes=[pltpu.VMEM(decode.shape, LOW), pltpu.SemaphoreType.DMA((1,))],
        compiler_params=params(16),
        cost_estimate=cost(2 * cells * width * sample.shape[1], 4 << 20),
        name="output",
    )(table, sample, turned, *decode.operands)


def factors_kernel(back, moments, noise, choose, comp_tables):
    cells, latent = noise.shape
    comps = choose.shape[1]

    def kernel(back_ref, mom_ref, noise_ref, choose_ref, tables_ref, plain_ref, factor_ref, comp_ref):
        mean_part, logvar = mom_ref[:, :latent], mom_ref[:, latent:]
        gap = mean_part - matmul(choose_ref[...], tables_ref[0])
        shrink = jnp.exp(-matmul(choose_ref[...], tables_ref[1]))
        ratio = jnp.exp(logvar) * shrink
        moved = gap * shrink
        factor_ref[:, :latent] = moved
        factor_ref[:, latent:] = (ratio - 1.0) * 0.5
        for i, value in enumerate((-moved, (1.0 - (ratio + gap * moved)) * 0.5)):
            high = value.astype(LOW)
            rest = (value - high.astype(FULL)).astype(LOW)
            chosen = choose_ref[...]
            comp_ref[i] = left_product(chosen, high) + left_product(chosen, rest)
        back = back_ref[...]
        plain_ref[:, :latent] = back
        plain_ref[:, latent:] = back * noise_ref[...] * jnp.exp(0.5 * logvar) * 0.5

    return pl.pallas_call(
        kernel,
        in_specs=[INSIDE] * 5,
        out_specs=[INSIDE] * 3,
        out_shape=[
            jax.ShapeDtypeStruct((cells, 2 * latent), FULL),
            jax.ShapeDtypeStruct((cells, 2 * latent), FULL),
            jax.ShapeDtypeStruct((2, comps, latent), FULL),
        ],
        compiler_params=params(16),
        cost_estimate=cost(200 * cells * latent, 10 << 20),
        name="factors",
    )(back, moments, noise, choose, comp_tables)


def plain_slots(slots, grads):
    far = slots.count // 4
    results = []
    for other in (False, True):
        owner, core = slot_owner(place(), jnp.arange(slots.count), far, other, slots.base == 0)
        result = jnp.zeros((slots.count, slots.rows, slots.cols), LOW)
        for grad, height, row, col in grads:
            blocks = grad.reshape(slots.count, 2, height, grad.shape[1])
            blocks = jnp.take(blocks[:, core], owner, axis=0)
            result = result.at[:, row : row + height, col : col + grad.shape[1]].set(blocks)
        results += [result[: slots.count // 2], result[slots.count // 2 :]]
    return results


def moments_kernel(table, kl_weight, total, kl_sum, plain, factor, carried, comp, grad_decode, to_latent, slots):
    cells, width = carried.shape
    latent = kl_sum.shape[1]
    parts = len(to_latent.operands)
    height = to_latent.piece[1]
    decode_height = grad_decode.shape[0] // (2 * slots.count)
    direct = height % 16 == 0 and decode_height % 16 == 0

    def kernel(table_ref, weight_ref, kl_ref, plain_ref, factor_ref, carried_ref, comp_ref, gd_ref, *rest):
        refs, rest = rest[:parts], rest[parts:]
        gc_ref, comp_out, *rest = rest
        outs, rest = rest[: 4 if direct else 1], rest[4 if direct else 1 :]
        held, grads, sums, sems = rest
        to_latent.start(table_ref, refs, held, sems.at[pl.ds(0, 1)])
        mean = kl_ref[...] * (1.0 / total)
        coef = weight_ref[0] * jax.nn.sigmoid((mean - FREE_BITS) * (1.0 / SOFTNESS))
        for i in range(2):
            some = pl.ds(i * latent, latent)
            comp_out[i] = comp_ref[i] * coef
            grads[:, some] = (plain_ref[:, some] + factor_ref[:, some] * coef).astype(LOW)
        sums[...] = left_product(carried_ref[...], grads[...]).astype(LOW)
        if direct:
            slots.start(
                table_ref, [(sums, height, 0, 0), (gd_ref, decode_height, height, 0)], outs, sems.at[1]
            )
        else:
            outs[0][...] = sums[...]
        arrived(held, sems.at[0])
        gc_ref[...] = right_product(grads[...], held[...]).astype(LOW)
        if direct:
            for out in outs:
                arrived(out, sems.at[1])

    results = pl.pallas_call(
        kernel,
        in_specs=[SCALARS, SCALARS] + [INSIDE] * 6 + [FAR_AWAY] * parts,
        out_specs=[INSIDE] * 2 + ([FAR_AWAY] * 4 if direct else [INSIDE]),
        out_shape=[
            jax.ShapeDtypeStruct((cells, width), LOW),
            jax.ShapeDtypeStruct(comp.shape, FULL),
        ]
        + (slots.shapes() if direct else [jax.ShapeDtypeStruct((width, 2 * latent), LOW)]),
        scratch_shapes=[
            pltpu.VMEM(to_latent.shape, LOW),
            pltpu.VMEM((cells, 2 * latent), LOW),
            pltpu.VMEM((width, 2 * latent), LOW),
            pltpu.SemaphoreType.DMA((2,)),
        ],
        compiler_params=params(24),
        cost_estimate=cost(8 * cells * width * latent, 16 << 20),
        name="moments",
    )(table, kl_weight, kl_sum, plain, factor, carried, comp, grad_decode, *to_latent.operands)
    if direct:
        return results
    grads = [(results[2], height, 0, 0), (grad_decode, decode_height, height, 0)]
    return list(results[:2]) + plain_slots(slots, grads)


def weight_grad(table, left, rights, slots, height, name, extra=()):
    cells, rows = left.shape
    each = rights[0].shape[1]
    cols = each * len(rights)
    direct = height % 16 == 0
    tile = 512 if cols <= 1024 else 256
    steps = rows // tile
    extra = list(extra)

    def product(left_ref, right_refs, target):
        for i, right_ref in enumerate(right_refs):
            block = left_product(left_ref[...], right_ref[...])
            target[:, pl.ds(i * each, each)] = block.astype(LOW)

    def kernel(table_ref, left_ref, *rest):
        right_refs, rest = rest[: len(rights)], rest[len(rights) :]
        if not direct:
            product(left_ref, right_refs, rest[0])
            return
        more, rest = rest[: len(extra)], rest[len(extra) :]
        outs, (sums, sems) = rest[:4], rest[4:]
        step = pl.program_id(0)

        @pl.when(step == 0)
        def _():
            for ref, one in zip(more, extra):
                slots.start(table_ref, [(ref, one[1], one[2], one[3])], outs, sems.at[2])

        current = lax.rem(step, 2)

        @pl.when(step >= 2)
        def _():
            arrived(sums.at[current], sems.at[current])

        product(left_ref, right_refs, sums.at[current])
        slots.send(table_ref, sums.at[current], step * (tile // height), outs, sems.at[current])

        @pl.when(step == steps - 1)
        def _():
            arrived(sums.at[0], sems.at[0])
            arrived(sums.at[1], sems.at[1])
            for ref in more:
                arrived(ref, sems.at[2])

    results = pl.pallas_call(
        kernel,
        grid=(steps,),
        in_specs=[SCALARS, pl.BlockSpec((cells, tile), lambda i: (0, i))]
        + [whole(cells, each)] * len(rights)
        + [whole(*one[0].shape) for one in (extra if direct else [])],
        out_specs=[ANYWHERE] * 4 if direct else [pl.BlockSpec((tile, cols), lambda i: (i, 0))],
        out_shape=slots.shapes() if direct else [jax.ShapeDtypeStruct((rows, cols), LOW)],
        scratch_shapes=[pltpu.VMEM((2, tile, cols), LOW), pltpu.SemaphoreType.DMA((3,))]
        if direct
        else [],
        compiler_params=params(28),
        cost_estimate=cost(2 * cells * rows * cols, 2 * rows * cols),
        name=name,
    )(table, left, *rights, *[one[0] for one in (extra if direct else [])])
    if direct:
        return results
    return plain_slots(slots, [(results[0], height, 0, 0)] + extra)


def up_back_kernel(table, grad_carried, slope, down):
    cells, width = grad_carried.shape
    cols = slope.shape[1]
    parts = len(down.operands)
    steps = down.count // 4
    tile = cols // steps

    def kernel(table_ref, grad_ref, slope_ref, *rest):
        refs, (out_ref, held, sems) = rest[:parts], rest[parts:]
        step = pl.program_id(0)

        @pl.when(step == 0)
        def _():
            down.start(table_ref, refs, held, sems, 1)

        some = held.at[down.region(table_ref, step)]
        arrived(some, sems.at[step])
        out_ref[...] = (right_product(grad_ref[...], some[...]) * slope_ref[...]).astype(LOW)

    return pl.pallas_call(
        kernel,
        grid_spec=by_region(
            steps,
            [whole(cells, width), pl.BlockSpec((cells, tile), region_columns)]
            + [FAR_AWAY] * parts,
            pl.BlockSpec((cells, tile), region_columns),
            [pltpu.VMEM(down.shape, LOW), pltpu.SemaphoreType.DMA((steps,))],
        ),
        out_shape=jax.ShapeDtypeStruct((cells, cols), LOW),
        compiler_params=params(24),
        cost_estimate=cost(2 * cells * width * cols, 22 << 20),
        name="up_back",
    )(table, grad_carried, slope, *down.operands)


def middle_back_kernel(table, grad_up_proj, grad_carried, middle, mixed, turned, up, out_proj):
    cells, width = grad_carried.shape
    cols = grad_up_proj.shape[1]
    parts, more = len(up.operands), len(out_proj.operands)
    steps = up.count // 8

    def kernel(table_ref, gu_ref, gc_ref, mid_ref, mixed_ref, turned_ref, *rest):
        refs, rest = rest[:parts], rest[parts:]
        out_refs, rest = rest[:more], rest[more:]
        gm_ref, go_ref, gx_ref, gain_ref, gu_held, second, held, out_held, sems = rest
        loading = pltpu.make_async_copy(gu_ref, gu_held, sems.at[steps + 1])
        loading.start()
        up.start(table_ref, refs, held, sems, 2)
        out_proj.start(table_ref, out_refs, out_held, sems.at[pl.ds(steps, 1)])
        loading.wait()
        for step in range(steps):
            some = up.region(table_ref, step, 2)
            arrived(held.at[some], sems.at[step])
            second[:, some] = right_product(gu_held[...], held[some])
        normed, scale = norm_parts(mid_ref[...])
        grad_second = second[...]
        gain_ref[...] = jnp.sum(normed * grad_second, axis=0, keepdims=True)
        back = norm_back(normed, scale, grad_second, turned_ref[1:2])
        grad_middle = gc_ref[...].astype(FULL) + back
        gm_ref[...] = grad_middle
        branch = grad_middle.astype(LOW)
        go_ref[...] = left_product(mixed_ref[...], branch).astype(LOW)
        arrived(out_held, sems.at[steps])
        gx_ref[...] = right_product(branch, out_held[...]).astype(LOW)

    return pl.pallas_call(
        kernel,
        in_specs=[SCALARS, ANYWHERE] + [INSIDE] * 4 + [ANYWHERE] * (parts + more),
        out_specs=[INSIDE] * 4,
        out_shape=[
            jax.ShapeDtypeStruct((cells, width), FULL),
            jax.ShapeDtypeStruct((width, width), LOW),
            jax.ShapeDtypeStruct((cells, width), LOW),
            jax.ShapeDtypeStruct((1, width), FULL),
        ],
        scratch_shapes=[
            pltpu.VMEM((cells, cols), LOW),
            pltpu.VMEM((cells, width), FULL),
            pltpu.VMEM(up.shape, LOW),
            pltpu.VMEM(out_proj.shape, LOW),
            pltpu.SemaphoreType.DMA((steps + 2,)),
        ],
        compiler_params=params(50),
        cost_estimate=cost(2 * cells * width * (cols + width), 22 << 20),
        name="middle_back",
    )(table, grad_up_proj, grad_carried, middle, mixed, turned, *up.operands, *out_proj.operands)


def input_back_kernel(table, grad_packed, grad_middle, inputs, turned, small, columns, weight):
    cells, width = inputs.shape
    parts = len(weight.operands)
    steps = weight.count // 8

    def kernel(table_ref, gq_ref, gk_ref, gv_ref, gm_ref, in_ref, turned_ref, small_ref, *rest):
        column_refs, rest = rest[: len(columns)], rest[len(columns) :]
        refs, (gx_ref, small_out, first, held, sems) = rest[:parts], rest[parts:]
        weight.start(table_ref, refs, held, sems, 2)
        normed, scale = norm_parts(in_ref[...].astype(FULL))
        for step in range(steps):
            some = weight.region(table_ref, step, 2)
            arrived(held.at[some], sems.at[step])
            first[:, some] = sum(
                right_product(ref[...], held[some, i * width : (i + 1) * width])
                for i, ref in enumerate((gq_ref, gk_ref, gv_ref))
            )
        grad_first = first[...]
        gain = jnp.sum(normed * grad_first, axis=0, keepdims=True)
        lane = lax.broadcasted_iota(jnp.int32, (width, 128), 1)
        block = small_ref[...]
        for k, one in enumerate((gain, *[ref[...] for ref in column_refs])):
            one = jnp.transpose(jnp.broadcast_to(one, (128, width)))
            block = jnp.where(lane == k, one, block)
        small_out[...] = block.astype(LOW)
        gx_ref[...] = gm_ref[...] + norm_back(normed, scale, grad_first, turned_ref[0:1])

    return pl.pallas_call(
        kernel,
        in_specs=[SCALARS] + [INSIDE] * (7 + len(columns)) + [FAR_AWAY] * parts,
        out_specs=[INSIDE] * 2,
        out_shape=[
            jax.ShapeDtypeStruct((cells, width), FULL),
            jax.ShapeDtypeStruct((width, 128), LOW),
        ],
        scratch_shapes=[
            pltpu.VMEM((cells, width), FULL),
            pltpu.VMEM(weight.shape, LOW),
            pltpu.SemaphoreType.DMA((steps,)),
        ],
        compiler_params=params(44),
        cost_estimate=cost(6 * cells * width * width, 18 << 20),
        name="input_back",
    )(table, *grad_packed, grad_middle, inputs, turned, small, *columns, *weight.operands)


def small_block(columns, rest):
    rows = rest.shape[0]
    gap = jnp.zeros((rows, 16 - len(columns)), rest.dtype)
    end = jnp.zeros((rows, 112 - rest.shape[1]), rest.dtype)
    return jnp.concatenate([*columns, gap, rest, end], axis=1)


def join(*parts):
    _, rows, cols = parts[0].shape
    flat = jnp.concatenate([part.reshape(-1, cols) for part in parts], axis=0)
    return flat.reshape(-1, rows, cols)


def far_start(block):
    return [far_exchange(block, mask) for mask in far_masks()]


def add_low(one, two):
    return (one.astype(FULL) + two.astype(FULL)).astype(LOW)


def add_slots(size, *terms):
    parts = [array[first : first + size] for array, first in terms]
    return add_all(parts[0], parts[1:]).astype(LOW)


def both_cores(slots, got, turn, far):
    return add_slots(far, *[(pair[turn // 2], turn % 2 * far) for pair in (slots, got)])


def add_all(first, others):
    total = first.astype(FULL)
    for one in others:
        total = total + one.astype(FULL)
    return total


def odd_even(*terms):
    pairs = [term.reshape(-1, 2, *term.shape[1:]) for term in terms]
    return [
        add_all(pairs[0][:, k], [pair[:, k] for pair in pairs[1:]]).astype(LOW) for k in (1, 0)
    ]


def far_last(odd, even, bit):
    got = far_exchange(odd, bit)
    while even.shape[0] > 1:
        bit *= 2
        odd, even = odd_even(even, got)
        got = far_exchange(odd, bit)
    return even, got


def far_slots(value, size):
    return [far_exchange(value[m * size : (m + 1) * size], m) for m in far_masks()]


def matmul(left_side, right_side):
    return jnp.dot(left_side, right_side, preferred_element_type=FULL)


def left_product(left_side, right_side):
    return lax.dot_general(
        left_side, right_side, (((0,), (0,)), ((), ())), preferred_element_type=FULL
    )


def right_product(left_side, right_side):
    return lax.dot_general(
        left_side, right_side, (((1,), (1,)), ((), ())), preferred_element_type=FULL
    )


def norm_parts(tensor):
    centred = tensor - jnp.mean(tensor, axis=-1, keepdims=True)
    scale = lax.rsqrt(jnp.mean(centred * centred, axis=-1, keepdims=True) + 1e-05)
    return centred * scale, scale


def norm_back(normed, scale, grad, gain):
    inner = grad * gain
    return scale * (
        inner
        - jnp.mean(inner, axis=-1, keepdims=True)
        - normed * jnp.mean(inner * normed, axis=-1, keepdims=True)
    )


def head_lanes(value, head, size):
    lane = lax.broadcasted_iota(jnp.int32, value.shape, 1)
    return jnp.where((lane // size) == head, value, jnp.zeros_like(value))


def attention_forward(packed, seg_col, seg_row, first, last, earlier=()):
    cells, three = packed.shape
    width = three // 3
    size = width // HEADS
    pair = 128 // size
    steps = HEADS // pair

    def kernel(seg_col, seg_row, q_ref, k_ref, v_ref, *rest):
        out_ref, attn_ref = rest[-2:]
        same = seg_col[...] == seg_row[...]
        queries, keys = q_ref[...], k_ref[...]
        values = jnp.transpose(v_ref[...])
        outs = []
        for head in range(pair):
            scores = right_product(head_lanes(keys, head, size), queries) * size ** (-0.5)
            scores = jnp.where(same, scores, NEGATIVE)
            powers = jnp.exp(scores - jnp.max(scores, axis=0, keepdims=True))
            attn = powers * (1.0 / jnp.sum(powers, axis=0, keepdims=True))
            attn_low = attn.astype(LOW)
            attn_ref[head] = attn_low
            outs.append(matmul(values[head * size : (head + 1) * size], attn_low))
        out_ref[...] = jnp.transpose(jnp.concatenate(outs, axis=0)).astype(LOW)

    return pl.pallas_call(
        kernel,
        grid=(last - first,),
        in_specs=[
            pl.BlockSpec((cells, 1), lambda i: (0, 0)),
            pl.BlockSpec((1, cells), lambda i: (0, 0)),
            pl.BlockSpec((cells, 128), lambda i: (0, i + first)),
            pl.BlockSpec((cells, 128), lambda i: (0, i + first + steps)),
            pl.BlockSpec((cells, 128), lambda i: (0, i + first + 2 * steps)),
        ]
        + [ANYWHERE] * len(earlier),
        out_specs=[
            pl.BlockSpec((cells, 128), lambda i: (0, i + first)),
            pl.BlockSpec((pair, cells, cells), lambda i: (i + first, 0, 0)),
        ],
        out_shape=[
            jax.ShapeDtypeStruct((cells, width), LOW),
            jax.ShapeDtypeStruct((HEADS, cells, cells), LOW),
        ],
        input_output_aliases={5 + i: i for i in range(len(earlier))},
        compiler_params=params(),
        cost_estimate=cost(4 * cells * cells * width, 24 << 20),
        name="attention_forward",
    )(seg_col, seg_row, packed, packed, packed, *earlier)


def attention_backward(packed, attn, mixed, grad_mixed):
    cells, three = packed.shape
    width = three // 3
    size = width // HEADS
    pair = 128 // size
    steps = HEADS // pair

    def kernel(q_ref, k_ref, v_ref, g_ref, mixed_ref, attn_ref, gq_ref, gk_ref, gv_ref):
        queries, keys, values, grad = q_ref[...], k_ref[...], v_ref[...], g_ref[...]
        keys_t = jnp.transpose(keys)
        inner = jnp.transpose(grad).astype(FULL) * jnp.transpose(mixed_ref[...]).astype(FULL)
        grad_q, grad_k, grad_v = [], 0.0, 0.0
        for head in range(pair):
            attn_low = attn_ref[head]
            attn = attn_low.astype(FULL)
            grad_attn = right_product(head_lanes(values, head, size), grad)
            some = slice(head * size, (head + 1) * size)
            grad_scores = attn * (grad_attn - jnp.sum(inner[some], axis=0, keepdims=True))
            grad_scores = grad_scores.astype(LOW)
            grad_q.append(matmul(keys_t[some], grad_scores))
            grad_k += head_lanes(matmul(grad_scores, queries), head, size)
            grad_v += head_lanes(matmul(attn_low, grad), head, size)
        scale = size ** (-0.5)
        gq_ref[...] = (jnp.transpose(jnp.concatenate(grad_q, axis=0)) * scale).astype(LOW)
        gk_ref[...] = (grad_k * scale).astype(LOW)
        gv_ref[...] = grad_v.astype(LOW)

    return pl.pallas_call(
        kernel,
        grid=(steps,),
        in_specs=[
            pl.BlockSpec((cells, 128), lambda i: (0, i)),
            pl.BlockSpec((cells, 128), lambda i: (0, i + steps)),
            pl.BlockSpec((cells, 128), lambda i: (0, i + 2 * steps)),
            pl.BlockSpec((cells, 128), lambda i: (0, i)),
            pl.BlockSpec((cells, 128), lambda i: (0, i)),
            pl.BlockSpec((pair, cells, cells), lambda i: (i, 0, 0)),
        ],
        out_specs=[pl.BlockSpec((cells, 128), lambda i: (0, i))] * 3,
        out_shape=[jax.ShapeDtypeStruct((cells, width), LOW)] * 3,
        compiler_params=params(20),
        cost_estimate=cost(10 * cells * cells * width, 24 << 20),
        name="attention_backward",
    )(packed, packed, packed, grad_mixed, mixed, attn)


def local(
    layer_ends,
    segment_ids,
    mixture,
    noise,
    plan_step,
    ln1_gain,
    w_qkv,
    w_out,
    ln2_gain,
    w_up,
    w_down,
    w_latent,
    w_decode,
    decode_bias,
    comp_mean,
    comp_logvar,
):
    core = lax.axis_index("pipe")
    cells = segment_ids.shape[1]
    devices = lax.axis_size("dp") * 2
    width = layer_ends.shape[2]
    latent = noise.shape[1]
    comps = comp_mean.shape[0]
    total_cells = cells * devices

    rows = w_qkv.shape[0]
    comp_cols = latent // devices
    lanes = 2 * comps * comp_cols // rows
    small = jnp.concatenate([comp_mean.reshape(-1), comp_logvar.reshape(-1)]).reshape(rows, lanes)
    columns = [ln1_gain[:, None], ln2_gain[:, None], decode_bias[:, None]]
    small = small_block(columns, small)
    qkv_cols, out_cols, up_cols = w_qkv.shape[1], w_out.shape[1], w_up.shape[1]
    first_pieces = (
        (0, rows, 0, qkv_cols),
        (0, rows, qkv_cols, out_cols),
        (0, rows, qkv_cols + out_cols, 128),
    )
    up_pieces = ((0, rows, 0, up_cols),)
    down_rows, decode_rows = w_down.shape[0], w_decode.shape[0]
    down_pieces = ((0, down_rows, 0, width),)
    last_pieces = ((0, rows, 0, width), (rows, decode_rows, 0, width))
    first_block = jnp.concatenate([w_qkv, w_out, small], axis=1)[None]
    up_block, down_block = w_up[None], w_down[None]
    last_block = jnp.concatenate([w_latent, w_decode], axis=0)[None]

    def my_rows(tensor, which):
        return lax.dynamic_slice_in_dim(tensor, which * cells, cells, axis=0)

    kept = my_rows(layer_ends[0], core)
    going = my_rows(layer_ends[0], 1 - core)
    segments = lax.dynamic_index_in_dim(segment_ids, core, keepdims=False)
    mixture_rows = my_rows(mixture, core)
    noise_rows = my_rows(noise, core)

    table = tables()
    first_far = far_start(first_block)
    got = send_core(going)
    last_near = near_first(last_block)
    got, last_near, up_block, *first_far = hold(got, last_near, up_block, *first_far)
    inputs_low = jnp.where(core == 0, kept, got)
    inputs = inputs_low.astype(FULL)
    cotangent = jnp.where(core == 0, got, kept)
    normed_one, scale_one = norm_parts(inputs)
    last_two = join(last_block, last_near)

    first_four = join(first_block, *first_far)
    first_m1, first_m2 = near_first(first_four), near_second(first_four)
    up_far = far_start(up_block)
    seg_col, seg_row = segments[:, None], segments[None, :]
    choose = mixture_rows[:, None] == jnp.arange(comps, dtype=jnp.int32)[None, :]
    first_m1, first_m2, normed_one, last_two, table, seg_col, seg_row, *rest = hold(
        first_m1,
        first_m2,
        normed_one,
        last_two,
        table,
        seg_col,
        seg_row,
        choose.astype(LOW),
        noise_rows,
        down_block,
        *up_far,
    )
    choose, noise_rows, down_block, *up_far = rest

    first_m3 = near_second(first_m1)
    first_c0, first_c1, first_c2 = [send_core(one) for one in (first_four, first_m1, first_m2)]
    down_far = [far_exchange(down_block, 1)]
    first_m3, first_c0, first_c1, first_c2, down_block, *rest = hold(
        first_m3, first_c0, first_c1, first_c2, down_block, *down_far, *up_far
    )
    down_far, up_far = rest[:1], rest[1:]

    up_four = join(up_block, *up_far)
    first_c3, up_four, down_block = hold(send_core(first_m3), up_four, down_block)
    up_m1, up_m2 = near_first(up_four), near_second(up_four)
    last_more = near_second(last_two)
    down_far += [far_exchange(down_block, mask) for mask in far_masks() if mask > 1]
    first_parts = [first_four, first_m1, first_m2, first_m3], [first_c0, first_c1, first_c2, first_c3]
    qkv, out_proj, small_rows = [Rows(*first_parts, piece) for piece in first_pieces]
    first_in, packed, small_all, turned = first_kernel(table, normed_one, qkv, small_rows)
    pairs = HEADS * (width // HEADS) // 128
    some_heads = attention_forward(packed, seg_col, seg_row, 0, pairs // 2)
    up_m1, up_m2, last_more, packed, *rest = hold(
        up_m1, up_m2, last_more, packed, *some_heads, *down_far
    )
    some_heads, down_far = rest[:2], rest[2:]
    last_four = join(last_two, last_more)

    up_m3 = near_second(up_m1)
    down_four = join(down_block, *down_far)
    down_m1 = near_first(down_four)
    up_c0 = send_core(up_four)
    last_early, last_late = [1, 2], list(far_masks())[2:]
    last_far = {mask: far_exchange(last_four, mask) for mask in last_early}
    mixed, attn = attention_forward(packed, seg_col, seg_row, pairs // 2, pairs, some_heads)
    middle, second_in = branch_kernel(table, mixed, inputs, turned, out_proj)
    small_all = small_all.reshape(devices, rows, 128)[:, :, 16 : 16 + lanes]
    small_all = small_all.reshape(devices, 2, comps, comp_cols).transpose(1, 2, 0, 3)
    comp_tables = small_all.reshape(2, comps, latent)
    early = [last_far[mask] for mask in last_early]
    up_m3, down_m1, up_c0, second_in, comp_tables, up_m1, up_m2, last_four, *early = hold(
        up_m3, down_m1, up_c0, second_in, comp_tables, up_m1, up_m2, last_four, *early
    )
    last_far.update(zip(last_early, early))

    down_m2, down_m3 = near_second(down_four), near_second(down_m1)
    up_c1, up_c2, up_c3 = [send_core(one) for one in (up_m1, up_m2, up_m3)]
    up_c1, up_c2, up_c3, last_four, down_four, down_m1 = hold(
        up_c1, up_c2, up_c3, last_four, down_four, down_m1
    )
    last_far.update((mask, far_exchange(last_four, mask)) for mask in last_late)
    up = Rows([up_four, up_m1, up_m2, up_m3], [up_c0, up_c1, up_c2, up_c3], up_pieces[0])
    hidden, slope = up_kernel(table, second_in, up)
    down_c0, down_c1 = send_core(down_four), send_core(down_m1)
    late = [last_far[mask] for mask in last_late]
    down_m2, down_m3, down_c0, down_c1, hidden, *late = hold(
        down_m2, down_m3, down_c0, down_c1, hidden, *late
    )
    last_far.update(zip(last_late, late))

    last_all = join(last_four, *[last_far[mask] for mask in far_masks()])
    last_there = send_core(last_all)
    down_c2, down_c3 = send_core(down_m2), send_core(down_m3)
    in_halves = down_rows % 128 == 0
    if in_halves:
        middle_half = down_half(
            table, hidden, middle, [down_four, down_m1, down_c0, down_c1], (0, 1)
        )
        last_there, down_c2, down_c3, middle_half = hold(
            last_there, down_c2, down_c3, middle_half
        )
    else:
        last_there, down_c2, down_c3 = hold(last_there, down_c2, down_c3)
    to_latent, decode = [Rows([last_all], [last_there], piece, False) for piece in last_pieces]
    down = Rows(
        [down_four, down_m1, down_m2, down_m3], [down_c0, down_c1, down_c2, down_c3], down_pieces[0]
    )
    carried, moments, sample, kl_part = latent_kernel(
        table,
        hidden,
        middle_half if in_halves else middle,
        noise_rows,
        choose,
        comp_tables,
        down,
        to_latent,
        [down_m2, down_m3, down_c2, down_c3] if in_halves else None,
        (2, 3),
    )
    kl_sum = kl_part + send_core(kl_part)
    kl_sum, sample = hold(kl_sum, sample)
    grad_decode, grad_sample, grad_bias = decode_kernel(table, sample, cotangent, decode)
    kl_near = [send(kl_sum, bit, bit) for bit in (2, 4, 6)]
    kl_sum = sum(kl_near, kl_sum)
    kl_sum, grad_sample = hold(kl_sum, grad_sample)
    kl_far = [far_exchange(kl_sum, mask) for mask in far_masks()]
    plain, factor, comp = factors_kernel(grad_sample, moments, noise_rows, choose, comp_tables)
    kl_sum = sum(kl_far, kl_sum)
    kl_sum, grad_decode, plain, factor, grad_bias = hold(
        kl_sum, grad_decode, plain, factor, grad_bias
    )

    far = lax.axis_size("dp") // 4
    kl_weight = jnp.minimum(1.0, (plan_step + 1).astype(FULL) / WARM)
    grad_carried, comp, *last_slots = moments_kernel(
        table,
        kl_weight,
        total_cells,
        kl_sum,
        plain,
        factor,
        carried,
        comp,
        grad_decode,
        to_latent,
        Slots(rows + decode_rows, width),
    )
    grad_carried, hidden, *last_slots = hold(grad_carried, hidden, *last_slots)
    last_got = [send_core(one) for one in last_slots[2:]]
    down_slots = weight_grad(
        table, hidden, [grad_carried], Slots(down_rows, width), down_rows, "grad_down"
    )
    grad_carried, *rest = hold(grad_carried, *last_got, *down_slots)
    last_got, down_slots = rest[:2], rest[2:]

    down_got = [send_core(one) for one in down_slots[2:]]
    last_3, last_2 = [both_cores(last_slots, last_got, turn, far) for turn in (3, 2)]
    last_m3, last_m2 = near_second(last_3), near_second(last_2)
    grad_up_proj = up_back_kernel(table, grad_carried, slope, down)
    grad_up_proj, last_m3, last_m2, *down_got = hold(grad_up_proj, last_m3, last_m2, *down_got)
    down_m3 = near_second(both_cores(down_slots, down_got, 3, far))
    up_slots = weight_grad(
        table, second_in, [grad_up_proj], Slots(rows, up_cols), rows, "grad_up"
    )
    down_0, down_1, down_2 = [both_cores(down_slots, down_got, turn, far) for turn in range(3)]
    tables_grad = comp.reshape(2, comps, devices, comp_cols)
    tables_grad = tables_grad.transpose(2, 0, 1, 3).reshape(devices * rows, lanes)
    small_grads = jnp.pad(tables_grad, ((0, 0), (16, 112 - lanes)))
    down_m3, last_m3, small_grads, down_0, down_1, down_2, *up_slots = hold(
        down_m3, last_m3, small_grads, down_0, down_1, down_2, *up_slots
    )

    up_got = [send_core(one) for one in up_slots[2:]]
    down_m2 = near_second(down_2)
    last_m1 = near_first(add_slots(far, (last_slots[0], far), (last_got[0], far), (last_m3, 0)))
    grad_middle, grad_out, grad_mixed, grad_gain_two = middle_back_kernel(
        table, grad_up_proj, grad_carried, middle, mixed, turned, up, out_proj
    )
    down_m2, last_m1, grad_mixed, grad_out, *up_got = hold(
        down_m2, last_m1, grad_mixed, grad_out, *up_got
    )

    up_m3 = near_second(both_cores(up_slots, up_got, 3, far))
    down_m1 = near_first(add_slots(far, (down_1, 0), (down_m3, 0)))
    grad_packed = attention_backward(packed, attn, mixed, grad_mixed)
    up_m3, down_m1, *grad_packed = hold(up_m3, down_m1, *grad_packed)

    up_m2 = near_second(both_cores(up_slots, up_got, 2, far))
    up_m1 = near_first(add_slots(far, (up_slots[0], far), (up_got[0], far), (up_m3, 0)))
    down_odd, down_even = odd_even(down_0, down_m2, down_m1)
    down_far = far_exchange(down_odd, 1)
    grad_inputs, small_grads = input_back_kernel(
        table,
        grad_packed,
        grad_middle,
        inputs_low,
        turned,
        small_grads,
        [grad_gain_two, grad_bias],
        qkv,
    )
    first_slots = weight_grad(
        table,
        first_in,
        grad_packed,
        Slots(rows, qkv_cols + out_cols + 128),
        rows,
        "grad_qkv",
        [(grad_out, rows, 0, qkv_cols), (small_grads, rows, 0, qkv_cols + out_cols)],
    )
    up_m2, up_m1, grad_inputs, down_far, *first_slots = hold(
        up_m2, up_m1, grad_inputs, down_far, *first_slots
    )

    first_high = send_core(first_slots[3])
    up_odd, up_even = odd_even(up_slots[0][:far], up_got[0][:far], up_m2, up_m1)
    last_odd, last_even = odd_even(last_slots[0][:far], last_got[0][:far], last_m2, last_m1)
    first_high, up_odd, up_even, last_odd, *first_slots = hold(
        first_high, up_odd, up_even, last_odd, *first_slots
    )
    last_far = far_exchange(last_odd, 1)
    first_low = send_core(first_slots[2])
    first_got = [first_low, first_high]
    first_3, first_2 = [both_cores(first_slots, first_got, turn, far) for turn in (3, 2)]
    down_odd, down_even = odd_even(down_even, down_far)
    first_low, first_3, first_2, last_far, down_odd, down_even, sample = hold(
        first_low, first_3, first_2, last_far, down_odd, down_even, sample
    )
    last_odd, last_even = odd_even(last_even, last_far)

    first_m3, first_m2 = near_second(first_3), near_second(first_2)
    up_far = far_exchange(up_odd, 1)
    last_even, last_far = far_last(last_odd, last_even, 2)
    down_even, down_far = far_last(down_odd, down_even, 2)
    decoded = output_kernel(table, sample, turned, decode)
    first_m3, first_m2, up_far, last_far, down_far, decoded = hold(
        first_m3, first_m2, up_far, last_far, down_far, decoded
    )

    first_m1 = near_first(add_slots(far, (first_slots[0], far), (first_low, far), (first_m3, 0)))
    inputs_there, decoded_there = send_core(grad_inputs), send_core(decoded)
    up_odd, up_even = odd_even(up_even, up_far)
    up_even, up_far = far_last(up_odd, up_even, 2)
    down_sum = add_all(down_even[0], [down_far[0]])
    last_sum = add_all(last_even[0], [last_far[0]])
    first_m1, inputs_there, decoded_there, down_sum, up_far, last_sum = hold(
        first_m1, inputs_there, decoded_there, down_sum, up_far, last_sum
    )
    up_sum = add_all(up_even[0], [up_far[0]])

    result = jnp.where(
        core == 0,
        jnp.concatenate([grad_inputs, inputs_there], axis=0),
        jnp.concatenate([decoded_there, decoded], axis=0).astype(FULL),
    )[None]
    first_all = add_slots(far, (first_slots[0], 0), (first_low, 0), (first_m2, 0), (first_m1, 0))
    first_far = far_slots(first_all, 1)
    pieces = [first_all[0], *[one[0] for one in first_far]]

    def first_sum(start, size):
        parts = [one[:, start : start + size] for one in pieces]
        return add_all(parts[0], parts[1:])

    small_sum = first_sum(qkv_cols + out_cols, 128)
    comp_mean_sum, comp_logvar_sum = small_sum[:, 16 : 16 + lanes].reshape(2, comps, comp_cols)
    return (
        result,
        small_sum[:, 0],
        first_sum(0, qkv_cols),
        first_sum(qkv_cols, out_cols),
        small_sum[:, 1],
        up_sum,
        down_sum,
        last_sum[:rows],
        last_sum[rows:],
        small_sum[:, 2],
        comp_mean_sum,
        comp_logvar_sum,
    )


def solution(mesh):
    split = P(EVERY)
    wide = P(EVERY, None)
    tall = P(None, EVERY)
    ends = P("pipe", "dp", None)
    return jax.shard_map(
        local,
        mesh=mesh,
        in_specs=(
            ends,
            P("dp", None),
            P("dp"),
            P("dp", None),
            P(),
            split,
            wide,
            wide,
            split,
            wide,
            wide,
            wide,
            wide,
            split,
            tall,
            tall,
        ),
        out_specs=(ends, split, wide, wide, split, wide, wide, wide, wide, split, tall, tall),
        check_vma=False,
    )
```
